256 devices in a mesh: dp: 64 (over z, x, core), rep: 4 (over y).
Axes of the slice: x: 4, y: 4, z: 8, core: 2. Of those that a mesh axis runs over, the one named last changes fastest.
Arguments:
- item_tokens: bfloat16 [6144, 24, 256], P(('dp', 'rep')), may hold values from -6 to 6
- owner_index: int32 [6144], P(('dp', 'rep')), may hold values from 0 to 63, as said below
- owner_row: int32 [6144], P(('dp', 'rep')), may hold values from 0 to 15
- parent_tokens: bfloat16 [4096, 32, 256], P(('dp', 'rep')), may hold values from -6 to 6
- cotangent: bfloat16 [4096, 32, 256], P(('dp', 'rep')), may hold values from -30 to 30
- column_gain: bfloat16 [256], replicated, may hold values from 0.5 to 1.5
- column_query: bfloat16 [256, 256], replicated, may hold values from -0.375 to 0.375
- column_key: bfloat16 [256, 256], replicated, may hold values from -0.375 to 0.375
- column_value: bfloat16 [256, 256], replicated, may hold values from -0.375 to 0.375
- column_out: bfloat16 [256, 256], replicated, may hold values from -0.375 to 0.375
- hidden_gain: bfloat16 [256], replicated, may hold values from 0.5 to 1.5
- up_weight: bfloat16 [256, 1024], replicated, may hold values from -0.375 to 0.375
- down_weight: bfloat16 [1024, 256], replicated, may hold values from -0.1875 to 0.1875
- link_weight: bfloat16 [256, 256], replicated, may hold values from -0.375 to 0.375
- parent_gain: bfloat16 [256], replicated, may hold values from 0.5 to 1.5
- parent_query: bfloat16 [256, 256], replicated, may hold values from -0.375 to 0.375
- parent_key: bfloat16 [256, 256], replicated, may hold values from -0.375 to 0.375
- parent_value: bfloat16 [256, 256], replicated, may hold values from -0.375 to 0.375
- parent_out: bfloat16 [256, 256], replicated, may hold values from -0.375 to 0.375
Outputs:
- parent_states: bfloat16 [4096, 32, 256], P(('dp', 'rep'))
- grad_column_gain: float32 [256], replicated
- grad_column_query: float32 [256, 256], replicated
- grad_column_key: float32 [256, 256], replicated
- grad_column_value: float32 [256, 256], replicated
- grad_column_out: float32 [256, 256], replicated
- grad_hidden_gain: float32 [256], replicated
- grad_up_weight: float32 [256, 1024], replicated
- grad_down_weight: float32 [1024, 256], replicated
- grad_link_weight: float32 [256, 256], replicated
- grad_parent_gain: float32 [256], replicated
- grad_parent_query: float32 [256, 256], replicated
- grad_parent_key: float32 [256, 256], replicated
- grad_parent_value: float32 [256, 256], replicated
- grad_parent_out: float32 [256, 256], replicated
The draws below stay inside these ranges and needn't reach their ends.
Inputs may be any that keep to these rules, and one draw needn't show every extreme that they name: `owner_index`: among the 24 transactions of one device no owner is named more than 2 times; in each group of devices along dp that share an index along rep, one owner is named exactly 2 times by every device.
All inputs are finite; a program needn't handle non-finite values.
Results may differ from the reference program's by a relative error of at most 0.03.
Values may be sent and summed in bfloat16 or wider, within the bound.
A program may use at most 64 MiB of HBM per device.

```python
import math
import jax
import jax.numpy as jnp
from jax import lax

W = 256
HEADS = 8
FF = 1024
COLS = 24
CTOK = 32
TX_DEV = 24
CUST_DEV = 16
SLOTS = 2
TRANSACTIONS = 6144
CUSTOMERS = 4096
N_DP = 64
N_REP = 4


def draw_owner_index(key, part):
    key = jax.random.fold_in(key, 3)
    blocks = N_DP * N_REP
    pool = N_DP * SLOTS
    owner_of = jnp.arange(pool, dtype=jnp.int32) // SLOTS
    favored = jax.random.randint(jax.random.fold_in(key, 1), (N_REP,), 0, N_DP)
    favored_block = jnp.tile(favored, N_DP)
    block_keys = jax.random.split(jax.random.fold_in(key, 2), blocks)
    scores = jax.vmap(lambda subkey: jax.random.permutation(subkey, pool))(block_keys).astype(jnp.int32)
    scores = scores - pool * (owner_of[None, :] == favored_block[:, None]).astype(jnp.int32)
    order = jnp.argsort(scores, axis=1, stable=True)[:, :TX_DEV]
    owners = owner_of[order]
    shuffle_keys = jax.random.split(jax.random.fold_in(key, 4), blocks)
    shuffle = jax.vmap(lambda subkey: jax.random.permutation(subkey, TX_DEV))(shuffle_keys)
    owners = jnp.take_along_axis(owners, shuffle, axis=1)
    return owners.reshape(blocks * TX_DEV).astype(jnp.int32)


def draw_owner_row(key, part):
    key = jax.random.fold_in(key, 5)
    count = N_DP * N_REP * TX_DEV
    first_draw = jax.random.randint(jax.random.fold_in(key, 1), (count,), 0, CUST_DEV)
    second_draw = jax.random.randint(jax.random.fold_in(key, 2), (count,), 0, CUST_DEV)
    return jnp.minimum(first_draw, second_draw).astype(jnp.int32)


def draw_cotangent(key, part):
    key = jax.random.fold_in(key, 7)
    blocks = N_DP * N_REP
    half = max(1, blocks // 2)
    levels = jnp.exp(jax.random.uniform(jax.random.fold_in(key, 1), (blocks,), jnp.float32, 0.0, math.log(8.0)))
    chosen = jax.random.randint(jax.random.fold_in(key, 2), (), 0, half)
    place = jnp.arange(blocks, dtype=jnp.int32) % half
    heavy = (place == 0) | (place == chosen)
    levels = jnp.where(heavy, 24.0, levels) * 0.2
    shape = (blocks, CUST_DEV, CTOK, W)
    base = jnp.clip(jax.random.normal(jax.random.fold_in(key, 3), shape, jnp.float32), -6.0, 6.0)
    values = base * levels[:, None, None, None]
    return values.reshape(blocks * CUST_DEV, CTOK, W).astype(jnp.bfloat16)


def steps_of(rng, extent, shards, smallest, largest):
    factor_of = 1.0
    for dim, parts in shards:
        steps = jax.random.uniform(jax.random.fold_in(jax.random.fold_in(rng, 6), dim), (parts,), jnp.float32, smallest / len(shards), largest / len(shards))
        factor_of = factor_of * jnp.repeat(jnp.exp(steps), extent[dim] // parts).reshape((-1,) + (1,) * (len(extent) - 1 - dim))
    return factor_of


def scatter_about(key, dims, scale, most, cuts=(), kind=jnp.bfloat16):
    array = jax.random.normal(key, dims, jnp.float32) * scale
    if len(cuts) > 0:
        array = steps_of(key, dims, cuts, -0.22, 0.18) * array
    return jnp.clip(array, min=-most, max=most).astype(kind)


def setup_inputs(seed: int = 0) -> dict:
    key_list = jax.random.split(jax.random.key(seed), 20)
    return {
        "item_tokens": scatter_about(key_list[0], (TRANSACTIONS, COLS, W), 1.0, 6.0, ((0, 256),)),
        "owner_index": draw_owner_index(jax.random.fold_in(key_list[19], 71), 0),
        "owner_row": draw_owner_row(jax.random.fold_in(key_list[19], 71), 0),
        "parent_tokens": scatter_about(key_list[3], (CUSTOMERS, CTOK, W), 1.0, 6.0, ((0, 256),)),
        "cotangent": draw_cotangent(jax.random.fold_in(key_list[19], 71), 0),
        "column_gain": jnp.clip(1.0 + 0.1 * jax.random.normal(key_list[5], (W,), jnp.float32), 0.5, 1.5).astype(jnp.bfloat16),
        "column_query": scatter_about(key_list[6], (W, W), W ** -0.5, 0.375),
        "column_key": scatter_about(key_list[7], (W, W), W ** -0.5, 0.375),
        "column_value": scatter_about(key_list[8], (W, W), W ** -0.5, 0.375),
        "column_out": scatter_about(key_list[9], (W, W), W ** -0.5, 0.375),
        "hidden_gain": jnp.clip(1.0 + 0.1 * jax.random.normal(key_list[10], (W,), jnp.float32), 0.5, 1.5).astype(jnp.bfloat16),
        "up_weight": scatter_about(key_list[11], (W, FF), W ** -0.5, 0.375),
        "down_weight": scatter_about(key_list[12], (FF, W), FF ** -0.5, 0.1875),
        "link_weight": scatter_about(key_list[13], (W, W), W ** -0.5, 0.375),
        "parent_gain": jnp.clip(1.0 + 0.1 * jax.random.normal(key_list[14], (W,), jnp.float32), 0.5, 1.5).astype(jnp.bfloat16),
        "parent_query": scatter_about(key_list[15], (W, W), W ** -0.5, 0.375),
        "parent_key": scatter_about(key_list[16], (W, W), W ** -0.5, 0.375),
        "parent_value": scatter_about(key_list[17], (W, W), W ** -0.5, 0.375),
        "parent_out": scatter_about(key_list[18], (W, W), W ** -0.5, 0.375),
    }


EPSILON = 1e-06

def scaled_norm(values, gain_vec):
    mean_square = lax.optimization_barrier(jnp.mean(values * values, axis=-1, keepdims=True))
    return values * lax.rsqrt(mean_square + EPSILON) * gain_vec

def project(inputs, matrix):
    return jnp.einsum('...i,ij->...j', inputs.astype(jnp.float32), matrix)

def attention(tokens, gain_vec, query_matrix, key_matrix, value_matrix, out_matrix, head_count):
    row_count, length, feature = tokens.shape
    head_dim = feature // head_count
    normed = scaled_norm(tokens.astype(jnp.float32), gain_vec).astype(jnp.bfloat16)
    queries = project(normed, query_matrix).astype(jnp.bfloat16).reshape(row_count, length, head_count, head_dim)
    key_rows = project(normed, key_matrix).astype(jnp.bfloat16).reshape(row_count, length, head_count, head_dim)
    value_rows = project(normed, value_matrix).astype(jnp.bfloat16).reshape(row_count, length, head_count, head_dim)
    scores = jnp.einsum('blhd,bmhd->bhlm', queries, key_rows, preferred_element_type=jnp.float32) * head_dim ** (-0.5)
    weights = jax.nn.softmax(scores, axis=-1).astype(jnp.bfloat16)
    mixture = jnp.einsum('bhlm,bmhd->blhd', weights, value_rows, preferred_element_type=jnp.float32)
    mixture = mixture.reshape(row_count, length, feature).astype(jnp.bfloat16)
    return project(mixture, out_matrix)

def encode_rows(tokens, params):
    gain_first, query_matrix, key_matrix, value_matrix, out_matrix, gain_second, up_matrix, down_matrix = params
    stream = (tokens.astype(jnp.float32) + attention(tokens, gain_first, query_matrix, key_matrix, value_matrix, out_matrix, HEADS)).astype(jnp.bfloat16)
    normed = scaled_norm(stream.astype(jnp.float32), gain_second).astype(jnp.bfloat16)
    hidden = jax.nn.gelu(project(normed, up_matrix), approximate=True).astype(jnp.bfloat16)
    output_rows = stream.astype(jnp.float32) + project(hidden, down_matrix)
    return lax.optimization_barrier(jnp.mean(output_rows, axis=1)).astype(jnp.bfloat16)

def parent_forward(tokens, pooled, params):
    link_matrix, gain_vec, query_matrix, key_matrix, value_matrix, out_matrix = params
    linked = project(pooled, link_matrix)
    based = (tokens.astype(jnp.float32) + linked[:, None, :]).astype(jnp.bfloat16)
    return based.astype(jnp.float32) + attention(based, gain_vec, query_matrix, key_matrix, value_matrix, out_matrix, HEADS)

def reference(item_tokens, owner_index, owner_row, parent_tokens, cotangent, column_gain, column_query, column_key, column_value, column_out, hidden_gain, up_weight, down_weight, link_weight, parent_gain, parent_query, parent_key, parent_value, parent_out):
    item_params = tuple((weight.astype(jnp.float32) for weight in (column_gain, column_query, column_key, column_value, column_out, hidden_gain, up_weight, down_weight)))
    parent_params = tuple((weight.astype(jnp.float32) for weight in (link_weight, parent_gain, parent_query, parent_key, parent_value, parent_out)))
    blocks = N_DP * N_REP
    grouped = item_tokens.reshape(blocks, TX_DEV, COLS, W)
    embedded = lax.map(lambda tokens: encode_rows(tokens, item_params), grouped).reshape(blocks * TX_DEV, W)
    block_of = jnp.arange(blocks * TX_DEV, dtype=jnp.int32) // TX_DEV
    target = ((owner_index * N_REP + block_of % N_REP) * CUST_DEV + owner_row).astype(jnp.int32)
    sum_rows = jax.ops.segment_sum(embedded.astype(jnp.float32), target, num_segments=CUSTOMERS)
    counts = jax.ops.segment_sum(jnp.ones(target.shape, jnp.float32), target, num_segments=CUSTOMERS)
    divisor = jnp.maximum(counts, 1.0)[:, None]
    pooled = (sum_rows / divisor).astype(jnp.bfloat16)
    loss_scale = 1.0 / math.sqrt(CUSTOMERS * CTOK)

    def parent_step(carry, inputs):
        tokens, pooled_block, cot_block = inputs
        states, pullback = jax.vjp(lambda params, pooled_in: parent_forward(tokens, pooled_in, params), parent_params, pooled_block)
        gradients, pooled_grad = pullback(cot_block.astype(jnp.float32) * loss_scale)
        return (jax.tree.map(jnp.add, carry, gradients), (states.astype(jnp.bfloat16), pooled_grad))
    parent_zero = tuple((jnp.zeros(weight.shape, jnp.float32) for weight in parent_params))
    parent_inputs = (parent_tokens.reshape(blocks, CUST_DEV, CTOK, W), pooled.reshape(blocks, CUST_DEV, W), cotangent.reshape(blocks, CUST_DEV, CTOK, W))
    parent_grads, (states, pooled_grads) = lax.scan(parent_step, parent_zero, parent_inputs)
    sum_grad = pooled_grads.reshape(CUSTOMERS, W).astype(jnp.float32) / divisor
    item_grad = sum_grad[target].astype(jnp.bfloat16).reshape(blocks, TX_DEV, W)

    def item_step(carry, inputs):
        tokens, grad_block = inputs
        unused, pullback = jax.vjp(lambda params: encode_rows(tokens, params), item_params)
        return (jax.tree.map(jnp.add, carry, pullback(grad_block)[0]), None)
    item_zero = tuple((jnp.zeros(weight.shape, jnp.float32) for weight in item_params))
    item_grads, unused_out = lax.scan(item_step, item_zero, (grouped, item_grad))
    parent_states = states.reshape(CUSTOMERS, CTOK, W)
    return (parent_states, item_grads[0], item_grads[1], item_grads[2], item_grads[3], item_grads[4], item_grads[5], item_grads[6], item_grads[7], parent_grads[0], parent_grads[1], parent_grads[2], parent_grads[3], parent_grads[4], parent_grads[5])
```

```python
import functools
import math

import jax
import jax.numpy as jnp
from jax import lax
from jax.experimental import pallas as pl
from jax.experimental.pallas import tpu as pltpu
from jax.sharding import PartitionSpec as P

HEADS = 8
EPSILON = 1e-06
MESH = pl.DeviceIdType.MESH
F32 = jnp.float32
BF16 = jnp.bfloat16
N_DP = 64


def place():
    dp, rep = lax.axis_index("dp"), lax.axis_index("rep")
    z, x, core = lax.div(dp, 8), lax.rem(lax.div(dp, 2), 4), lax.rem(dp, 2)
    first = (1 - core) * rep + core * x
    second = (1 - core) * x + core * rep
    return dp, rep, z, x, core, first, second


def core_peer(at):
    dp, rep, z, x, core, first, second = at
    return (dp + 1 - 2 * core, rep)


def first_peer(at, j):
    dp, rep, z, x, core, first, second = at
    return ((1 - core) * dp + core * (8 * z + 2 * j + core), (1 - core) * j + core * rep)


def second_peer(at, j):
    dp, rep, z, x, core, first, second = at
    return (core * dp + (1 - core) * (8 * z + 2 * j + core), core * j + (1 - core) * rep)


def z_peer(at, j):
    dp, rep, z, x, core, first, second = at
    return (8 * j + 2 * x + core, rep)


def greet_ring(at, barrier):
    dp, rep, z, x, core, first, second = at
    peers = [core_peer(at)]
    peers += [first_peer(at, lax.rem(first + d, 4)) for d in (1, 2, 3)]
    peers += [second_peer(at, lax.rem(second + d, 4)) for d in (1, 2, 3)]
    peers += [z_peer(at, lax.rem(z + d, 8)) for d in range(1, 8)]
    for peer in peers:
        pl.semaphore_signal(barrier, inc=1, device_id=peer, device_id_type=MESH)
    return len(peers)


def remote(src, dst, send, recv, peer):
    copy = pltpu.make_async_remote_copy(
        src_ref=src, dst_ref=dst, send_sem=send, recv_sem=recv, device_id=peer, device_id_type=MESH
    )
    copy.start()
    return copy


class Summing:
    def __init__(self, at, n, mine, total, scratch):
        self.at, self.n, self.mine, self.total = at, n, mine, total
        self.m = -(-2 * n // 8)
        (self.core_in, self.first_out, self.first_in, self.second_out, self.second_in,
         self.z_out, self.z_in, self.z_all, self.send, self.recv) = scratch
        self.copies = []

    @staticmethod
    def scratch(n):
        m = -(-2 * n // 8)
        return [
            pltpu.VMEM((4, 4, n, 16, 128), BF16),
            pltpu.VMEM((4, 4, n, 16, 128), BF16),
            pltpu.VMEM((3, 4, n, 16, 128), BF16),
            pltpu.VMEM((4, n, 16, 128), BF16),
            pltpu.VMEM((3, n, 16, 128), BF16),
            pltpu.VMEM((8, m, 8, 128), F32),
            pltpu.VMEM((7, m, 8, 128), F32),
            pltpu.VMEM((8, m, 8, 128), F32),
            pltpu.SemaphoreType.DMA((34,)),
            pltpu.SemaphoreType.DMA((34,)),
        ]

    def _send(self, src, dst, k, peer):
        copy = remote(src, dst, self.send.at[k], self.recv.at[k], peer)
        self.copies.append(copy)
        return copy

    def start(self):
        dp, rep, z, x, core, first, second = self.at
        self.from_core = []
        for k, d in enumerate((1, 2, 3, 0)):
            q = lax.rem(second + d, 4)
            self.from_core.append(
                self._send(self.mine.at[1 - core, q], self.core_in.at[q], k, core_peer(self.at))
            )

    def scatter_first(self):
        dp, rep, z, x, core, first, second = self.at
        self.from_first = []
        for k, d in enumerate((1, 2, 3, 0)):
            q = lax.rem(first + d, 4)
            self.from_core[k].wait_recv()
            both = self.mine[core, q].astype(F32) + self.core_in[q].astype(F32)
            self.first_out[q] = both.astype(BF16)
            if d:
                self.from_first.append(
                    self._send(self.first_out.at[q], self.first_in.at[d - 1], 3 + d, first_peer(self.at, q))
                )

    def scatter_second(self):
        dp, rep, z, x, core, first, second = self.at
        for copy in self.from_first:
            copy.wait_recv()
        self.from_second = []
        for d in (1, 2, 3, 0):
            q = lax.rem(second + d, 4)
            value = self.first_out[first, q].astype(F32)
            for i in range(3):
                value = value + self.first_in[i, q].astype(F32)
            self.second_out[q] = value.astype(BF16)
            if d:
                self.from_second.append(
                    self._send(self.second_out.at[q], self.second_in.at[d - 1], 6 + d, second_peer(self.at, q))
                )

    def scatter_z(self):
        dp, rep, z, x, core, first, second = self.at
        for copy in self.from_second:
            copy.wait_recv()
        value = self.second_out[second].astype(F32)
        for i in range(3):
            value = value + self.second_in[i].astype(F32)
        value = value.reshape(2 * self.n, 8, 128)
        extra = 8 * self.m - 2 * self.n
        if extra:
            value = jnp.concatenate([value, jnp.zeros((extra, 8, 128), F32)], axis=0)
        self.z_out[...] = value.reshape(8, self.m, 8, 128)
        self.from_z = []
        for d in range(1, 8):
            q = lax.rem(z + d, 8)
            self.from_z.append(
                self._send(self.z_out.at[q], self.z_in.at[d - 1], 9 + d, z_peer(self.at, q))
            )

    def gather_z(self):
        dp, rep, z, x, core, first, second = self.at
        for copy in self.from_z:
            copy.wait_recv()
        value = self.z_out[z]
        for i in range(7):
            value = value + self.z_in[i]
        self.z_all[z] = value
        self.from_z = []
        for d in range(1, 8):
            q = lax.rem(z + d, 8)
            self.from_z.append(
                self._send(self.z_all.at[z], self.z_all.at[z], 16 + d, z_peer(self.at, q))
            )

    def gather_second(self):
        dp, rep, z, x, core, first, second = self.at
        for copy in self.from_z:
            copy.wait_recv()
        value = self.z_all[...].reshape(8 * self.m, 8, 128)[: 2 * self.n]
        self.total[core, first, second] = value.reshape(self.n, 16, 128).astype(BF16)
        here = self.total.at[core, first, second]
        self.from_second = []
        for d in (1, 2, 3):
            q = lax.rem(second + d, 4)
            self.from_second.append(self._send(here, here, 23 + d, second_peer(self.at, q)))

    def gather_first(self):
        dp, rep, z, x, core, first, second = self.at
        for copy in self.from_second:
            copy.wait_recv()
        here = self.total.at[core, first]
        self.from_first = []
        for d in (1, 2, 3):
            q = lax.rem(first + d, 4)
            self.from_first.append(self._send(here, here, 26 + d, first_peer(self.at, q)))
        self.from_core = [self._send(here, here, 30, core_peer(self.at))]

    def gather_core(self):
        dp, rep, z, x, core, first, second = self.at
        for d, copy in zip((1, 2, 3), self.from_first, strict=True):
            copy.wait_recv()
            here = self.total.at[core, lax.rem(first + 4 - d, 4)]
            self.from_core.append(self._send(here, here, 30 + d, core_peer(self.at)))

    def finish(self):
        for copy in self.from_core:
            copy.wait_recv()
        for copy in self.copies:
            copy.wait_send()


def exchange_start(at, out_ref, in_ref, send, recv):
    dp, rep = at[:2]
    in_ref[dp] = out_ref[dp]

    def step(d, carry):
        j = lax.rem(dp + d, N_DP)
        remote(out_ref.at[j], in_ref.at[dp], send, recv, (j, rep))
        return carry

    lax.fori_loop(1, N_DP, step, 0)


def exchange_wait(at, out_ref, in_ref, send, recv):
    rest = pl.ds(0, N_DP - 1)
    copy = pltpu.make_async_remote_copy(
        src_ref=out_ref.at[rest], dst_ref=in_ref.at[rest], send_sem=send, recv_sem=recv,
        device_id=core_peer(at), device_id_type=MESH,
    )
    copy.wait_recv()
    copy.wait_send()


def greet_group(at, barrier):
    dp, rep = at[:2]

    def step(d, carry):
        pl.semaphore_signal(
            barrier, inc=1, device_id=(lax.rem(dp + d, N_DP), rep), device_id_type=MESH
        )
        return carry

    lax.fori_loop(1, N_DP, step, 0)
    return N_DP - 1


VMEM_LIMIT = 48 * 1024 * 1024


def exchange_kernel(out_ref, in_ref, send, recv):
    at = place()
    barrier = pltpu.get_barrier_semaphore()
    pl.semaphore_wait(barrier, greet_group(at, barrier))
    exchange_start(at, out_ref, in_ref, send, recv)
    exchange_wait(at, out_ref, in_ref, send, recv)


def exchange(rows, collective_id):
    return pl.pallas_call(
        exchange_kernel,
        out_shape=jax.ShapeDtypeStruct(rows.shape, rows.dtype),
        in_specs=[pl.BlockSpec(memory_space=pltpu.VMEM)],
        out_specs=pl.BlockSpec(memory_space=pltpu.VMEM),
        scratch_shapes=[pltpu.SemaphoreType.DMA, pltpu.SemaphoreType.DMA],
        compiler_params=pltpu.CompilerParams(
            collective_id=collective_id, has_side_effects=True, vmem_limit_bytes=VMEM_LIMIT
        ),
    )(rows)


def summing_kernel(n, mine_ref, total_ref, *scratch):
    at = place()
    barrier = pltpu.get_barrier_semaphore()
    pl.semaphore_wait(barrier, greet_ring(at, barrier))
    job = Summing(at, n, mine_ref, total_ref, scratch)
    job.start()
    job.scatter_first()
    job.scatter_second()
    job.scatter_z()
    job.gather_z()
    job.gather_second()
    job.gather_first()
    job.gather_core()
    job.finish()


def summed_over_devices(mine, collective_id):
    n = mine.shape[3]
    return pl.pallas_call(
        functools.partial(summing_kernel, n),
        out_shape=jax.ShapeDtypeStruct(mine.shape, mine.dtype),
        in_specs=[pl.BlockSpec(memory_space=pltpu.VMEM)],
        out_specs=pl.BlockSpec(memory_space=pltpu.VMEM),
        scratch_shapes=Summing.scratch(n),
        compiler_params=pltpu.CompilerParams(
            collective_id=collective_id, has_side_effects=True, vmem_limit_bytes=VMEM_LIMIT
        ),
    )(mine)


def scaled_norm(values, gain_vec):
    mean_square = jnp.mean(values * values, axis=-1, keepdims=True)
    return values * lax.rsqrt(mean_square + EPSILON) * gain_vec


def project(inputs, matrix):
    return jnp.einsum("...i,ij->...j", inputs.astype(jnp.float32), matrix)


def attention(tokens, gain_vec, query_matrix, key_matrix, value_matrix, out_matrix, head_count):
    row_count, length, feature = tokens.shape
    head_dim = feature // head_count
    normed = scaled_norm(tokens.astype(jnp.float32), gain_vec).astype(jnp.bfloat16)
    queries = (
        project(normed, query_matrix)
        .astype(jnp.bfloat16)
        .reshape(row_count, length, head_count, head_dim)
    )
    key_rows = (
        project(normed, key_matrix)
        .astype(jnp.bfloat16)
        .reshape(row_count, length, head_count, head_dim)
    )
    value_rows = (
        project(normed, value_matrix)
        .astype(jnp.bfloat16)
        .reshape(row_count, length, head_count, head_dim)
    )
    scores = jnp.einsum(
        "blhd,bmhd->bhlm", queries, key_rows, preferred_element_type=jnp.float32
    ) * head_dim ** (-0.5)
    weights = jax.nn.softmax(scores, axis=-1).astype(jnp.bfloat16)
    mixture = jnp.einsum("bhlm,bmhd->blhd", weights, value_rows, preferred_element_type=jnp.float32)
    mixture = mixture.reshape(row_count, length, feature).astype(jnp.bfloat16)
    return project(mixture, out_matrix)


def encode_rows(tokens, params):
    (
        gain_first,
        query_matrix,
        key_matrix,
        value_matrix,
        out_matrix,
        gain_second,
        up_matrix,
        down_matrix,
    ) = params
    stream = (
        tokens.astype(jnp.float32)
        + attention(tokens, gain_first, query_matrix, key_matrix, value_matrix, out_matrix, HEADS)
    ).astype(jnp.bfloat16)
    normed = scaled_norm(stream.astype(jnp.float32), gain_second).astype(jnp.bfloat16)
    hidden = jax.nn.gelu(project(normed, up_matrix), approximate=True).astype(jnp.bfloat16)
    output_rows = stream.astype(jnp.float32) + project(hidden, down_matrix)
    return jnp.mean(output_rows, axis=1).astype(jnp.bfloat16)


def parent_forward(tokens, pooled, params):
    link_matrix, gain_vec, query_matrix, key_matrix, value_matrix, out_matrix = params
    linked = project(pooled, link_matrix)
    based = (tokens.astype(jnp.float32) + linked[:, None, :]).astype(jnp.bfloat16)
    return based.astype(jnp.float32) + attention(
        based, gain_vec, query_matrix, key_matrix, value_matrix, out_matrix, HEADS
    )


def body(
    item_tokens,
    owner_index,
    owner_row,
    parent_tokens,
    cotangent,
    column_gain,
    column_query,
    column_key,
    column_value,
    column_out,
    hidden_gain,
    up_weight,
    down_weight,
    link_weight,
    parent_gain,
    parent_query,
    parent_key,
    parent_value,
    parent_out,
):
    item_params = tuple(
        (
            weight.astype(jnp.float32)
            for weight in (
                column_gain,
                column_query,
                column_key,
                column_value,
                column_out,
                hidden_gain,
                up_weight,
                down_weight,
            )
        )
    )
    parent_params = tuple(
        (
            weight.astype(jnp.float32)
            for weight in (
                link_weight,
                parent_gain,
                parent_query,
                parent_key,
                parent_value,
                parent_out,
            )
        )
    )
    dp_count = lax.axis_size("dp")
    rep_count = lax.axis_size("rep")
    item_count = item_tokens.shape[0]
    parent_count = parent_tokens.shape[0]
    feature = item_tokens.shape[2]
    embedded, item_pullback = jax.vjp(lambda params: encode_rows(item_tokens, params), item_params)
    slot_count = max(2, 2 * item_count // dp_count)
    positions = jnp.arange(item_count)
    earlier = (owner_index[None, :] == owner_index[:, None]) & (
        positions[None, :] < positions[:, None]
    )
    slot_index = owner_index * slot_count + jnp.sum(earlier.astype(jnp.int32), axis=1)
    placing = slot_index[None, :] == jnp.arange(dp_count * slot_count)[:, None]
    send_rows = jnp.dot(
        placing.astype(jnp.bfloat16), embedded, preferred_element_type=jnp.float32
    ).astype(jnp.bfloat16)
    send_ids = jnp.sum(placing.astype(jnp.int32) * (owner_row + 1)[None, :], axis=1)
    packed = jnp.concatenate(
        [
            send_rows.astype(F32).reshape(dp_count, 4, 128),
            jnp.broadcast_to(send_ids.astype(F32).reshape(dp_count, 2, 1), (dp_count, 2, 128)),
            jnp.zeros((dp_count, 2, 128), F32),
        ],
        axis=1,
    )
    got = exchange(packed, 1)
    got_rows = got[:, :4].astype(BF16).reshape(dp_count * slot_count, feature)
    got_ids = got[:, 4:6, 0].astype(jnp.int32)
    member = got_ids.reshape(-1)[None, :] == jnp.arange(1, parent_count + 1)[:, None]
    counts = jnp.sum(member.astype(jnp.float32), axis=1)
    sum_rows = jnp.dot(member.astype(jnp.bfloat16), got_rows, preferred_element_type=jnp.float32)
    divisor = jnp.maximum(counts, 1.0)[:, None]
    pooled = (sum_rows / divisor).astype(jnp.bfloat16)
    states, parent_pullback = jax.vjp(
        lambda params, pooled_in: parent_forward(parent_tokens, pooled_in, params),
        parent_params,
        pooled,
    )
    loss_scale = 1.0 / math.sqrt(parent_count * dp_count * rep_count * parent_tokens.shape[1])
    parent_grads, pooled_grad = parent_pullback(cotangent.astype(jnp.float32) * loss_scale)
    sum_grad = pooled_grad.astype(jnp.float32) / divisor
    slot_grad = jnp.dot(member.T.astype(jnp.float32), sum_grad).astype(jnp.bfloat16)
    returned = exchange(
        jnp.concatenate(
            [slot_grad.astype(F32).reshape(dp_count, 4, 128), jnp.zeros((dp_count, 4, 128), F32)], axis=1
        ),
        2,
    )[:, :4].astype(BF16)
    item_grad = jnp.dot(
        placing.T.astype(jnp.bfloat16),
        returned.reshape(dp_count * slot_count, feature),
        preferred_element_type=jnp.float32,
    ).astype(jnp.bfloat16)
    item_grads = item_pullback(item_grad)[0]
    gradients = tuple(item_grads) + tuple(parent_grads)
    matrices = [gradient for gradient in gradients if gradient.ndim == 2]
    gains = [gradient for gradient in gradients if gradient.ndim == 1]
    flattened = jnp.concatenate([gradient.reshape(-1) for gradient in matrices]).astype(BF16)
    summed = summed_over_devices(flattened.reshape(2, 4, 4, 17, 16, 128), 3).astype(F32).reshape(-1)
    gain_sums = list(lax.psum(jnp.stack(gains), ("dp", "rep")))
    outputs = []
    offset = 0
    for gradient in gradients:
        if gradient.ndim == 1:
            outputs.append(gain_sums.pop(0))
            continue
        outputs.append(summed[offset : offset + gradient.size].reshape(gradient.shape))
        offset = offset + gradient.size
    return (states.astype(jnp.bfloat16),) + tuple(outputs)


def solution(mesh):
    return jax.shard_map(
        body,
        mesh=mesh,
        in_specs=(
            P(("dp", "rep"), None, None),
            P(("dp", "rep")),
            P(("dp", "rep")),
            P(("dp", "rep"), None, None),
            P(("dp", "rep"), None, None),
            P(),
            P(),
            P(),
            P(),
            P(),
            P(),
            P(),
            P(),
            P(),
            P(),
            P(),
            P(),
            P(),
            P(),
        ),
        out_specs=(
            P(("dp", "rep"), None, None),
            P(),
            P(),
            P(),
            P(),
            P(),
            P(),
            P(),
            P(),
            P(),
            P(),
            P(),
            P(),
            P(),
            P(),
        ),
        check_vma=False,
    )
```

```python
import math

import jax
import jax.numpy as jnp
from jax import lax
from jax.experimental import pallas as pl
from jax.experimental.pallas import tpu as pltpu
from jax.sharding import PartitionSpec as P

MESH = pl.DeviceIdType.MESH
F32 = jnp.float32
BF16 = jnp.bfloat16
N_DP = 64


def place():
    dp, rep = lax.axis_index("dp"), lax.axis_index("rep")
    z, x, core = lax.div(dp, 8), lax.rem(lax.div(dp, 2), 4), lax.rem(dp, 2)
    first = (1 - core) * rep + core * x
    second = (1 - core) * x + core * rep
    return dp, rep, z, x, core, first, second


def core_peer(at):
    dp, rep, z, x, core, first, second = at
    return (dp + 1 - 2 * core, rep)


def first_peer(at, j):
    dp, rep, z, x, core, first, second = at
    return ((1 - core) * dp + core * (8 * z + 2 * j + core), (1 - core) * j + core * rep)


def second_peer(at, j):
    dp, rep, z, x, core, first, second = at
    return (core * dp + (1 - core) * (8 * z + 2 * j + core), core * j + (1 - core) * rep)


def z_peer(at, j):
    dp, rep, z, x, core, first, second = at
    return (8 * j + 2 * x + core, rep)


def remote(src, dst, send, recv, peer):
    copy = pltpu.make_async_remote_copy(
        src_ref=src, dst_ref=dst, send_sem=send, recv_sem=recv, device_id=peer, device_id_type=MESH
    )
    copy.start()
    return copy


class Summing:
    def __init__(self, at, n, mine, total, scratch):
        self.at, self.n, self.mine, self.total = at, n, mine, total
        self.m = -(-2 * n // 8)
        (self.core_in, self.first_out, self.first_in, self.second_out, self.second_in,
         self.z_out, self.z_in, self.z_all, self.send, self.recv) = scratch
        self.copies = []

    @staticmethod
    def scratch(n):
        m = -(-2 * n // 8)
        return [
            pltpu.VMEM((4, 4, n, 16, 128), BF16),
            pltpu.VMEM((4, 4, n, 16, 128), BF16),
            pltpu.VMEM((3, 4, n, 16, 128), BF16),
            pltpu.VMEM((4, n, 16, 128), BF16),
            pltpu.VMEM((3, n, 16, 128), BF16),
            pltpu.VMEM((8, m, 8, 128), F32),
            pltpu.VMEM((7, m, 8, 128), F32),
            pltpu.VMEM((8, m, 8, 128), F32),
            pltpu.SemaphoreType.DMA((34,)),
            pltpu.SemaphoreType.DMA((34,)),
        ]

    def _send(self, src, dst, k, peer):
        copy = remote(src, dst, self.send.at[k], self.recv.at[k], peer)
        self.copies.append(copy)
        return copy

    def start(self):
        dp, rep, z, x, core, first, second = self.at
        self.from_core = []
        for k, d in enumerate((1, 2, 3, 0)):
            q = lax.rem(second + d, 4)
            self.from_core.append(
                self._send(self.mine.at[1 - core, q], self.core_in.at[q], k, core_peer(self.at))
            )

    def scatter_first(self):
        dp, rep, z, x, core, first, second = self.at
        self.from_first = []
        for k, d in enumerate((1, 2, 3, 0)):
            q = lax.rem(first + d, 4)
            self.from_core[k].wait_recv()
            both = self.mine[core, q].astype(F32) + self.core_in[q].astype(F32)
            self.first_out[q] = both.astype(BF16)
            if d:
                self.from_first.append(
                    self._send(self.first_out.at[q], self.first_in.at[d - 1], 3 + d, first_peer(self.at, q))
                )

    def scatter_second(self):
        dp, rep, z, x, core, first, second = self.at
        for copy in self.from_first:
            copy.wait_recv()
        self.from_second = []
        for d in (1, 2, 3, 0):
            q = lax.rem(second + d, 4)
            value = self.first_out[first, q].astype(F32)
            for i in range(3):
                value = value + self.first_in[i, q].astype(F32)
            self.second_out[q] = value.astype(BF16)
            if d:
                self.from_second.append(
                    self._send(self.second_out.at[q], self.second_in.at[d - 1], 6 + d, second_peer(self.at, q))
                )

    def scatter_z(self):
        dp, rep, z, x, core, first, second = self.at
        for copy in self.from_second:
            copy.wait_recv()
        value = self.second_out[second].astype(F32)
        for i in range(3):
            value = value + self.second_in[i].astype(F32)
        value = value.reshape(2 * self.n, 8, 128)
        extra = 8 * self.m - 2 * self.n
        if extra:
            value = jnp.concatenate([value, jnp.zeros((extra, 8, 128), F32)], axis=0)
        self.z_out[...] = value.reshape(8, self.m, 8, 128)
        self.from_z = []
        for d in range(1, 8):
            q = lax.rem(z + d, 8)
            self.from_z.append(
                self._send(self.z_out.at[q], self.z_in.at[d - 1], 9 + d, z_peer(self.at, q))
            )

    def gather_z(self):
        dp, rep, z, x, core, first, second = self.at
        for copy in self.from_z:
            copy.wait_recv()
        value = self.z_out[z]
        for i in range(7):
            value = value + self.z_in[i]
        self.z_all[z] = value
        self.from_z = []
        for d in range(1, 8):
            q = lax.rem(z + d, 8)
            self.from_z.append(
                self._send(self.z_all.at[z], self.z_all.at[z], 16 + d, z_peer(self.at, q))
            )

    def gather_second(self):
        dp, rep, z, x, core, first, second = self.at
        for copy in self.from_z:
            copy.wait_recv()
        value = self.z_all[...].reshape(8 * self.m, 8, 128)[: 2 * self.n]
        self.total[core, first, second] = value.reshape(self.n, 16, 128).astype(BF16)
        here = self.total.at[core, first, second]
        self.from_second = []
        for d in (1, 2, 3):
            q = lax.rem(second + d, 4)
            self.from_second.append(self._send(here, here, 23 + d, second_peer(self.at, q)))

    def gather_first(self):
        dp, rep, z, x, core, first, second = self.at
        for copy in self.from_second:
            copy.wait_recv()
        here = self.total.at[core, first]
        self.from_first = []
        for d in (1, 2, 3):
            q = lax.rem(first + d, 4)
            self.from_first.append(self._send(here, here, 26 + d, first_peer(self.at, q)))
        self.from_core = [self._send(here, here, 30, core_peer(self.at))]

    def gather_core(self):
        dp, rep, z, x, core, first, second = self.at
        for d, copy in zip((1, 2, 3), self.from_first, strict=True):
            copy.wait_recv()
            here = self.total.at[core, lax.rem(first + 4 - d, 4)]
            self.from_core.append(self._send(here, here, 30 + d, core_peer(self.at)))

    def finish(self):
        for copy in self.from_core:
            copy.wait_recv()
        for copy in self.copies:
            copy.wait_send()


def exchange_start(at, out_ref, in_ref, send, recv):
    dp, rep = at[:2]
    in_ref[dp] = out_ref[dp]

    def to(d):
        j = lax.rem(dp + d, N_DP)
        remote(out_ref.at[j], in_ref.at[dp], send, recv, (j, rep))

    def step(d, carry):
        to(N_DP // 2 - d)
        to(N_DP // 2 + d)
        return carry

    to(N_DP // 2)
    lax.fori_loop(1, N_DP // 2, step, 0)


def exchange_wait(at, out_ref, in_ref, send, recv):
    rest = pl.ds(0, N_DP - 1)
    copy = pltpu.make_async_remote_copy(
        src_ref=out_ref.at[rest], dst_ref=in_ref.at[rest], send_sem=send, recv_sem=recv,
        device_id=core_peer(at), device_id_type=MESH,
    )
    copy.wait_recv()
    copy.wait_send()


def greet_all(at, barrier):
    dp, rep = at[:2]

    def step(d, carry):
        pl.semaphore_signal(
            barrier, inc=1, device_id=(lax.rem(dp + d, N_DP), rep), device_id_type=MESH
        )
        return carry

    lax.fori_loop(1, N_DP, step, 0)
    for d in (1, 2, 3):
        pl.semaphore_signal(
            barrier, inc=1, device_id=(dp, lax.rem(rep + d, 4)), device_id_type=MESH
        )
    return N_DP + 2


VMEM_LIMIT = 56 * 1024 * 1024
EPSILON = 1e-06
HEADS = 8
W = 256
HEAD = 32
FF = 1024
TX, COLS = 24, 24
CUST, CTOK = 16, 32
ROWS = TX * COLS
PROWS = CUST * CTOK
GROUP = 4
GROWS = GROUP * COLS
GPROWS = GROUP * CTOK
GROUPS = TX // GROUP
PGROUPS = CUST // GROUP


def dot(a, b):
    return lax.dot_general(a, b, (((1,), (0,)), ((), ())), preferred_element_type=F32)


def dot_nt(a, b):
    return lax.dot_general(a, b, (((1,), (1,)), ((), ())), preferred_element_type=F32)


def dot_tn(a, b):
    return lax.dot_general(a, b, (((0,), (0,)), ((), ())), preferred_element_type=F32)


def each(count, step, body, unroll=1):
    def one(i, carry):
        body(pl.ds(pl.multiple_of(i * step, step), step), i)
        return carry

    lax.fori_loop(0, count, one, 0, unroll=unroll)


def head_masks():
    lane = lax.broadcasted_iota(jnp.int32, (1, W), 1)
    return [jnp.where(lax.div(lane, HEAD) == h, 1.0, 0.0) for h in range(HEADS)]


def spread_heads(value, masks):
    return jnp.concatenate([value * mask.astype(BF16) for mask in masks], axis=0)


def join_heads(value, masks, rows):
    total = value[:rows] * masks[0]
    for h in range(1, HEADS):
        total = total + value[h * rows : (h + 1) * rows] * masks[h]
    return total


def same_owner(rows, length):
    i = lax.div(lax.broadcasted_iota(jnp.int32, (rows, rows), 0), length)
    j = lax.div(lax.broadcasted_iota(jnp.int32, (rows, rows), 1), length)
    return jnp.concatenate([jnp.where(i == j, 0.0, -1e30)] * HEADS, axis=0)


def attend(q, k, v, probs, mix, groups, rows, length):
    masks = head_masks()
    bias = same_owner(rows, length)

    def body(at, i):
        wide = spread_heads(q[at], masks)
        scores = dot_nt(wide, k[at]) * HEAD**-0.5 + bias
        e = jnp.exp(scores - jnp.max(scores, axis=1, keepdims=True))
        p = (e * (1.0 / jnp.sum(e, axis=1, keepdims=True))).astype(BF16)
        probs[i] = p
        mix[at] = join_heads(dot(p, v[at]), masks, rows).astype(BF16)

    each(groups, rows, body)


def attend_back(q, k, v, probs, dmix, dqkv, groups, rows):
    masks = head_masks()

    def body(at, i):
        p = probs[i]
        wide_d = spread_heads(dmix[at], masks)
        wide_q = spread_heads(q[at], masks)
        dp = dot_nt(wide_d, v[at]).astype(BF16).astype(F32)
        weighted = p.astype(F32)
        ds = weighted * (dp - jnp.sum(weighted * dp, axis=1, keepdims=True))
        ds = (ds * HEAD**-0.5).astype(BF16)
        dqkv[at, 0:W] = join_heads(dot(ds, k[at]), masks, rows).astype(BF16)
        dqkv[at, W : 2 * W] = dot_tn(ds, wide_q).astype(BF16)
        dqkv[at, 2 * W : 3 * W] = dot_tn(p, wide_d).astype(BF16)

    each(groups, rows, body)


def put_block(mine, b, value):
    for half in range(2):
        part = value[:, half * 128 : (half + 1) * 128].astype(BF16)
        mine[half, :, :, b] = part.reshape(4, 4, 16, 128)


def rms_scale(value):
    return lax.rsqrt(jnp.mean(value * value, axis=1, keepdims=True) + EPSILON)


def averaging():
    t = lax.broadcasted_iota(jnp.int32, (TX, ROWS), 0)
    r = lax.div(lax.broadcasted_iota(jnp.int32, (TX, ROWS), 1), COLS)
    return jnp.where(t == r, 1.0, 0.0).astype(BF16)


def placing(owner_ref):
    owner = owner_ref[...]
    i = lax.broadcasted_iota(jnp.int32, (TX, TX), 0)
    j = lax.broadcasted_iota(jnp.int32, (TX, TX), 1)
    along = jnp.broadcast_to(owner, (TX, TX))
    down = jnp.sum(jnp.where(i == j, along, 0), axis=1, keepdims=True)
    slot = jnp.sum(jnp.where((down == along) & (i < j), 1, 0), axis=0, keepdims=True)
    device = lax.broadcasted_iota(jnp.int32, (N_DP, TX), 0)
    goes = device == jnp.broadcast_to(owner, (N_DP, TX))
    return [
        jnp.where(goes & (jnp.broadcast_to(slot, (N_DP, TX)) == s), 1.0, 0.0).astype(BF16)
        for s in range(2)
    ]


def encoder_kernel(
    item_ref, owner_ref, row_ref, parent_ref, cot_ref,
    cgain, cq, ck, cv, co, hgain, up, down, link, pgain, pq, pk, pv, po,
    states_ref, parent_sum, mlp_sum, att_sum,
    n1, q, k, v, probs, mix, s_, n2, u, h, slope, dn2, da, dmix, dqkv, hmean,
    pbased, pn, pq_, pk_, pv_, pprobs, pmix, pda, pdmix, pdqkv, pdn,
    parent_mine, mlp_mine, att_mine,
    out1, in1, out2, in2, x_send, x_recv,
    *job_scratch,
):
    at = place()
    barrier = pltpu.get_barrier_semaphore()
    greeted = greet_all(at, barrier)
    per = len(job_scratch) // 3
    parent_job = Summing(at, 5, parent_mine, parent_sum, job_scratch[:per])
    mlp_job = Summing(at, 8, mlp_mine, mlp_sum, job_scratch[per : 2 * per])
    att_job = Summing(at, 4, att_mine, att_sum, job_scratch[2 * per :])

    def norm_items(rows, i):
        x = item_ref[pl.ds(i * GROUP, GROUP)].astype(F32).reshape(GROWS, W)
        n1[rows] = (x * rms_scale(x) * cgain[...].astype(F32)).astype(BF16)

    each(GROUPS, GROWS, norm_items, unroll=2)
    q[...] = dot(n1[...], cq[...]).astype(BF16)
    k[...] = dot(n1[...], ck[...]).astype(BF16)
    v[...] = dot(n1[...], cv[...]).astype(BF16)
    attend(q, k, v, probs, mix, GROUPS, GROWS, COLS)
    u[:, :W] = dot(mix[...], co[...])

    def norm_stream(rows, i):
        x = item_ref[pl.ds(i * GROUP, GROUP)].astype(F32).reshape(GROWS, W)
        stream = (x + u[rows, :W]).astype(BF16)
        s_[rows] = stream
        stream = stream.astype(F32)
        n2[rows] = (stream * rms_scale(stream) * hgain[...].astype(F32)).astype(BF16)

    each(GROUPS, GROWS, norm_stream, unroll=2)
    u[...] = dot(n2[...], up[...])

    def gelu(rows, i):
        for c in range(0, FF, 256):
            value = u[rows, c : c + 256]
            square = value * value
            t = jnp.tanh(math.sqrt(2.0 / math.pi) * value * (1.0 + 0.044715 * square))
            half = 0.5 * (1.0 + t)
            h[rows, c : c + 256] = (value * half).astype(BF16)
            inner = math.sqrt(2.0 / math.pi) * (1.0 + 3 * 0.044715 * square)
            slope[rows, c : c + 256] = (half + 0.5 * value * (1.0 - t * t) * inner).astype(BF16)

    each(ROWS // 32, 32, gelu)
    average = averaging()
    hidden = (dot(average, h[...]) * (1.0 / COLS)).astype(BF16)
    hmean[...] = hidden
    embedding = (dot(average, s_[...]) * (1.0 / COLS) + dot(hidden, down[...])).astype(BF16)

    places = placing(owner_ref)
    ids = jnp.broadcast_to(row_ref[...].astype(F32) + 1.0, (128, TX)).astype(BF16)
    for slot in range(2):
        moved = dot(places[slot], embedding)
        out1[:, 2 * slot, :] = moved[:, :128]
        out1[:, 2 * slot + 1, :] = moved[:, 128:]
        out1[:, 4 + slot, :] = dot_nt(places[slot], ids)
        out1[:, 6 + slot, :] = jnp.zeros((N_DP, 128), F32)
    pl.semaphore_wait(barrier, greeted)
    exchange_start(at, out1, in1, x_send.at[0], x_recv.at[0])
    exchange_wait(at, out1, in1, x_send.at[0], x_recv.at[0])

    members = []
    customer = lax.broadcasted_iota(jnp.int32, (N_DP, CUST), 1).astype(F32) + 1.0
    counts, sums = jnp.zeros((CUST, W), F32), jnp.zeros((CUST, W), F32)
    for slot in range(2):
        got = jnp.concatenate([in1[:, 2 * slot, :], in1[:, 2 * slot + 1, :]], axis=1).astype(BF16)
        member = jnp.where(in1[:, 4 + slot, :][:, :CUST] == customer, 1.0, 0.0).astype(BF16)
        members.append(member)
        counts = counts + dot_tn(member, jnp.ones((N_DP, W), BF16))
        sums = sums + dot_tn(member, got)
    divisor = jnp.maximum(counts, 1.0)
    pooled = (sums / divisor).astype(BF16)
    linked = dot(pooled, link[...])
    scale = 1.0 / math.sqrt(CUST * CTOK * 256)
    pbased_value = (
        (parent_ref[...].astype(F32).reshape(CUST, CTOK, W) + linked[:, None, :])
        .astype(BF16)
        .reshape(PROWS, W)
    )
    pbased[...] = pbased_value

    def norm_based(rows, i):
        x = pbased[rows].astype(F32)
        pn[rows] = (x * rms_scale(x) * pgain[...].astype(F32)).astype(BF16)
        pda[rows] = (cot_ref[rows].astype(F32) * scale).astype(BF16)

    each(PGROUPS, GPROWS, norm_based, unroll=2)
    pq_[...] = dot(pn[...], pq[...]).astype(BF16)
    pk_[...] = dot(pn[...], pk[...]).astype(BF16)
    pv_[...] = dot(pn[...], pv[...]).astype(BF16)
    pdmix[...] = dot_nt(pda[...], po[...]).astype(BF16)
    attend(pq_, pk_, pv_, pprobs, pmix, PGROUPS, GPROWS, CTOK)
    attend_back(pq_, pk_, pv_, pprobs, pdmix, pdqkv, PGROUPS, GPROWS)
    pdn[...] = (
        dot_nt(pdqkv[:, :W], pq[...])
        + dot_nt(pdqkv[:, W : 2 * W], pk[...])
        + dot_nt(pdqkv[:, 2 * W :], pv[...])
    )

    dlinked = []
    for i in range(PGROUPS):
        rows = slice(i * GPROWS, (i + 1) * GPROWS)
        x = pbased[rows].astype(F32)
        r = rms_scale(x)
        unit = x * r
        dunit = pdn[rows] * pgain[...].astype(F32)
        dx = r * (dunit - unit * jnp.mean(dunit * unit, axis=1, keepdims=True))
        dx = dx + cot_ref[rows].astype(F32) * scale
        dlinked.append(jnp.sum(dx.reshape(GROUP, CTOK, W), axis=1))
    dlinked = jnp.concatenate(dlinked, axis=0)
    dpooled = dot_nt(dlinked.astype(BF16), link[...]).astype(BF16).astype(F32)
    sum_grad = (dpooled / divisor).astype(BF16)
    for slot in range(2):
        moved = dot(members[slot], sum_grad)
        out2[:, 2 * slot, :] = moved[:, :128]
        out2[:, 2 * slot + 1, :] = moved[:, 128:]
        out2[:, 4 + slot, :] = jnp.zeros((N_DP, 128), F32)
        out2[:, 6 + slot, :] = jnp.zeros((N_DP, 128), F32)
    exchange_start(at, out2, in2, x_send.at[1], x_recv.at[1])

    put_block(parent_mine, 0, dot_tn(pooled, dlinked.astype(BF16)))
    dweights = dot_tn(pn[...], pdqkv[...])
    for b in range(3):
        put_block(parent_mine, 1 + b, dweights[:, b * W : (b + 1) * W])
    put_block(parent_mine, 4, dot_tn(pmix[...], pda[...]))
    parent_job.start()
    states_ref[...] = (pbased[...].astype(F32) + dot(pmix[...], po[...])).astype(BF16)
    exchange_wait(at, out2, in2, x_send.at[1], x_recv.at[1])

    ditem = jnp.zeros((TX, W), F32)
    for slot in range(2):
        got = jnp.concatenate([in2[:, 2 * slot, :], in2[:, 2 * slot + 1, :]], axis=1).astype(BF16)
        ditem = ditem + dot_tn(places[slot], got)
    ditem_b = ditem.astype(BF16)
    dhidden = (dot_nt(ditem_b, down[...]) * (1.0 / COLS)).astype(BF16)

    spread = averaging()
    u[...] = dot_tn(spread, dhidden)
    dy = dot_tn(spread, ditem_b)

    def back_hidden(rows, i):
        for c in range(0, FF, 256):
            h[rows, c : c + 256] = (
                u[rows, c : c + 256] * slope[rows, c : c + 256].astype(F32)
            ).astype(BF16)

    each(ROWS // 32, 32, back_hidden)
    ddown = dot_tn(hmean[...], ditem_b)
    for b in range(4):
        put_block(mlp_mine, b, ddown[b * W : (b + 1) * W])
    dup = dot_tn(n2[...], h[...])
    for b in range(4):
        put_block(mlp_mine, 4 + b, dup[:, b * W : (b + 1) * W])
    mlp_job.start()
    parent_job.scatter_first()
    u[:, :W] = dot_nt(h[...], up[...])
    u[:, W : 2 * W] = dy

    def back_stream(rows, i):
        x = s_[rows].astype(F32)
        r = rms_scale(x)
        unit = x * r
        dunit = u[rows, :W].astype(BF16).astype(F32) * hgain[...].astype(F32)
        dx = r * (dunit - unit * jnp.mean(dunit * unit, axis=1, keepdims=True))
        da[rows] = (dx + u[rows, W : 2 * W] * (1.0 / COLS)).astype(BF16)

    each(GROUPS, GROWS, back_stream, unroll=2)
    dmix[...] = dot_nt(da[...], co[...]).astype(BF16)
    put_block(att_mine, 3, dot_tn(mix[...], da[...]))
    mlp_job.scatter_first()
    parent_job.scatter_second()
    attend_back(q, k, v, probs, dmix, dqkv, GROUPS, GROWS)
    dweights = dot_tn(n1[...], dqkv[...])
    for b in range(3):
        put_block(att_mine, b, dweights[:, b * W : (b + 1) * W])
    att_job.start()

    mlp_job.scatter_second()
    att_job.scatter_first()
    parent_job.scatter_z()
    mlp_job.scatter_z()
    att_job.scatter_second()
    parent_job.gather_z()
    mlp_job.gather_z()
    att_job.scatter_z()
    parent_job.gather_second()
    mlp_job.gather_second()
    att_job.gather_z()
    parent_job.gather_first()
    mlp_job.gather_first()
    att_job.gather_second()
    parent_job.gather_core()
    mlp_job.gather_core()
    att_job.gather_first()
    att_job.gather_core()
    for job in (parent_job, mlp_job, att_job):
        job.finish()


def gain_row(weights, sums, gain):
    total = jnp.zeros((W, W), F32)
    for weight, value in zip(weights, sums, strict=True):
        total = total + weight.astype(F32) * value
    high = total.astype(BF16)
    low = (total - high.astype(F32)).astype(BF16)
    ones = jnp.ones((8, W), BF16)
    return (dot_nt(ones, high) + dot_nt(ones, low))[:1] / gain.astype(F32)


def unpack_kernel(
    states_in, parent_sum, mlp_sum, att_sum, cgain, cq, ck, cv, hgain, up, pgain, pq, pk, pv,
    states, dcg, dcq, dck, dcv, dco, dhg, dup, ddown, dlink, dpg, dpq, dpk, dpv, dpo,
):
    def block(total, b):
        return jnp.concatenate(
            [total[half, :, :, b].astype(F32).reshape(W, 128) for half in range(2)], axis=1
        )

    states[...] = states_in[...]
    grads = []
    for b, ref in enumerate((dcq, dck, dcv, dco)):
        grads.append(block(att_sum, b))
        ref[...] = grads[-1]
    dcg[...] = gain_row([cq[...], ck[...], cv[...]], grads[:3], cgain[...])
    grads = []
    for b in range(4):
        ddown[b * W : (b + 1) * W] = block(mlp_sum, b)
        grads.append(block(mlp_sum, 4 + b))
        dup[:, b * W : (b + 1) * W] = grads[-1]
    dhg[...] = gain_row([up[:, b * W : (b + 1) * W] for b in range(4)], grads, hgain[...])
    grads = []
    for b, ref in enumerate((dlink, dpq, dpk, dpv, dpo)):
        grads.append(block(parent_sum, b))
        ref[...] = grads[-1]
    dpg[...] = gain_row([pq[...], pk[...], pv[...]], grads[1:4], pgain[...])


def body(
    item_tokens, owner_index, owner_row, parent_tokens, cotangent,
    column_gain, column_query, column_key, column_value, column_out,
    hidden_gain, up_weight, down_weight, link_weight,
    parent_gain, parent_query, parent_key, parent_value, parent_out,
):
    vmem = pl.BlockSpec(memory_space=pltpu.VMEM)
    shape = jax.ShapeDtypeStruct
    cgain, hgain, pgain = (
        g.reshape(1, W) for g in (column_gain, hidden_gain, parent_gain)
    )
    items = lambda width, dtype=BF16: pltpu.VMEM((ROWS, width), dtype)
    parents = lambda width, dtype=BF16: pltpu.VMEM((PROWS, width), dtype)
    scratch = [
        items(W), items(W), items(W), items(W),
        pltpu.VMEM((GROUPS, HEADS * GROWS, GROWS), BF16),
        items(W), items(W), items(W), items(FF, F32), items(FF), items(FF),
        items(W), items(W), items(W), items(3 * W),
        pltpu.VMEM((TX, FF), BF16),
        parents(W), parents(W), parents(W), parents(W), parents(W),
        pltpu.VMEM((PGROUPS, HEADS * GPROWS, GPROWS), BF16),
        parents(W), parents(W), parents(W), parents(3 * W), parents(W, F32),
        pltpu.VMEM((2, 4, 4, 5, 16, 128), BF16),
        pltpu.VMEM((2, 4, 4, 8, 16, 128), BF16),
        pltpu.VMEM((2, 4, 4, 4, 16, 128), BF16),
        pltpu.VMEM((N_DP, 8, 128), F32),
        pltpu.VMEM((N_DP, 8, 128), F32),
        pltpu.VMEM((N_DP, 8, 128), F32),
        pltpu.VMEM((N_DP, 8, 128), F32),
        pltpu.SemaphoreType.DMA((2,)),
        pltpu.SemaphoreType.DMA((2,)),
    ]
    for n in (5, 8, 4):
        scratch += Summing.scratch(n)
    states, parent_sum, mlp_sum, att_sum = pl.pallas_call(
        encoder_kernel,
        out_shape=[shape((PROWS, W), BF16)]
        + [shape((2, 4, 4, n, 16, 128), BF16) for n in (5, 8, 4)],
        in_specs=[vmem] * 19,
        out_specs=[vmem] * 4,
        scratch_shapes=scratch,
        compiler_params=pltpu.CompilerParams(
            collective_id=1, has_side_effects=True, vmem_limit_bytes=VMEM_LIMIT
        ),
        name="encoder",
    )(
        item_tokens, owner_index.reshape(1, TX), owner_row.reshape(1, TX),
        parent_tokens.reshape(PROWS, W), cotangent.reshape(PROWS, W),
        cgain, column_query, column_key, column_value, column_out,
        hgain, up_weight, down_weight, link_weight,
        pgain, parent_query, parent_key, parent_value, parent_out,
    )
    square = shape((W, W), F32)
    row = shape((1, W), F32)
    out = pl.pallas_call(
        unpack_kernel,
        out_shape=[
            shape((PROWS, W), BF16), row, square, square, square, square, row,
            shape((W, FF), F32), shape((FF, W), F32), square, row, square, square, square, square,
        ],
        in_specs=[vmem] * 14,
        out_specs=[vmem] * 15,
        compiler_params=pltpu.CompilerParams(vmem_limit_bytes=VMEM_LIMIT),
        name="unpack",
    )(
        states, parent_sum, mlp_sum, att_sum, cgain, column_query, column_key, column_value,
        hgain, up_weight, pgain, parent_query, parent_key, parent_value,
    )
    out = [o.reshape(W) if o.shape == (1, W) else o for o in out]
    return (out[0].reshape(CUST, CTOK, W), *out[1:])


def solution(mesh):
    split, whole = P(("dp", "rep")), P()
    return jax.shard_map(
        body,
        mesh=mesh,
        in_specs=(split,) * 5 + (whole,) * 14,
        out_specs=(split,) + (whole,) * 14,
        check_vma=False,
    )
```

```python
import math

import jax
import jax.numpy as jnp
from jax import lax
from jax.experimental import pallas as pl
from jax.experimental.pallas import tpu as pltpu
from jax.sharding import PartitionSpec as P

MESH = pl.DeviceIdType.MESH
F32 = jnp.float32
BF16 = jnp.bfloat16
N_DP = 64


def place():
    dp, rep = lax.axis_index("dp"), lax.axis_index("rep")
    z, x, core = lax.div(dp, 8), lax.rem(lax.div(dp, 2), 4), lax.rem(dp, 2)
    return dp, rep, z, core, rep * 4 + x


def core_peer(at):
    dp, rep, z, core, spot = at
    return (dp + 1 - 2 * core, rep)


def plane_peer(at, j):
    dp, rep, z, core, spot = at
    return (8 * z + 2 * lax.rem(j, 4) + core, lax.div(j, 4))


def z_peer(at, j):
    dp, rep, z, core, spot = at
    return (8 * j + lax.rem(dp, 8), rep)


def remote(src, dst, send, recv, peer):
    copy = pltpu.make_async_remote_copy(
        src_ref=src, dst_ref=dst, send_sem=send, recv_sem=recv, device_id=peer, device_id_type=MESH
    )
    copy.start()
    return copy


def wait_sent(at, like, sem):
    pltpu.make_async_remote_copy(
        src_ref=like, dst_ref=like, send_sem=sem, recv_sem=sem,
        device_id=core_peer(at), device_id_type=MESH,
    ).wait_send()


def wait_received(at, like, sem):
    pltpu.make_async_remote_copy(
        src_ref=like, dst_ref=like, send_sem=sem, recv_sem=sem,
        device_id=core_peer(at), device_id_type=MESH,
    ).wait_recv()


class Summing:
    def __init__(self, at, n, mine, total, scratch):
        self.at, self.n, self.mine, self.total = at, n, mine, total
        self.core_in, self.plane_out, self.plane_in, self.z_all, self.send, self.recv = scratch

    @staticmethod
    def scratch(n):
        return [
            pltpu.VMEM((16, n, 16, 128), BF16),
            pltpu.VMEM((16, n, 16, 128), BF16),
            pltpu.VMEM((15, n, 16, 128), BF16),
            pltpu.VMEM((8, n, 16, 128), BF16),
            pltpu.SemaphoreType.DMA((5,)),
            pltpu.SemaphoreType.DMA((20,)),
        ]

    def start(self):
        dp, rep, z, core, spot = self.at
        self.from_core = remote(
            self.mine.at[1 - core], self.core_in, self.send.at[0], self.recv.at[0], core_peer(self.at)
        )

    def scatter_plane(self):
        dp, rep, z, core, spot = self.at
        self.from_core.wait_recv()
        self.plane_out[...] = (
            self.mine[core].astype(F32) + self.core_in[...].astype(F32)
        ).astype(BF16)
        for d in range(1, 16):
            q = lax.rem(spot + d, 16)
            remote(
                self.plane_out.at[q], self.plane_in.at[d - 1], self.send.at[1], self.recv.at[1],
                plane_peer(self.at, q),
            )

    def scatter_z(self):
        dp, rep, z, core, spot = self.at
        wait_received(self.at, self.plane_in, self.recv.at[1])
        value = self.plane_out[spot].astype(F32)
        for i in range(15):
            value = value + self.plane_in[i].astype(F32)
        self.z_all[z] = value.astype(BF16)
        for d in range(1, 8):
            here = self.z_all.at[z]
            remote(here, here, self.send.at[2], self.recv.at[2], z_peer(self.at, lax.rem(z + d, 8)))

    def gather_plane(self):
        dp, rep, z, core, spot = self.at
        wait_received(self.at, self.z_all.at[pl.ds(0, 7)], self.recv.at[2])
        value = self.z_all[0].astype(F32)
        for i in range(1, 8):
            value = value + self.z_all[i].astype(F32)
        self.total[core, spot] = value.astype(BF16)
        here = self.total.at[core, spot]
        self.from_plane = [
            remote(
                here, here, self.send.at[3], self.recv.at[3 + d],
                plane_peer(self.at, lax.rem(spot + d, 16)),
            )
            for d in range(1, 16)
        ]
        remote(here, here, self.send.at[4], self.recv.at[3], core_peer(self.at))

    def gather_core(self):
        dp, rep, z, core, spot = self.at
        for d, copy in zip(range(1, 16), self.from_plane, strict=True):
            copy.wait_recv()
            here = self.total.at[core, lax.rem(spot + 16 - d, 16)]
            remote(here, here, self.send.at[4], self.recv.at[3], core_peer(self.at))

    def finish(self):
        dp, rep, z, core, spot = self.at
        wait_received(self.at, self.total.at[1 - core], self.recv.at[3])
        self.from_core.wait_send()
        wait_sent(self.at, self.plane_in, self.send.at[1])
        wait_sent(self.at, self.z_all.at[pl.ds(0, 7)], self.send.at[2])
        wait_sent(self.at, self.total.at[core, pl.ds(0, 15)], self.send.at[3])
        wait_sent(self.at, self.total.at[core], self.send.at[4])


def exchange_start(at, out_ref, in_ref, send, recv):
    dp, rep = at[:2]
    in_ref[dp] = out_ref[dp]

    def to(d):
        j = lax.rem(dp + d, N_DP)
        remote(out_ref.at[j], in_ref.at[dp], send, recv, (j, rep))

    def step(d, carry):
        to(N_DP // 2 - d)
        to(N_DP // 2 + d)
        return carry

    to(N_DP // 2)
    lax.fori_loop(1, N_DP // 2, step, 0)


def exchange_wait(at, in_ref, send, recv):
    rest = in_ref.at[pl.ds(0, N_DP - 1)]
    wait_received(at, rest, recv)
    wait_sent(at, rest, send)


def greet_all(at, barrier):
    dp, rep, z, core, spot = at

    def group(d, carry):
        peer = (lax.rem(dp + d, N_DP), rep)
        pl.semaphore_signal(barrier, inc=1, device_id=peer, device_id_type=MESH)
        return carry

    lax.fori_loop(1, N_DP, group, 0)
    for d in range(1, 4):
        for x in range(4):
            peer = (8 * z + 2 * x + core, lax.rem(rep + d, 4))
            pl.semaphore_signal(barrier, inc=1, device_id=peer, device_id_type=MESH)
    return N_DP - 1 + 12


VMEM_LIMIT = 56 * 1024 * 1024
EPSILON = 1e-06
HEADS = 8
W = 256
HEAD = 32
FF = 1024
TX, COLS = 24, 24
CUST, CTOK = 16, 32
ROWS = TX * COLS
PROWS = CUST * CTOK
GROUP = 4
GROWS = GROUP * COLS
GPROWS = GROUP * CTOK
GROUPS = TX // GROUP
PGROUPS = CUST // GROUP


def dot(a, b):
    return lax.dot_general(a, b, (((1,), (0,)), ((), ())), preferred_element_type=F32)


def dot_nt(a, b):
    return lax.dot_general(a, b, (((1,), (1,)), ((), ())), preferred_element_type=F32)


def dot_tn(a, b):
    return lax.dot_general(a, b, (((0,), (0,)), ((), ())), preferred_element_type=F32)


def each(count, step, body, unroll=1):
    def one(i, carry):
        body(pl.ds(pl.multiple_of(i * step, step), step), i)
        return carry

    lax.fori_loop(0, count, one, 0, unroll=unroll)


def head_masks():
    lane = lax.broadcasted_iota(jnp.int32, (1, W), 1)
    return [jnp.where(lax.div(lane, HEAD) == h, 1.0, 0.0) for h in range(HEADS)]


def spread_heads(value, masks):
    return jnp.concatenate([value * mask.astype(BF16) for mask in masks], axis=0)


def join_heads(value, masks, rows):
    total = value[:rows] * masks[0]
    for h in range(1, HEADS):
        total = total + value[h * rows : (h + 1) * rows] * masks[h]
    return total


def same_owner(rows, length):
    i = lax.div(lax.broadcasted_iota(jnp.int32, (rows, rows), 0), length)
    j = lax.div(lax.broadcasted_iota(jnp.int32, (rows, rows), 1), length)
    return jnp.concatenate([jnp.where(i == j, 0.0, -1e30)] * HEADS, axis=0)


def attend(q, k, v, probs, mix, groups, rows, length):
    masks = head_masks()
    bias = same_owner(rows, length)

    def body(at, i):
        wide = spread_heads(q[at], masks)
        scores = dot_nt(wide, k[at]) * HEAD**-0.5 + bias
        e = jnp.exp(scores - jnp.max(scores, axis=1, keepdims=True))
        p = (e * (1.0 / jnp.sum(e, axis=1, keepdims=True))).astype(BF16)
        probs[i] = p
        mix[at] = join_heads(dot(p, v[at]), masks, rows).astype(BF16)

    each(groups, rows, body)


def attend_back(q, k, v, probs, dmix, dqkv, groups, rows):
    masks = head_masks()

    def body(at, i):
        p = probs[i]
        wide_d = spread_heads(dmix[at], masks)
        wide_q = spread_heads(q[at], masks)
        dp = dot_nt(wide_d, v[at]).astype(BF16).astype(F32)
        weighted = p.astype(F32)
        ds = weighted * (dp - jnp.sum(weighted * dp, axis=1, keepdims=True))
        ds = (ds * HEAD**-0.5).astype(BF16)
        dqkv[at, 0:W] = join_heads(dot(ds, k[at]), masks, rows).astype(BF16)
        dqkv[at, W : 2 * W] = dot_tn(ds, wide_q).astype(BF16)
        dqkv[at, 2 * W : 3 * W] = dot_tn(p, wide_d).astype(BF16)

    each(groups, rows, body)


def put_block(mine, b, value):
    for half in range(2):
        part = value[:, half * 128 : (half + 1) * 128].astype(BF16)
        mine[half, :, b] = part.reshape(16, 16, 128)


def rms_scale(value):
    return lax.rsqrt(jnp.mean(value * value, axis=1, keepdims=True) + EPSILON)


def averaging():
    t = lax.broadcasted_iota(jnp.int32, (TX, ROWS), 0)
    r = lax.div(lax.broadcasted_iota(jnp.int32, (TX, ROWS), 1), COLS)
    return jnp.where(t == r, 1.0, 0.0).astype(BF16)


def placing(owner_ref):
    owner = owner_ref[...]
    i = lax.broadcasted_iota(jnp.int32, (TX, TX), 0)
    j = lax.broadcasted_iota(jnp.int32, (TX, TX), 1)
    along = jnp.broadcast_to(owner, (TX, TX))
    down = jnp.sum(jnp.where(i == j, along, 0), axis=1, keepdims=True)
    slot = jnp.sum(jnp.where((down == along) & (i < j), 1, 0), axis=0, keepdims=True)
    device = lax.broadcasted_iota(jnp.int32, (N_DP, TX), 0)
    goes = device == jnp.broadcast_to(owner, (N_DP, TX))
    return [
        jnp.where(goes & (jnp.broadcast_to(slot, (N_DP, TX)) == s), 1.0, 0.0).astype(BF16)
        for s in range(2)
    ]


def encoder_kernel(
    item_ref, owner_ref, row_ref, parent_ref, cot_ref,
    cgain, cq, ck, cv, co, hgain, up, down, link, pgain, pq, pk, pv, po,
    states_ref, parent_sum, down_sum, up_sum, att_sum,
    n1, q, k, v, probs, mix, s_, n2, u, h, slope, dn2, da, dmix, dqkv, hmean,
    pbased, pn, pq_, pk_, pv_, pprobs, pmix, pda, pdmix, pdqkv, pdn,
    parent_mine, down_mine, up_mine, att_mine,
    out1, in1, out2, in2, x_send, x_recv,
    *job_scratch,
):
    at = place()
    barrier = pltpu.get_barrier_semaphore()
    greeted = greet_all(at, barrier)
    jobs = zip(
        (5, 4, 4, 4),
        (parent_mine, down_mine, up_mine, att_mine),
        (parent_sum, down_sum, up_sum, att_sum),
        strict=True,
    )
    per = len(job_scratch) // 4
    parent_job, down_job, up_job, att_job = [
        Summing(at, *job, job_scratch[i * per : (i + 1) * per]) for i, job in enumerate(jobs)
    ]

    def norm_items(rows, i):
        x = item_ref[pl.ds(i * GROUP, GROUP)].astype(F32).reshape(GROWS, W)
        n1[rows] = (x * rms_scale(x) * cgain[...].astype(F32)[None, :]).astype(BF16)

    each(GROUPS, GROWS, norm_items, unroll=2)
    q[...] = dot(n1[...], cq[...]).astype(BF16)
    k[...] = dot(n1[...], ck[...]).astype(BF16)
    v[...] = dot(n1[...], cv[...]).astype(BF16)
    attend(q, k, v, probs, mix, GROUPS, GROWS, COLS)
    u[:, :W] = dot(mix[...], co[...])

    def norm_stream(rows, i):
        x = item_ref[pl.ds(i * GROUP, GROUP)].astype(F32).reshape(GROWS, W)
        stream = (x + u[rows, :W]).astype(BF16)
        s_[rows] = stream
        stream = stream.astype(F32)
        n2[rows] = (stream * rms_scale(stream) * hgain[...].astype(F32)[None, :]).astype(BF16)

    each(GROUPS, GROWS, norm_stream, unroll=2)
    u[...] = dot(n2[...], up[...])

    def gelu(rows, i):
        for c in range(0, FF, 256):
            value = u[rows, c : c + 256]
            square = value * value
            t = jnp.tanh(math.sqrt(2.0 / math.pi) * value * (1.0 + 0.044715 * square))
            half = 0.5 * (1.0 + t)
            h[rows, c : c + 256] = (value * half).astype(BF16)
            inner = math.sqrt(2.0 / math.pi) * (1.0 + 3 * 0.044715 * square)
            slope[rows, c : c + 256] = (half + 0.5 * value * (1.0 - t * t) * inner).astype(BF16)

    each(ROWS // 32, 32, gelu)
    average = averaging()
    hidden = (dot(average, h[...]) * (1.0 / COLS)).astype(BF16)
    hmean[...] = hidden
    embedding = (dot(average, s_[...]) * (1.0 / COLS) + dot(hidden, down[...])).astype(BF16)

    places = placing(owner_ref)
    ids = jnp.broadcast_to(row_ref[...].astype(F32) + 1.0, (128, TX)).astype(BF16)
    for slot in range(2):
        moved = dot(places[slot], embedding)
        out1[:, 2 * slot, :] = moved[:, :128]
        out1[:, 2 * slot + 1, :] = moved[:, 128:]
        out1[:, 4 + slot, :] = dot_nt(places[slot], ids)
        out1[:, 6 + slot, :] = jnp.zeros((N_DP, 128), F32)
    pl.semaphore_wait(barrier, greeted)
    exchange_start(at, out1, in1, x_send.at[0], x_recv.at[0])
    exchange_wait(at, in1, x_send.at[0], x_recv.at[0])

    members = []
    customer = lax.broadcasted_iota(jnp.int32, (N_DP, CUST), 1).astype(F32) + 1.0
    counts, sums = jnp.zeros((CUST, W), F32), jnp.zeros((CUST, W), F32)
    for slot in range(2):
        got = jnp.concatenate([in1[:, 2 * slot, :], in1[:, 2 * slot + 1, :]], axis=1).astype(BF16)
        member = jnp.where(in1[:, 4 + slot, :][:, :CUST] == customer, 1.0, 0.0).astype(BF16)
        members.append(member)
        counts = counts + dot_tn(member, jnp.ones((N_DP, W), BF16))
        sums = sums + dot_tn(member, got)
    divisor = jnp.maximum(counts, 1.0)
    pooled = (sums / divisor).astype(BF16)
    linked = dot(pooled, link[...])
    scale = 1.0 / math.sqrt(CUST * CTOK * 256)
    pbased_value = (
        (parent_ref[...].astype(F32).reshape(CUST, CTOK, W) + linked[:, None, :])
        .astype(BF16)
        .reshape(PROWS, W)
    )
    pbased[...] = pbased_value

    def norm_based(rows, i):
        x = pbased[rows].astype(F32)
        pn[rows] = (x * rms_scale(x) * pgain[...].astype(F32)[None, :]).astype(BF16)
        pda[rows] = (cot_ref[rows].astype(F32) * scale).astype(BF16)

    each(PGROUPS, GPROWS, norm_based, unroll=2)
    pq_[...] = dot(pn[...], pq[...]).astype(BF16)
    pk_[...] = dot(pn[...], pk[...]).astype(BF16)
    pv_[...] = dot(pn[...], pv[...]).astype(BF16)
    pdmix[...] = dot_nt(pda[...], po[...]).astype(BF16)
    attend(pq_, pk_, pv_, pprobs, pmix, PGROUPS, GPROWS, CTOK)
    attend_back(pq_, pk_, pv_, pprobs, pdmix, pdqkv, PGROUPS, GPROWS)
    pdn[...] = (
        dot_nt(pdqkv[:, :W], pq[...])
        + dot_nt(pdqkv[:, W : 2 * W], pk[...])
        + dot_nt(pdqkv[:, 2 * W :], pv[...])
    )

    dlinked = []
    for i in range(PGROUPS):
        rows = slice(i * GPROWS, (i + 1) * GPROWS)
        x = pbased[rows].astype(F32)
        r = rms_scale(x)
        unit = x * r
        dunit = pdn[rows] * pgain[...].astype(F32)[None, :]
        dx = r * (dunit - unit * jnp.mean(dunit * unit, axis=1, keepdims=True))
        dx = dx + cot_ref[rows].astype(F32) * scale
        dlinked.append(jnp.sum(dx.reshape(GROUP, CTOK, W), axis=1))
    dlinked = jnp.concatenate(dlinked, axis=0)
    dpooled = dot_nt(dlinked.astype(BF16), link[...]).astype(BF16).astype(F32)
    sum_grad = (dpooled / divisor).astype(BF16)
    for slot in range(2):
        moved = dot(members[slot], sum_grad)
        out2[:, 2 * slot, :] = moved[:, :128]
        out2[:, 2 * slot + 1, :] = moved[:, 128:]
        out2[:, 4 + slot, :] = jnp.zeros((N_DP, 128), F32)
        out2[:, 6 + slot, :] = jnp.zeros((N_DP, 128), F32)
    exchange_start(at, out2, in2, x_send.at[1], x_recv.at[1])

    put_block(parent_mine, 0, dot_tn(pooled, dlinked.astype(BF16)))
    dweights = dot_tn(pn[...], pdqkv[...])
    for b in range(3):
        put_block(parent_mine, 1 + b, dweights[:, b * W : (b + 1) * W])
    put_block(parent_mine, 4, dot_tn(pmix[...], pda[...]))
    parent_job.start()
    states_ref[...] = (pbased[...].astype(F32) + dot(pmix[...], po[...])).astype(BF16)
    parent_job.scatter_plane()
    exchange_wait(at, in2, x_send.at[1], x_recv.at[1])

    ditem = jnp.zeros((TX, W), F32)
    for slot in range(2):
        got = jnp.concatenate([in2[:, 2 * slot, :], in2[:, 2 * slot + 1, :]], axis=1).astype(BF16)
        ditem = ditem + dot_tn(places[slot], got)
    ditem_b = ditem.astype(BF16)
    ddown = dot_tn(hmean[...], ditem_b)
    for b in range(4):
        put_block(down_mine, b, ddown[b * W : (b + 1) * W])
    down_job.start()
    dhidden = (dot_nt(ditem_b, down[...]) * (1.0 / COLS)).astype(BF16)
    spread = averaging()
    u[...] = dot_tn(spread, dhidden)
    dy = dot_tn(spread, ditem_b)

    def back_hidden(rows, i):
        for c in range(0, FF, 256):
            h[rows, c : c + 256] = (
                u[rows, c : c + 256] * slope[rows, c : c + 256].astype(F32)
            ).astype(BF16)

    each(ROWS // 32, 32, back_hidden)
    down_job.scatter_plane()
    dup = dot_tn(n2[...], h[...])
    for b in range(4):
        put_block(up_mine, b, dup[:, b * W : (b + 1) * W])
    up_job.start()
    parent_job.scatter_z()
    u[:, :W] = dot_nt(h[...], up[...])
    u[:, W : 2 * W] = dy

    def back_stream(rows, i):
        x = s_[rows].astype(F32)
        r = rms_scale(x)
        unit = x * r
        dunit = u[rows, :W].astype(BF16).astype(F32) * hgain[...].astype(F32)[None, :]
        dx = r * (dunit - unit * jnp.mean(dunit * unit, axis=1, keepdims=True))
        da[rows] = (dx + u[rows, W : 2 * W] * (1.0 / COLS)).astype(BF16)

    each(GROUPS, GROWS, back_stream, unroll=2)
    up_job.scatter_plane()
    dmix[...] = dot_nt(da[...], co[...]).astype(BF16)
    put_block(att_mine, 3, dot_tn(mix[...], da[...]))
    attend_back(q, k, v, probs, dmix, dqkv, GROUPS, GROWS)
    dweights = dot_tn(n1[...], dqkv[...])
    for b in range(3):
        put_block(att_mine, b, dweights[:, b * W : (b + 1) * W])
    att_job.start()

    parent_job.gather_plane()
    down_job.scatter_z()
    att_job.scatter_plane()
    up_job.scatter_z()
    parent_job.gather_core()
    down_job.gather_plane()
    att_job.scatter_z()
    up_job.gather_plane()
    down_job.gather_core()
    att_job.gather_plane()
    up_job.gather_core()
    att_job.gather_core()
    for job in (parent_job, down_job, up_job, att_job):
        job.finish()


def gain_row(weights, sums, gain):
    total = jnp.zeros((W, W), F32)
    for weight, value in zip(weights, sums, strict=True):
        total = total + weight.astype(F32) * value
    high = total.astype(BF16)
    low = (total - high.astype(F32)).astype(BF16)
    ones = jnp.ones((8, W), BF16)
    return (dot_nt(ones, high) + dot_nt(ones, low))[:1] / gain.astype(F32)[None, :]


def unpack_kernel(
    states_in, parent_sum, down_sum, up_sum, att_sum, cgain, cq, ck, cv, hgain, up, pgain, pq, pk, pv,
    states, dcg, dcq, dck, dcv, dco, dhg, dup, ddown, dlink, dpg, dpq, dpk, dpv, dpo,
):
    def block(total, b):
        return jnp.concatenate(
            [total[half, :, b].astype(F32).reshape(W, 128) for half in range(2)], axis=1
        )

    states[...] = states_in[...]
    grads = []
    for b, ref in enumerate((dcq, dck, dcv, dco)):
        grads.append(block(att_sum, b))
        ref[...] = grads[-1]
    dcg[...] = gain_row([cq[...], ck[...], cv[...]], grads[:3], cgain[...])
    grads = []
    for b in range(4):
        ddown[b * W : (b + 1) * W] = block(down_sum, b)
        grads.append(block(up_sum, b))
        dup[:, b * W : (b + 1) * W] = grads[-1]
    dhg[...] = gain_row([up[:, b * W : (b + 1) * W] for b in range(4)], grads, hgain[...])
    grads = []
    for b, ref in enumerate((dlink, dpq, dpk, dpv, dpo)):
        grads.append(block(parent_sum, b))
        ref[...] = grads[-1]
    dpg[...] = gain_row([pq[...], pk[...], pv[...]], grads[1:4], pgain[...])


def body(
    item_tokens, owner_index, owner_row, parent_tokens, cotangent,
    column_gain, column_query, column_key, column_value, column_out,
    hidden_gain, up_weight, down_weight, link_weight,
    parent_gain, parent_query, parent_key, parent_value, parent_out,
):
    vmem = pl.BlockSpec(memory_space=pltpu.VMEM)
    shape = jax.ShapeDtypeStruct
    cgain, hgain, pgain = column_gain, hidden_gain, parent_gain
    items = lambda width, dtype=BF16: pltpu.VMEM((ROWS, width), dtype)
    parents = lambda width, dtype=BF16: pltpu.VMEM((PROWS, width), dtype)
    scratch = [
        items(W), items(W), items(W), items(W),
        pltpu.VMEM((GROUPS, HEADS * GROWS, GROWS), BF16),
        items(W), items(W), items(W), items(FF, F32), items(FF), items(FF),
        items(W), items(W), items(W), items(3 * W),
        pltpu.VMEM((TX, FF), BF16),
        parents(W), parents(W), parents(W), parents(W), parents(W),
        pltpu.VMEM((PGROUPS, HEADS * GPROWS, GPROWS), BF16),
        parents(W), parents(W), parents(W), parents(3 * W), parents(W, F32),
        *[pltpu.VMEM((2, 16, n, 16, 128), BF16) for n in (5, 4, 4, 4)],
        pltpu.VMEM((N_DP, 8, 128), F32),
        pltpu.VMEM((N_DP, 8, 128), F32),
        pltpu.VMEM((N_DP, 8, 128), F32),
        pltpu.VMEM((N_DP, 8, 128), F32),
        pltpu.SemaphoreType.DMA((2,)),
        pltpu.SemaphoreType.DMA((2,)),
    ]
    for n in (5, 4, 4, 4):
        scratch += Summing.scratch(n)
    states, parent_sum, down_sum, up_sum, att_sum = pl.pallas_call(
        encoder_kernel,
        out_shape=[shape((PROWS, W), BF16)]
        + [shape((2, 16, n, 16, 128), BF16) for n in (5, 4, 4, 4)],
        in_specs=[vmem] * 19,
        out_specs=[vmem] * 5,
        scratch_shapes=scratch,
        compiler_params=pltpu.CompilerParams(
            collective_id=1, has_side_effects=True, vmem_limit_bytes=VMEM_LIMIT
        ),
        name="encoder",
    )(
        item_tokens, owner_index.reshape(1, TX), owner_row.reshape(1, TX),
        parent_tokens.reshape(PROWS, W), cotangent.reshape(PROWS, W),
        cgain, column_query, column_key, column_value, column_out,
        hgain, up_weight, down_weight, link_weight,
        pgain, parent_query, parent_key, parent_value, parent_out,
    )
    square = shape((W, W), F32)
    row = shape((1, W), F32)
    out = pl.pallas_call(
        unpack_kernel,
        out_shape=[
            shape((PROWS, W), BF16), row, square, square, square, square, row,
            shape((W, FF), F32), shape((FF, W), F32), square, row, square, square, square, square,
        ],
        in_specs=[vmem] * 15,
        out_specs=[vmem] * 15,
        compiler_params=pltpu.CompilerParams(vmem_limit_bytes=VMEM_LIMIT),
        name="unpack",
    )(
        states, parent_sum, down_sum, up_sum, att_sum, cgain, column_query, column_key, column_value,
        hgain, up_weight, pgain, parent_query, parent_key, parent_value,
    )
    out = [o.reshape(W) if o.shape == (1, W) else o for o in out]
    return (out[0].reshape(CUST, CTOK, W), *out[1:])


def solution(mesh):
    split, whole = P(("dp", "rep")), P()
    return jax.shard_map(
        body,
        mesh=mesh,
        in_specs=(split,) * 5 + (whole,) * 14,
        out_specs=(split,) + (whole,) * 14,
        check_vma=False,
    )
```

```python
import math

import jax
import jax.numpy as jnp
from jax import lax
from jax.experimental import pallas as pl
from jax.experimental.pallas import tpu as pltpu
from jax.sharding import PartitionSpec as P

MESH = pl.DeviceIdType.MESH
F32 = jnp.float32
BF16 = jnp.bfloat16
CHIPS = 32


def place():
    dp, rep = lax.axis_index("dp"), lax.axis_index("rep")
    z, x, core = lax.div(dp, 8), lax.rem(lax.div(dp, 2), 4), lax.rem(dp, 2)
    return dp, rep, z, core, rep * 4 + x


def core_peer(at):
    dp, rep, z, core, spot = at
    return (dp + 1 - 2 * core, rep)


def plane_peer(at, j):
    dp, rep, z, core, spot = at
    return (8 * z + 2 * lax.rem(j, 4) + core, lax.div(j, 4))


def z_peer(at, j):
    dp, rep, z, core, spot = at
    return (8 * j + lax.rem(dp, 8), rep)


def remote(src, dst, send, recv, peer):
    copy = pltpu.make_async_remote_copy(
        src_ref=src, dst_ref=dst, send_sem=send, recv_sem=recv, device_id=peer, device_id_type=MESH
    )
    copy.start()
    return copy


def wait_sent(at, like, sem):
    pltpu.make_async_remote_copy(
        src_ref=like, dst_ref=like, send_sem=sem, recv_sem=sem,
        device_id=core_peer(at), device_id_type=MESH,
    ).wait_send()


def wait_received(at, like, sem):
    pltpu.make_async_remote_copy(
        src_ref=like, dst_ref=like, send_sem=sem, recv_sem=sem,
        device_id=core_peer(at), device_id_type=MESH,
    ).wait_recv()


class Summing:
    def __init__(self, at, n, mine, total, scratch):
        self.at, self.n, self.mine, self.total = at, n, mine, total
        self.core_in, self.plane_out, self.plane_in, self.z_all, self.send, self.recv = scratch

    @staticmethod
    def scratch(n):
        return [
            pltpu.VMEM((16, n, 16, 128), BF16),
            pltpu.VMEM((16, n, 16, 128), BF16),
            pltpu.VMEM((15, n, 16, 128), BF16),
            pltpu.VMEM((8, n, 16, 128), BF16),
            pltpu.SemaphoreType.DMA((5,)),
            pltpu.SemaphoreType.DMA((20,)),
        ]

    def start(self):
        dp, rep, z, core, spot = self.at
        self.from_core = remote(
            self.mine.at[1 - core], self.core_in, self.send.at[0], self.recv.at[0], core_peer(self.at)
        )

    def scatter_plane(self):
        dp, rep, z, core, spot = self.at
        self.from_core.wait_recv()
        self.plane_out[...] = (
            self.mine[core].astype(F32) + self.core_in[...].astype(F32)
        ).astype(BF16)
        for d in range(1, 16):
            q = lax.rem(spot + d, 16)
            remote(
                self.plane_out.at[q], self.plane_in.at[d - 1], self.send.at[1], self.recv.at[1],
                plane_peer(self.at, q),
            )

    def scatter_z(self):
        dp, rep, z, core, spot = self.at
        wait_received(self.at, self.plane_in, self.recv.at[1])
        value = self.plane_out[spot].astype(F32)
        for i in range(15):
            value = value + self.plane_in[i].astype(F32)
        self.z_all[z] = value.astype(BF16)
        for d in range(1, 8):
            here = self.z_all.at[z]
            remote(here, here, self.send.at[2], self.recv.at[2], z_peer(self.at, lax.rem(z + d, 8)))

    def gather_plane(self):
        dp, rep, z, core, spot = self.at
        wait_received(self.at, self.z_all.at[pl.ds(0, 7)], self.recv.at[2])
        value = self.z_all[0].astype(F32)
        for i in range(1, 8):
            value = value + self.z_all[i].astype(F32)
        self.total[core, spot] = value.astype(BF16)
        here = self.total.at[core, spot]
        self.from_plane = [
            remote(
                here, here, self.send.at[3], self.recv.at[3 + d],
                plane_peer(self.at, lax.rem(spot + d, 16)),
            )
            for d in range(1, 16)
        ]
        remote(here, here, self.send.at[4], self.recv.at[3], core_peer(self.at))

    def gather_core(self):
        dp, rep, z, core, spot = self.at
        for d, copy in zip(range(1, 16), self.from_plane, strict=True):
            copy.wait_recv()
            here = self.total.at[core, lax.rem(spot + 16 - d, 16)]
            remote(here, here, self.send.at[4], self.recv.at[3], core_peer(self.at))

    def finish(self):
        dp, rep, z, core, spot = self.at
        wait_received(self.at, self.total.at[1 - core], self.recv.at[3])
        self.from_core.wait_send()
        wait_sent(self.at, self.plane_in, self.send.at[1])
        wait_sent(self.at, self.z_all.at[pl.ds(0, 7)], self.send.at[2])
        wait_sent(self.at, self.total.at[core, pl.ds(0, 15)], self.send.at[3])
        wait_sent(self.at, self.total.at[core], self.send.at[4])


class Exchange:
    def __init__(self, at, scratch):
        self.at = at
        self.wide, self.out, self.near, self.far, self.send, self.recv = scratch

    @staticmethod
    def scratch():
        return [
            pltpu.VMEM((CHIPS, 16, 128), F32),
            pltpu.VMEM((CHIPS, 16, 128), BF16),
            pltpu.VMEM((CHIPS, 16, 128), BF16),
            pltpu.VMEM((CHIPS, 16, 128), BF16),
            pltpu.SemaphoreType.DMA((2,)),
            pltpu.SemaphoreType.DMA((2,)),
        ]

    def put(self, p, value, extra=None):
        self.wide[:, 2 * p, :] = value[:, :128]
        self.wide[:, 2 * p + 1, :] = value[:, 128:]
        self.wide[:, 8 + p, :] = jnp.zeros((CHIPS, 128), F32) if extra is None else extra
        self.wide[:, 12 + p, :] = jnp.zeros((CHIPS, 128), F32)

    def start(self):
        dp, rep, z, core, spot = self.at
        chip = lax.div(dp, 2)
        self.out[...] = self.wide[...].astype(BF16)
        self.near[chip] = self.out[chip]

        def to(d):
            j = lax.rem(chip + d, CHIPS)
            remote(
                self.out.at[j], self.near.at[chip], self.send.at[0], self.recv.at[0],
                (2 * j + core, rep),
            )

        to(CHIPS // 2)
        for d in range(1, CHIPS // 2):
            to(CHIPS // 2 - d)
            to(CHIPS // 2 + d)

    def wait(self):
        rest = self.near.at[pl.ds(0, CHIPS - 1)]
        wait_received(self.at, rest, self.recv.at[0])
        across = remote(
            self.near, self.far, self.send.at[1], self.recv.at[1], core_peer(self.at)
        )
        wait_sent(self.at, rest, self.send.at[0])
        across.wait_recv()
        across.wait_send()

    def rows(self, source):
        dp, rep, z, core, spot = self.at
        wide = self.wide
        wide[...] = source[...].astype(F32)
        mine = lambda r, step: jnp.where(core == 0, wide[:, r, :], wide[:, r + step, :])
        return [
            (
                jnp.concatenate([mine(2 * slot, 4), mine(2 * slot + 1, 4)], axis=1).astype(BF16),
                mine(8 + slot, 2),
            )
            for slot in range(2)
        ]


def greet_all(at, barrier):
    dp, rep, z, core, spot = at
    chip = lax.div(dp, 2)
    peers = [(2 * lax.rem(chip + d, CHIPS) + core, rep) for d in range(1, CHIPS)]
    peers += [core_peer(at)]
    peers += [(8 * z + 2 * x + core, lax.rem(rep + d, 4)) for d in range(1, 4) for x in range(4)]
    for peer in peers:
        pl.semaphore_signal(barrier, inc=1, device_id=peer, device_id_type=MESH)
    return len(peers)


VMEM_LIMIT = 56 * 1024 * 1024
EPSILON = 1e-06
ROOT = math.sqrt(2.0 / math.pi)
HEADS = 8
W = 256
HEAD = 32
FF = 1024
TX, COLS = 24, 24
CUST, CTOK = 16, 32
ROWS = TX * COLS
PROWS = CUST * CTOK
GROUP = 4
GROWS = GROUP * COLS
GPROWS = GROUP * CTOK
GROUPS = TX // GROUP
PGROUPS = CUST // GROUP


def dot(a, b):
    return lax.dot_general(a, b, (((1,), (0,)), ((), ())), preferred_element_type=F32)


def dot_nt(a, b):
    return lax.dot_general(a, b, (((1,), (1,)), ((), ())), preferred_element_type=F32)


def dot_tn(a, b):
    return lax.dot_general(a, b, (((0,), (0,)), ((), ())), preferred_element_type=F32)


def each(count, step, body, unroll=1):
    def one(i, carry):
        body(pl.ds(pl.multiple_of(i * step, step), step), i)
        return carry

    lax.fori_loop(0, count, one, 0, unroll=unroll)


def head_masks():
    lane = lax.broadcasted_iota(jnp.int32, (1, W), 1)
    return [jnp.where(lax.div(lane, HEAD) == h, 1.0, 0.0) for h in range(HEADS)]


def spread_heads(value, masks):
    return jnp.concatenate([value * mask.astype(BF16) for mask in masks], axis=0)


def join_heads(value, masks, rows):
    total = value[:rows] * masks[0]
    for h in range(1, HEADS):
        total = total + value[h * rows : (h + 1) * rows] * masks[h]
    return total


def same_owner(rows, length):
    i = lax.div(lax.broadcasted_iota(jnp.int32, (rows, rows), 0), length)
    j = lax.div(lax.broadcasted_iota(jnp.int32, (rows, rows), 1), length)
    return jnp.concatenate([jnp.where(i == j, 0.0, -1e30)] * HEADS, axis=0)


def attend(q, k, v, probs, mix, groups, rows, length):
    masks = head_masks()
    bias = same_owner(rows, length)
    for i in range(groups):
        at = slice(i * rows, (i + 1) * rows)
        wide = spread_heads(q[at], masks)
        scores = dot_nt(wide, k[at]) * HEAD**-0.5 + bias
        e = jnp.exp(scores - jnp.max(scores, axis=1, keepdims=True))
        p = (e * (1.0 / jnp.sum(e, axis=1, keepdims=True))).astype(BF16)
        probs[i] = p
        mix[at] = join_heads(dot(p, v[at]), masks, rows).astype(BF16)


def attend_back(q, k, v, probs, dmix, dqkv, groups, rows, meanwhile=None):
    masks = head_masks()
    for i in range(groups):
        at = slice(i * rows, (i + 1) * rows)
        p = probs[i]
        wide_d = spread_heads(dmix[at], masks)
        wide_q = spread_heads(q[at], masks)
        weighted = p.astype(F32)
        ds = weighted * dot_nt(wide_d, v[at])
        ds = ds - weighted * jnp.sum(ds, axis=1, keepdims=True)
        ds = (ds * HEAD**-0.5).astype(BF16)
        dqkv[at, 0:W] = join_heads(dot(ds, k[at]), masks, rows).astype(BF16)
        dqkv[at, W : 2 * W] = dot_tn(ds, wide_q).astype(BF16)
        dqkv[at, 2 * W : 3 * W] = dot_tn(p, wide_d).astype(BF16)
        if meanwhile is not None:
            meanwhile(i)


def put_block(mine, b, value):
    for half in range(2):
        part = value[:, half * 128 : (half + 1) * 128].astype(BF16)
        mine[half, :, b] = part.reshape(16, 16, 128)


def rms_scale(value):
    return lax.rsqrt(jnp.mean(value * value, axis=1, keepdims=True) + EPSILON)


def averaging():
    t = lax.broadcasted_iota(jnp.int32, (TX, ROWS), 0)
    r = lax.div(lax.broadcasted_iota(jnp.int32, (TX, ROWS), 1), COLS)
    return jnp.where(t == r, 1.0, 0.0).astype(BF16)


def placing(owner_ref):
    owner = owner_ref[...]
    i = lax.broadcasted_iota(jnp.int32, (TX, TX), 0)
    j = lax.broadcasted_iota(jnp.int32, (TX, TX), 1)
    along = jnp.broadcast_to(owner, (TX, TX))
    down = jnp.sum(jnp.where(i == j, along, 0), axis=1, keepdims=True)
    slot = jnp.sum(jnp.where((down == along) & (i < j), 1, 0), axis=0, keepdims=True)
    chip = lax.broadcasted_iota(jnp.int32, (CHIPS, TX), 0)
    owner = jnp.broadcast_to(owner, (CHIPS, TX))
    slot = jnp.broadcast_to(slot, (CHIPS, TX))
    return [
        jnp.where((owner == 2 * chip + core) & (slot == s), 1.0, 0.0).astype(BF16)
        for core in range(2)
        for s in range(2)
    ]


LATER = ("parent", "cot", "co", "up", "down", "link", "pq", "pk", "pv", "po")


def encoder_kernel(
    item_ref, owner_ref, row_ref, parent_any, cot_any,
    cgain, cq, ck, cv, co_any, hgain, up_any, down_any, link_any, pgain, pq_any, pk_any, pv_any, po_any,
    states_ref, parent_sum, down_sum, up_sum, att_sum,
    n1, q, k, v, probs, mix, s_, n2, u, h, slope, dhidden, da, dmix, dqkv, hmean,
    pbased, pn, pq_, pk_, pv_, pprobs, pmix, pda, pdmix, pdqkv, pdn,
    parent_mine, down_mine, up_mine, att_mine,
    parent_ref, cot_ref, co, up, down, link, pq, pk, pv, po, load_sem,
    *comm_scratch,
):
    loads = {}
    for i, (name, source, target) in enumerate(
        zip(
            LATER,
            (parent_any, cot_any, co_any, up_any, down_any, link_any, pq_any, pk_any, pv_any, po_any),
            (parent_ref, cot_ref, co, up, down, link, pq, pk, pv, po),
            strict=True,
        )
    ):
        loads[name] = pltpu.make_async_copy(source, target, load_sem.at[i])
    for name in ("co", "up", "down", "cot", "po", "parent", "link", "pq", "pk", "pv"):
        loads[name].start()
    at = place()
    barrier = pltpu.get_barrier_semaphore()
    greeted = greet_all(at, barrier)
    jobs = zip(
        (5, 4, 4, 4),
        (parent_mine, down_mine, up_mine, att_mine),
        (parent_sum, down_sum, up_sum, att_sum),
        strict=True,
    )
    there = Exchange(at, comm_scratch[:6])
    back = Exchange(at, comm_scratch[6:12])
    job_scratch = comm_scratch[12:]
    per = len(job_scratch) // 4
    parent_job, down_job, up_job, att_job = [
        Summing(at, *job, job_scratch[i * per : (i + 1) * per]) for i, job in enumerate(jobs)
    ]

    def norm_items(rows, i):
        x = item_ref[pl.ds(i * GROUP, GROUP)].astype(F32).reshape(GROWS, W)
        n1[rows] = (x * rms_scale(x) * cgain[...].astype(F32)[None, :]).astype(BF16)

    each(GROUPS, GROWS, norm_items, unroll=2)
    q[...] = dot(n1[...], cq[...]).astype(BF16)
    k[...] = dot(n1[...], ck[...]).astype(BF16)
    v[...] = dot(n1[...], cv[...]).astype(BF16)
    attend(q, k, v, probs, mix, GROUPS, GROWS, COLS)
    loads["co"].wait()
    u[:, :W] = dot(mix[...], co[...])

    def norm_stream(rows, i):
        x = item_ref[pl.ds(i * GROUP, GROUP)].astype(F32).reshape(GROWS, W)
        stream = (x + u[rows, :W]).astype(BF16)
        s_[rows] = stream
        stream = stream.astype(F32)
        n2[rows] = (stream * rms_scale(stream) * hgain[...].astype(F32)[None, :]).astype(BF16)

    each(GROUPS, GROWS, norm_stream, unroll=2)
    loads["up"].wait()
    u[...] = dot(n2[...], up[...])

    def gelu(rows, i):
        for c in range(0, FF, 256):
            value = u[rows, c : c + 256]
            t = jnp.tanh(value * (ROOT + ROOT * 0.044715 * (value * value)))
            h[rows, c : c + 256] = (value * (0.5 + 0.5 * t)).astype(BF16)

    each(ROWS // 32, 32, gelu, unroll=3)
    average = averaging()
    hidden = (dot(average, h[...]) * (1.0 / COLS)).astype(BF16)
    hmean[...] = hidden
    loads["down"].wait()
    embedding = (dot(average, s_[...]) * (1.0 / COLS) + dot(hidden, down[...])).astype(BF16)

    places = placing(owner_ref)
    ids = jnp.broadcast_to(row_ref[...].astype(F32) + 1.0, (128, TX)).astype(BF16)
    for p in range(4):
        there.put(p, dot(places[p], embedding), dot_nt(places[p], ids))
    pl.semaphore_wait(barrier, greeted)
    there.start()

    def gelu_slope(rows, i):
        for c in range(0, FF, 256):
            value = u[rows, c : c + 256]
            square = value * value
            t = jnp.tanh(value * (ROOT + ROOT * 0.044715 * square))
            inner = value * (ROOT + 3 * ROOT * 0.044715 * square)
            half = 0.5 + 0.5 * t
            slope[rows, c : c + 256] = (half + 0.5 * (1.0 - t * t) * inner).astype(BF16)

    each(ROWS // 32, 32, gelu_slope, unroll=3)
    loads["cot"].wait()
    loads["po"].wait()
    scale = 1.0 / math.sqrt(CUST * CTOK * 256)
    pda[...] = (cot_ref[...].astype(F32) * scale).astype(BF16)
    pdmix[...] = dot_nt(pda[...], po[...]).astype(BF16)
    for name in ("parent", "link", "pq", "pk", "pv"):
        loads[name].wait()
    there.wait()

    members = []
    customer = lax.broadcasted_iota(jnp.int32, (CHIPS, CUST), 1).astype(F32) + 1.0
    counts, sums = jnp.zeros((CUST, W), F32), jnp.zeros((CUST, W), F32)
    for source in (there.near, there.far):
        for got, name in there.rows(source):
            member = jnp.where(name[:, :CUST] == customer, 1.0, 0.0).astype(BF16)
            members.append(member)
            counts = counts + dot_tn(member, jnp.ones((CHIPS, W), BF16))
            sums = sums + dot_tn(member, got)
    divisor = jnp.maximum(counts, 1.0)
    pooled = (sums / divisor).astype(BF16)
    linked = dot(pooled, link[...])
    pbased_value = (
        (parent_ref[...].astype(F32).reshape(CUST, CTOK, W) + linked[:, None, :])
        .astype(BF16)
        .reshape(PROWS, W)
    )
    pbased[...] = pbased_value

    def norm_based(rows, i):
        x = pbased[rows].astype(F32)
        pn[rows] = (x * rms_scale(x) * pgain[...].astype(F32)[None, :]).astype(BF16)

    each(PGROUPS, GPROWS, norm_based, unroll=2)
    pq_[...] = dot(pn[...], pq[...]).astype(BF16)
    pk_[...] = dot(pn[...], pk[...]).astype(BF16)
    pv_[...] = dot(pn[...], pv[...]).astype(BF16)
    attend(pq_, pk_, pv_, pprobs, pmix, PGROUPS, GPROWS, CTOK)
    attend_back(pq_, pk_, pv_, pprobs, pdmix, pdqkv, PGROUPS, GPROWS)
    pdn[...] = (
        dot_nt(pdqkv[:, :W], pq[...])
        + dot_nt(pdqkv[:, W : 2 * W], pk[...])
        + dot_nt(pdqkv[:, 2 * W :], pv[...])
    )

    dlinked = []
    for i in range(PGROUPS):
        rows = slice(i * GPROWS, (i + 1) * GPROWS)
        x = pbased[rows].astype(F32)
        r = rms_scale(x)
        unit = x * r
        dunit = pdn[rows] * pgain[...].astype(F32)[None, :]
        dx = r * (dunit - unit * jnp.mean(dunit * unit, axis=1, keepdims=True))
        dx = dx + cot_ref[rows].astype(F32) * scale
        dlinked.append(jnp.sum(dx.reshape(GROUP, CTOK, W), axis=1))
    dlinked = jnp.concatenate(dlinked, axis=0)
    dpooled = dot_nt(dlinked.astype(BF16), link[...]).astype(BF16).astype(F32)
    sum_grad = (dpooled / divisor).astype(BF16)
    core = at[3]
    moved = [dot(member, sum_grad) for member in members]
    for p in range(4):
        home, slot = p // 2, p % 2
        back.put(p, jnp.where(core == home, moved[slot], moved[2 + slot]))
    back.start()

    put_block(parent_mine, 0, dot_tn(pooled, dlinked.astype(BF16)))
    dweights = dot_tn(pn[...], pdqkv[...])
    for b in range(3):
        put_block(parent_mine, 1 + b, dweights[:, b * W : (b + 1) * W])
    put_block(parent_mine, 4, dot_tn(pmix[...], pda[...]))
    parent_job.start()
    states_ref[...] = (pbased[...].astype(F32) + dot(pmix[...], po[...])).astype(BF16)
    parent_job.scatter_plane()
    back.wait()

    ditem = jnp.zeros((TX, W), F32)
    near, far = back.rows(back.near), back.rows(back.far)
    for p in range(4):
        home, slot = p // 2, p % 2
        got = jnp.where(core == home, near[slot][0].astype(F32), far[slot][0].astype(F32))
        ditem = ditem + dot_tn(places[p], got.astype(BF16))
    ditem_b = ditem.astype(BF16)
    ddown = dot_tn(hmean[...], ditem_b)
    for b in range(4):
        put_block(down_mine, b, ddown[b * W : (b + 1) * W])
    down_job.start()
    dhidden[...] = (dot_nt(ditem_b, down[...]) * (1.0 / COLS)).astype(BF16).astype(F32)
    dy = dot_tn(averaging(), ditem_b)
    parent_job.scatter_z()

    def back_hidden(rows, i):
        for c in range(0, FF, 256):
            spread = jnp.concatenate(
                [
                    jnp.broadcast_to(dhidden[pl.ds(2 * i + t, 1), c : c + 256], (COLS, 256))
                    for t in range(2)
                ],
                axis=0,
            )
            h[rows, c : c + 256] = (spread * slope[rows, c : c + 256].astype(F32)).astype(BF16)

    each(TX // 2, 2 * COLS, back_hidden, unroll=3)
    down_job.scatter_plane()
    dup = dot_tn(n2[...], h[...])
    for b in range(4):
        put_block(up_mine, b, dup[:, b * W : (b + 1) * W])
    up_job.start()
    u[:, :W] = dot_nt(h[...], up[...])
    u[:, W : 2 * W] = dy

    def back_stream(rows, i):
        x = s_[rows].astype(F32)
        r = rms_scale(x)
        unit = x * r
        dunit = u[rows, :W].astype(BF16).astype(F32) * hgain[...].astype(F32)[None, :]
        dx = r * (dunit - unit * jnp.mean(dunit * unit, axis=1, keepdims=True))
        da[rows] = (dx + u[rows, W : 2 * W] * (1.0 / COLS)).astype(BF16)

    each(GROUPS, GROWS, back_stream, unroll=2)
    up_job.scatter_plane()
    dmix[...] = dot_nt(da[...], co[...]).astype(BF16)
    put_block(att_mine, 3, dot_tn(mix[...], da[...]))
    meanwhile = {2: down_job.scatter_z, 4: parent_job.gather_plane}
    attend_back(q, k, v, probs, dmix, dqkv, GROUPS, GROWS, lambda i: meanwhile.get(i, int)())
    dweights = dot_tn(n1[...], dqkv[...])
    for b in range(3):
        put_block(att_mine, b, dweights[:, b * W : (b + 1) * W])
    att_job.start()

    att_job.scatter_plane()
    up_job.scatter_z()
    parent_job.gather_core()
    down_job.gather_plane()
    att_job.scatter_z()
    up_job.gather_plane()
    down_job.gather_core()
    att_job.gather_plane()
    up_job.gather_core()
    att_job.gather_core()
    for job in (parent_job, down_job, up_job, att_job):
        job.finish()


def gain_row(weights, sums, gain):
    total = jnp.zeros((W, W), F32)
    for weight, value in zip(weights, sums, strict=True):
        total = total + weight.astype(F32) * value
    high = total.astype(BF16)
    low = (total - high.astype(F32)).astype(BF16)
    ones = jnp.ones((8, W), BF16)
    return (dot_nt(ones, high) + dot_nt(ones, low))[:1] / gain.astype(F32)[None, :]


def unpack_kernel(
    states_in, parent_sum, down_sum, up_sum, att_sum, cgain, cq, ck, cv, hgain, up, pgain, pq, pk, pv,
    states, dcg, dcq, dck, dcv, dco, dhg, dup, ddown, dlink, dpg, dpq, dpk, dpv, dpo,
):
    def block(total, b):
        return jnp.concatenate(
            [total[half, :, b].astype(F32).reshape(W, 128) for half in range(2)], axis=1
        )

    states[...] = states_in[...]
    grads = []
    for b, ref in enumerate((dcq, dck, dcv, dco)):
        grads.append(block(att_sum, b))
        ref[...] = grads[-1]
    dcg[...] = gain_row([cq[...], ck[...], cv[...]], grads[:3], cgain[...])
    grads = []
    for b in range(4):
        ddown[b * W : (b + 1) * W] = block(down_sum, b)
        grads.append(block(up_sum, b))
        dup[:, b * W : (b + 1) * W] = grads[-1]
    dhg[...] = gain_row([up[:, b * W : (b + 1) * W] for b in range(4)], grads, hgain[...])
    grads = []
    for b, ref in enumerate((dlink, dpq, dpk, dpv, dpo)):
        grads.append(block(parent_sum, b))
        ref[...] = grads[-1]
    dpg[...] = gain_row([pq[...], pk[...], pv[...]], grads[1:4], pgain[...])


def body(
    item_tokens, owner_index, owner_row, parent_tokens, cotangent,
    column_gain, column_query, column_key, column_value, column_out,
    hidden_gain, up_weight, down_weight, link_weight,
    parent_gain, parent_query, parent_key, parent_value, parent_out,
):
    vmem = pl.BlockSpec(memory_space=pltpu.VMEM)
    later = pl.BlockSpec(memory_space=pl.ANY)
    shape = jax.ShapeDtypeStruct
    cgain, hgain, pgain = column_gain, hidden_gain, parent_gain
    items = lambda width, dtype=BF16: pltpu.VMEM((ROWS, width), dtype)
    parents = lambda width, dtype=BF16: pltpu.VMEM((PROWS, width), dtype)
    scratch = [
        items(W), items(W), items(W), items(W),
        pltpu.VMEM((GROUPS, HEADS * GROWS, GROWS), BF16),
        items(W), items(W), items(W), items(FF, F32), items(FF), items(FF),
        pltpu.VMEM((TX, FF), F32), items(W), items(W), items(3 * W),
        pltpu.VMEM((TX, FF), BF16),
        parents(W), parents(W), parents(W), parents(W), parents(W),
        pltpu.VMEM((PGROUPS, HEADS * GPROWS, GPROWS), BF16),
        parents(W), parents(W), parents(W), parents(3 * W), parents(W, F32),
        *[pltpu.VMEM((2, 16, n, 16, 128), BF16) for n in (5, 4, 4, 4)],
        parents(W), parents(W), pltpu.VMEM((W, W), BF16), pltpu.VMEM((W, FF), BF16),
        pltpu.VMEM((FF, W), BF16), *[pltpu.VMEM((W, W), BF16) for _ in range(5)],
        pltpu.SemaphoreType.DMA((len(LATER),)),
        *Exchange.scratch(), *Exchange.scratch(),
    ]
    for n in (5, 4, 4, 4):
        scratch += Summing.scratch(n)
    states, parent_sum, down_sum, up_sum, att_sum = pl.pallas_call(
        encoder_kernel,
        out_shape=[shape((PROWS, W), BF16)]
        + [shape((2, 16, n, 16, 128), BF16) for n in (5, 4, 4, 4)],
        in_specs=[vmem] * 3 + [later] * 2 + [vmem] * 4 + [later] + [vmem] + [later] * 3 + [vmem]
        + [later] * 4,
        out_specs=[vmem] * 5,
        scratch_shapes=scratch,
        compiler_params=pltpu.CompilerParams(
            collective_id=1, has_side_effects=True, vmem_limit_bytes=VMEM_LIMIT
        ),
        name="encoder",
    )(
        item_tokens, owner_index.reshape(1, TX), owner_row.reshape(1, TX),
        parent_tokens.reshape(PROWS, W), cotangent.reshape(PROWS, W),
        cgain, column_query, column_key, column_value, column_out,
        hgain, up_weight, down_weight, link_weight,
        pgain, parent_query, parent_key, parent_value, parent_out,
    )
    square = shape((W, W), F32)
    row = shape((1, W), F32)
    out = pl.pallas_call(
        unpack_kernel,
        out_shape=[
            shape((PROWS, W), BF16), row, square, square, square, square, row,
            shape((W, FF), F32), shape((FF, W), F32), square, row, square, square, square, square,
        ],
        in_specs=[vmem] * 15,
        out_specs=[vmem] * 15,
        compiler_params=pltpu.CompilerParams(vmem_limit_bytes=VMEM_LIMIT),
        name="unpack",
    )(
        states, parent_sum, down_sum, up_sum, att_sum, cgain, column_query, column_key, column_value,
        hgain, up_weight, pgain, parent_query, parent_key, parent_value,
    )
    out = [o.reshape(W) if o.shape == (1, W) else o for o in out]
    return (out[0].reshape(CUST, CTOK, W), *out[1:])


def solution(mesh):
    split, whole = P(("dp", "rep")), P()
    return jax.shard_map(
        body,
        mesh=mesh,
        in_specs=(split,) * 5 + (whole,) * 14,
        out_specs=(split,) + (whole,) * 14,
        check_vma=False,
    )
```

```python
import math

import jax
import jax.numpy as jnp
from jax import lax
from jax.experimental import pallas as pl
from jax.experimental.pallas import tpu as pltpu
from jax.sharding import PartitionSpec as P

MESH = pl.DeviceIdType.MESH
F32 = jnp.float32
BF16 = jnp.bfloat16
CHIPS = 32


def place():
    dp, rep = lax.axis_index("dp"), lax.axis_index("rep")
    z, x, core = lax.div(dp, 8), lax.rem(lax.div(dp, 2), 4), lax.rem(dp, 2)
    return dp, rep, z, core, rep * 4 + x


def core_peer(at):
    dp, rep, z, core, spot = at
    return (dp + 1 - 2 * core, rep)


def plane_peer(at, j):
    dp, rep, z, core, spot = at
    return (8 * z + 2 * lax.rem(j, 4) + core, lax.div(j, 4))


def z_peer(at, j):
    dp, rep, z, core, spot = at
    return (8 * j + lax.rem(dp, 8), rep)


def remote(src, dst, send, recv, peer):
    copy = pltpu.make_async_remote_copy(
        src_ref=src, dst_ref=dst, send_sem=send, recv_sem=recv, device_id=peer, device_id_type=MESH
    )
    copy.start()
    return copy


def wait_sent(at, like, sem):
    pltpu.make_async_remote_copy(
        src_ref=like, dst_ref=like, send_sem=sem, recv_sem=sem,
        device_id=core_peer(at), device_id_type=MESH,
    ).wait_send()


def wait_received(at, like, sem):
    pltpu.make_async_remote_copy(
        src_ref=like, dst_ref=like, send_sem=sem, recv_sem=sem,
        device_id=core_peer(at), device_id_type=MESH,
    ).wait_recv()


class Summing:
    def __init__(self, at, n, mine, total, scratch):
        self.at, self.n, self.mine, self.total = at, n, mine, total
        self.core_in, self.plane_out, self.plane_in, self.z_all, self.send, self.recv = scratch

    @staticmethod
    def scratch(n):
        return [
            pltpu.VMEM((16, n, 16, 128), BF16),
            pltpu.VMEM((16, n, 16, 128), BF16),
            pltpu.VMEM((15, n, 16, 128), BF16),
            pltpu.VMEM((8, n, 16, 128), BF16),
            pltpu.SemaphoreType.DMA((5,)),
            pltpu.SemaphoreType.DMA((20,)),
        ]

    def start(self):
        dp, rep, z, core, spot = self.at
        self.from_core = remote(
            self.mine.at[1 - core], self.core_in, self.send.at[0], self.recv.at[0], core_peer(self.at)
        )

    def scatter_plane(self):
        dp, rep, z, core, spot = self.at
        self.from_core.wait_recv()
        self.plane_out[...] = (
            self.mine[core].astype(F32) + self.core_in[...].astype(F32)
        ).astype(BF16)
        for d in range(1, 16):
            q = lax.rem(spot + d, 16)
            remote(
                self.plane_out.at[q], self.plane_in.at[d - 1], self.send.at[1], self.recv.at[1],
                plane_peer(self.at, q),
            )

    def scatter_z(self):
        dp, rep, z, core, spot = self.at
        wait_received(self.at, self.plane_in, self.recv.at[1])
        value = self.plane_out[spot].astype(F32)
        for i in range(15):
            value = value + self.plane_in[i].astype(F32)
        self.z_all[z] = value.astype(BF16)
        for d in range(1, 8):
            here = self.z_all.at[z]
            remote(here, here, self.send.at[2], self.recv.at[2], z_peer(self.at, lax.rem(z + d, 8)))

    def gather_plane(self):
        dp, rep, z, core, spot = self.at
        wait_received(self.at, self.z_all.at[pl.ds(0, 7)], self.recv.at[2])
        value = self.z_all[0].astype(F32)
        for i in range(1, 8):
            value = value + self.z_all[i].astype(F32)
        self.total[core, spot] = value.astype(BF16)
        here = self.total.at[core, spot]
        self.from_plane = [
            remote(
                here, here, self.send.at[3], self.recv.at[3 + d],
                plane_peer(self.at, lax.rem(spot + d, 16)),
            )
            for d in range(1, 16)
        ]
        remote(here, here, self.send.at[4], self.recv.at[3], core_peer(self.at))

    def gather_core(self):
        dp, rep, z, core, spot = self.at
        for d, copy in zip(range(1, 16), self.from_plane, strict=True):
            copy.wait_recv()
            here = self.total.at[core, lax.rem(spot + 16 - d, 16)]
            remote(here, here, self.send.at[4], self.recv.at[3], core_peer(self.at))

    def finish(self):
        dp, rep, z, core, spot = self.at
        wait_received(self.at, self.total.at[1 - core], self.recv.at[3])
        self.from_core.wait_send()
        wait_sent(self.at, self.plane_in, self.send.at[1])
        wait_sent(self.at, self.z_all.at[pl.ds(0, 7)], self.send.at[2])
        wait_sent(self.at, self.total.at[core, pl.ds(0, 15)], self.send.at[3])
        wait_sent(self.at, self.total.at[core], self.send.at[4])


class Exchange:
    def __init__(self, at, scratch):
        self.at = at
        self.wide, self.out, self.near, self.far, self.send, self.recv = scratch

    @staticmethod
    def scratch():
        return [
            pltpu.VMEM((CHIPS, 16, 128), F32),
            pltpu.VMEM((CHIPS, 16, 128), BF16),
            pltpu.VMEM((CHIPS, 16, 128), BF16),
            pltpu.VMEM((CHIPS, 16, 128), BF16),
            pltpu.SemaphoreType.DMA((2,)),
            pltpu.SemaphoreType.DMA((2,)),
        ]

    def put(self, p, value, extra=None):
        self.wide[:, 2 * p, :] = value[:, :128]
        self.wide[:, 2 * p + 1, :] = value[:, 128:]
        self.wide[:, 8 + p, :] = jnp.zeros((CHIPS, 128), F32) if extra is None else extra
        self.wide[:, 12 + p, :] = jnp.zeros((CHIPS, 128), F32)

    def start(self):
        dp, rep, z, core, spot = self.at
        chip = lax.div(dp, 2)
        self.out[...] = self.wide[...].astype(BF16)
        self.near[chip] = self.out[chip]

        def to(d):
            j = lax.rem(chip + d, CHIPS)
            remote(
                self.out.at[j], self.near.at[chip], self.send.at[0], self.recv.at[0],
                (2 * j + core, rep),
            )

        to(CHIPS // 2)
        for d in range(1, CHIPS // 2):
            to(CHIPS // 2 - d)
            to(CHIPS // 2 + d)

    def wait(self):
        rest = self.near.at[pl.ds(0, CHIPS - 1)]
        wait_received(self.at, rest, self.recv.at[0])
        across = remote(
            self.near, self.far, self.send.at[1], self.recv.at[1], core_peer(self.at)
        )
        wait_sent(self.at, rest, self.send.at[0])
        across.wait_recv()
        across.wait_send()

    def rows(self, source):
        dp, rep, z, core, spot = self.at
        wide = self.wide
        wide[...] = source[...].astype(F32)
        mine = lambda r, step: jnp.where(core == 0, wide[:, r, :], wide[:, r + step, :])
        return [
            (
                jnp.concatenate([mine(2 * slot, 4), mine(2 * slot + 1, 4)], axis=1).astype(BF16),
                mine(8 + slot, 2),
            )
            for slot in range(2)
        ]


def greet_all(at, barrier):
    dp, rep, z, core, spot = at
    chip = lax.div(dp, 2)
    peers = [(2 * lax.rem(chip + d, CHIPS) + core, rep) for d in range(1, CHIPS)]
    peers += [core_peer(at)]
    peers += [(8 * z + 2 * x + core, lax.rem(rep + d, 4)) for d in range(1, 4) for x in range(4)]
    for peer in peers:
        pl.semaphore_signal(barrier, inc=1, device_id=peer, device_id_type=MESH)
    return len(peers)


VMEM_LIMIT = 56 * 1024 * 1024
UNPACK_LIMIT = 50 * 1024 * 1024
EPSILON = 1e-06
ROOT = math.sqrt(2.0 / math.pi)
HEADS = 8
W = 256
HEAD = 32
FF = 1024
TX, COLS = 24, 24
CUST, CTOK = 16, 32
ROWS = TX * COLS
PROWS = CUST * CTOK
GROUP = 4
GROWS = GROUP * COLS
GPROWS = GROUP * CTOK
GROUPS = TX // GROUP
PGROUPS = CUST // GROUP


def dot(a, b):
    return lax.dot_general(a, b, (((1,), (0,)), ((), ())), preferred_element_type=F32)


def dot_nt(a, b):
    return lax.dot_general(a, b, (((1,), (1,)), ((), ())), preferred_element_type=F32)


def dot_tn(a, b):
    return lax.dot_general(a, b, (((0,), (0,)), ((), ())), preferred_element_type=F32)


def each(count, step, body):
    for i in range(count):
        body(slice(i * step, (i + 1) * step), i)


def head_masks():
    lane = lax.broadcasted_iota(jnp.int32, (1, W), 1)
    return [jnp.where(lax.div(lane, HEAD) == h, 1.0, 0.0) for h in range(HEADS)]


def spread_heads(value, masks):
    return jnp.concatenate([value * mask.astype(BF16) for mask in masks], axis=0)


def join_heads(value, masks, rows):
    total = value[:rows] * masks[0]
    for h in range(1, HEADS):
        total = total + value[h * rows : (h + 1) * rows] * masks[h]
    return total


def same_owner(rows, length):
    i = lax.div(lax.broadcasted_iota(jnp.int32, (rows, rows), 0), length)
    j = lax.div(lax.broadcasted_iota(jnp.int32, (rows, rows), 1), length)
    return jnp.concatenate([jnp.where(i == j, 0.0, -1e30)] * HEADS, axis=0)


def attend(q, k, v, probs, mix, groups, rows, length):
    masks = head_masks()
    bias = same_owner(rows, length)
    for i in range(groups):
        at = slice(i * rows, (i + 1) * rows)
        wide = spread_heads(q[at], masks)
        scores = dot_nt(wide, k[at]) * HEAD**-0.5 + bias
        e = jnp.exp(scores - jnp.max(scores, axis=1, keepdims=True))
        p = (e * (1.0 / jnp.sum(e, axis=1, keepdims=True))).astype(BF16)
        probs[i] = p
        mix[at] = join_heads(dot(p, v[at]), masks, rows).astype(BF16)


def attend_back(q, k, v, probs, dmix, dqkv, groups, rows, meanwhile=None):
    masks = head_masks()
    for i in range(groups):
        at = slice(i * rows, (i + 1) * rows)
        p = probs[i]
        wide_d = spread_heads(dmix[at], masks)
        wide_q = spread_heads(q[at], masks)
        weighted = p.astype(F32)
        ds = weighted * dot_nt(wide_d, v[at])
        ds = ds - weighted * jnp.sum(ds, axis=1, keepdims=True)
        ds = (ds * HEAD**-0.5).astype(BF16)
        dqkv[at, 0:W] = join_heads(dot(ds, k[at]), masks, rows).astype(BF16)
        dqkv[at, W : 2 * W] = dot_tn(ds, wide_q).astype(BF16)
        dqkv[at, 2 * W : 3 * W] = dot_tn(p, wide_d).astype(BF16)
        if meanwhile is not None:
            meanwhile(i)


def put_block(mine, b, value):
    for half in range(2):
        part = value[:, half * 128 : (half + 1) * 128].astype(BF16)
        mine[half, :, b] = part.reshape(16, 16, 128)


def rms_scale(value):
    return lax.rsqrt(jnp.mean(value * value, axis=1, keepdims=True) + EPSILON)


def averaging():
    t = lax.broadcasted_iota(jnp.int32, (TX, ROWS), 0)
    r = lax.div(lax.broadcasted_iota(jnp.int32, (TX, ROWS), 1), COLS)
    return jnp.where(t == r, 1.0, 0.0).astype(BF16)


def placing(owner_ref):
    owner = owner_ref[...]
    i = lax.broadcasted_iota(jnp.int32, (TX, TX), 0)
    j = lax.broadcasted_iota(jnp.int32, (TX, TX), 1)
    along = jnp.broadcast_to(owner, (TX, TX))
    down = jnp.sum(jnp.where(i == j, along, 0), axis=1, keepdims=True)
    slot = jnp.sum(jnp.where((down == along) & (i < j), 1, 0), axis=0, keepdims=True)
    chip = lax.broadcasted_iota(jnp.int32, (CHIPS, TX), 0)
    owner = jnp.broadcast_to(owner, (CHIPS, TX))
    slot = jnp.broadcast_to(slot, (CHIPS, TX))
    return [
        jnp.where((owner == 2 * chip + core) & (slot == s), 1.0, 0.0).astype(BF16)
        for core in range(2)
        for s in range(2)
    ]


BLOCKS = (5, 4, 5, 3)
LATER = ("cq", "ck", "cv", "parent", "cot", "co", "up", "down", "link", "pq", "pk", "pv", "po")


def encoder_kernel(
    item_ref, owner_ref, row_ref, parent_any, cot_any,
    cgain, cq_any, ck_any, cv_any, co_any, hgain, up_any, down_any, link_any, pgain, pq_any, pk_any, pv_any, po_any,
    states_ref, parent_sum, down_sum, up_sum, att_sum, kept, up, gains,
    n1, q, k, v, probs, mix, s_, n2, u, h, slope, dhidden, da, dmix, dqkv, hmean,
    pbased, pn, pq_, pk_, pv_, pprobs, pmix, pda, pdmix, pdqkv, pdn,
    parent_mine, down_mine, up_mine, att_mine,
    parent_ref, cot_ref, co, down, link, po, load_sem,
    *comm_scratch,
):
    cq, ck, cv, pq, pk, pv = (kept.at[i] for i in range(6))
    loads = {}
    for i, (name, source, target) in enumerate(
        zip(
            LATER,
            (
                cq_any, ck_any, cv_any, parent_any, cot_any, co_any, up_any, down_any, link_any,
                pq_any, pk_any, pv_any, po_any,
            ),
            (cq, ck, cv, parent_ref, cot_ref, co, up, down, link, pq, pk, pv, po),
            strict=True,
        )
    ):
        loads[name] = pltpu.make_async_copy(source, target, load_sem.at[i])
    for name in ("cq", "ck", "cv", "co", "up", "down", "cot", "po", "parent", "link", "pq", "pk", "pv"):
        loads[name].start()
    at = place()
    barrier = pltpu.get_barrier_semaphore()
    greeted = greet_all(at, barrier)
    jobs = zip(
        BLOCKS,
        (parent_mine, down_mine, up_mine, att_mine),
        (parent_sum, down_sum, up_sum, att_sum),
        strict=True,
    )
    there = Exchange(at, comm_scratch[:6])
    back = Exchange(at, comm_scratch[6:12])
    job_scratch = comm_scratch[12:]
    per = len(job_scratch) // 4
    parent_job, down_job, up_job, att_job = [
        Summing(at, *job, job_scratch[i * per : (i + 1) * per]) for i, job in enumerate(jobs)
    ]

    def norm_items(rows, i):
        x = item_ref[i * GROUP : (i + 1) * GROUP].astype(F32).reshape(GROWS, W)
        n1[rows] = (x * rms_scale(x) * cgain[...].astype(F32)[None, :]).astype(BF16)

    each(GROUPS, GROWS, norm_items)
    for i, gain in enumerate((cgain, pgain, hgain)):
        gains[i : i + 1] = gain[...].astype(F32)[None, :]
    for name in ("cq", "ck", "cv"):
        loads[name].wait()
    q[...] = dot(n1[...], cq[...]).astype(BF16)
    k[...] = dot(n1[...], ck[...]).astype(BF16)
    v[...] = dot(n1[...], cv[...]).astype(BF16)
    attend(q, k, v, probs, mix, GROUPS, GROWS, COLS)
    loads["co"].wait()
    u[:, :W] = dot(mix[...], co[...])

    def norm_stream(rows, i):
        x = item_ref[i * GROUP : (i + 1) * GROUP].astype(F32).reshape(GROWS, W)
        stream = (x + u[rows, :W]).astype(BF16)
        s_[rows] = stream
        stream = stream.astype(F32)
        n2[rows] = (stream * rms_scale(stream) * hgain[...].astype(F32)[None, :]).astype(BF16)

    each(GROUPS, GROWS, norm_stream)
    loads["up"].wait()
    u[...] = dot(n2[...], up[...])

    def gelu(rows, i):
        for c in range(0, FF, 256):
            value = u[rows, c : c + 256]
            t = jnp.tanh(value * (ROOT + ROOT * 0.044715 * (value * value)))
            h[rows, c : c + 256] = (value * (0.5 + 0.5 * t)).astype(BF16)

    each(ROWS // 32, 32, gelu)
    average = averaging()
    hidden = (dot(average, h[...]) * (1.0 / COLS)).astype(BF16)
    hmean[...] = hidden
    loads["down"].wait()
    embedding = (dot(average, s_[...]) * (1.0 / COLS) + dot(hidden, down[...])).astype(BF16)

    places = placing(owner_ref)
    ids = jnp.broadcast_to(row_ref[...].astype(F32) + 1.0, (128, TX)).astype(BF16)
    for p in range(4):
        there.put(p, dot(places[p], embedding), dot_nt(places[p], ids))
    pl.semaphore_wait(barrier, greeted)
    there.start()

    def gelu_slope(rows, i):
        for c in range(0, FF, 256):
            value = u[rows, c : c + 256]
            square = value * value
            t = jnp.tanh(value * (ROOT + ROOT * 0.044715 * square))
            inner = value * (ROOT + 3 * ROOT * 0.044715 * square)
            half = 0.5 + 0.5 * t
            slope[rows, c : c + 256] = (half + 0.5 * (1.0 - t * t) * inner).astype(BF16)

    each(ROWS // 32, 32, gelu_slope)
    loads["cot"].wait()
    loads["po"].wait()
    scale = 1.0 / math.sqrt(CUST * CTOK * 256)
    pda[...] = (cot_ref[...].astype(F32) * scale).astype(BF16)
    pdmix[...] = dot_nt(pda[...], po[...]).astype(BF16)
    for name in ("parent", "link", "pq", "pk", "pv"):
        loads[name].wait()
    there.wait()

    members = []
    customer = lax.broadcasted_iota(jnp.int32, (CHIPS, CUST), 1).astype(F32) + 1.0
    counts, sums = jnp.zeros((CUST, W), F32), jnp.zeros((CUST, W), F32)
    for source in (there.near, there.far):
        for got, name in there.rows(source):
            member = jnp.where(name[:, :CUST] == customer, 1.0, 0.0).astype(BF16)
            members.append(member)
            counts = counts + dot_tn(member, jnp.ones((CHIPS, W), BF16))
            sums = sums + dot_tn(member, got)
    divisor = jnp.maximum(counts, 1.0)
    pooled = (sums / divisor).astype(BF16)
    linked = dot(pooled, link[...])
    pbased_value = (
        (parent_ref[...].astype(F32).reshape(CUST, CTOK, W) + linked[:, None, :])
        .astype(BF16)
        .reshape(PROWS, W)
    )
    pbased[...] = pbased_value

    def norm_based(rows, i):
        x = pbased[rows].astype(F32)
        pn[rows] = (x * rms_scale(x) * pgain[...].astype(F32)[None, :]).astype(BF16)

    each(PGROUPS, GPROWS, norm_based)
    pq_[...] = dot(pn[...], pq[...]).astype(BF16)
    pk_[...] = dot(pn[...], pk[...]).astype(BF16)
    pv_[...] = dot(pn[...], pv[...]).astype(BF16)
    attend(pq_, pk_, pv_, pprobs, pmix, PGROUPS, GPROWS, CTOK)
    attend_back(pq_, pk_, pv_, pprobs, pdmix, pdqkv, PGROUPS, GPROWS)
    pdn[...] = (
        dot_nt(pdqkv[:, :W], pq[...])
        + dot_nt(pdqkv[:, W : 2 * W], pk[...])
        + dot_nt(pdqkv[:, 2 * W :], pv[...])
    )

    dlinked = []
    for i in range(PGROUPS):
        rows = slice(i * GPROWS, (i + 1) * GPROWS)
        x = pbased[rows].astype(F32)
        r = rms_scale(x)
        unit = x * r
        dunit = pdn[rows] * pgain[...].astype(F32)[None, :]
        dx = r * (dunit - unit * jnp.mean(dunit * unit, axis=1, keepdims=True))
        dx = dx + cot_ref[rows].astype(F32) * scale
        dlinked.append(jnp.sum(dx.reshape(GROUP, CTOK, W), axis=1))
    dlinked = jnp.concatenate(dlinked, axis=0)
    dpooled = dot_nt(dlinked.astype(BF16), link[...]).astype(BF16).astype(F32)
    sum_grad = (dpooled / divisor).astype(BF16)
    core = at[3]
    moved = [dot(member, sum_grad) for member in members]
    for p in range(4):
        home, slot = p // 2, p % 2
        back.put(p, jnp.where(core == home, moved[slot], moved[2 + slot]))
    back.start()

    put_block(parent_mine, 0, dot_tn(pooled, dlinked.astype(BF16)))
    dweights = dot_tn(pn[...], pdqkv[...])
    for b in range(3):
        put_block(parent_mine, 1 + b, dweights[:, b * W : (b + 1) * W])
    put_block(parent_mine, 4, dot_tn(pmix[...], pda[...]))
    parent_job.start()
    states_ref[...] = (pbased[...].astype(F32) + dot(pmix[...], po[...])).astype(BF16)
    parent_job.scatter_plane()
    back.wait()

    ditem = jnp.zeros((TX, W), F32)
    near, far = back.rows(back.near), back.rows(back.far)
    for p in range(4):
        home, slot = p // 2, p % 2
        got = jnp.where(core == home, near[slot][0].astype(F32), far[slot][0].astype(F32))
        ditem = ditem + dot_tn(places[p], got.astype(BF16))
    ditem_b = ditem.astype(BF16)
    ddown = dot_tn(hmean[...], ditem_b)
    for b in range(4):
        put_block(down_mine, b, ddown[b * W : (b + 1) * W])
    down_job.start()
    dhidden[...] = (dot_nt(ditem_b, down[...]) * (1.0 / COLS)).astype(BF16).astype(F32)
    dy = dot_tn(averaging(), ditem_b)

    def back_hidden(rows, i):
        spread = jnp.concatenate(
            [jnp.broadcast_to(dhidden[t : t + 1], (COLS, FF)) for t in (2 * i, 2 * i + 1)], axis=0
        )
        h[rows] = (spread * slope[rows].astype(F32)).astype(BF16)

    each(TX // 2, 2 * COLS, back_hidden)
    down_job.scatter_plane()
    dup = dot_tn(n2[...], h[...])
    for b in range(4):
        put_block(up_mine, b, dup[:, b * W : (b + 1) * W])
    u[:, :W] = dot_nt(h[...], up[...])
    u[:, W : 2 * W] = dy

    def back_stream(rows, i):
        x = s_[rows].astype(F32)
        r = rms_scale(x)
        unit = x * r
        dunit = u[rows, :W].astype(BF16).astype(F32) * hgain[...].astype(F32)[None, :]
        dx = r * (dunit - unit * jnp.mean(dunit * unit, axis=1, keepdims=True))
        da[rows] = (dx + u[rows, W : 2 * W] * (1.0 / COLS)).astype(BF16)

    each(GROUPS, GROWS, back_stream)
    put_block(up_mine, 4, dot_tn(mix[...], da[...]))
    up_job.start()
    dmix[...] = dot_nt(da[...], co[...]).astype(BF16)
    up_job.scatter_plane()
    meanwhile = {1: parent_job.scatter_z, 4: down_job.scatter_z}
    attend_back(q, k, v, probs, dmix, dqkv, GROUPS, GROWS, lambda i: meanwhile.get(i, int)())
    dweights = dot_tn(n1[...], dqkv[...])
    for b in range(3):
        put_block(att_mine, b, dweights[:, b * W : (b + 1) * W])
    att_job.start()

    att_job.scatter_plane()
    parent_job.gather_plane()
    up_job.scatter_z()
    down_job.gather_plane()
    att_job.scatter_z()
    parent_job.gather_core()
    up_job.gather_plane()
    down_job.gather_core()
    att_job.gather_plane()
    up_job.gather_core()
    att_job.gather_core()
    for job in (parent_job, down_job, up_job, att_job):
        job.finish()


def gain_row(weights, sums, gain):
    total = jnp.zeros((W, W), F32)
    for weight, value in zip(weights, sums, strict=True):
        total = total + weight.astype(F32) * value
    high = total.astype(BF16)
    low = (total - high.astype(F32)).astype(BF16)
    ones = jnp.ones((8, W), BF16)
    return (dot_nt(ones, high) + dot_nt(ones, low))[:1] / gain


def unpack_kernel(
    states_in, parent_sum, down_sum, up_sum, att_sum, kept, up, gains,
    states, dcg, dcq, dck, dcv, dco, dhg, dup, ddown, dlink, dpg, dpq, dpk, dpv, dpo,
    stage, wide_stage, tall_stage, gain_stage, store_sem,
):
    def block(total, b):
        return jnp.concatenate(
            [total[half, :, b].astype(F32).reshape(W, 128) for half in range(2)], axis=1
        )

    copies = []

    def store(source, target):
        copies.append(pltpu.make_async_copy(source, target, store_sem.at[len(copies)]))
        copies[-1].start()

    store(states_in, states)
    for b in range(4):
        tall_stage[b * W : (b + 1) * W] = block(down_sum, b)
    store(tall_stage, ddown)
    for b in range(4):
        wide_stage[:, b * W : (b + 1) * W] = block(up_sum, b)
    store(wide_stage, dup)
    squares = [(att_sum, b, ref) for b, ref in enumerate((dcq, dck, dcv))]
    squares += [(parent_sum, b, ref) for b, ref in enumerate((dlink, dpq, dpk, dpv, dpo))]
    squares += [(up_sum, 4, dco)]
    for i, (total, b, ref) in enumerate(squares):
        stage[i] = block(total, b)
        store(stage.at[i], ref)
    for i in range(2):
        grads = [stage[j] for j in ((0, 1, 2), (4, 5, 6))[i]]
        gain_stage[i] = gain_row([kept[3 * i + j] for j in range(3)], grads, gains[i : i + 1])
    cuts = [slice(b * W, (b + 1) * W) for b in range(4)]
    gain_stage[2] = gain_row(
        [up[:, c] for c in cuts], [wide_stage[:, c] for c in cuts], gains[2:3]
    )
    for i, ref in enumerate((dcg, dpg, dhg)):
        store(gain_stage.at[i], ref)
    for done in copies:
        done.wait()


def body(
    item_tokens, owner_index, owner_row, parent_tokens, cotangent,
    column_gain, column_query, column_key, column_value, column_out,
    hidden_gain, up_weight, down_weight, link_weight,
    parent_gain, parent_query, parent_key, parent_value, parent_out,
):
    vmem = pl.BlockSpec(memory_space=pltpu.VMEM)
    later = pl.BlockSpec(memory_space=pl.ANY)
    shape = jax.ShapeDtypeStruct
    cgain, hgain, pgain = column_gain, hidden_gain, parent_gain
    items = lambda width, dtype=BF16: pltpu.VMEM((ROWS, width), dtype)
    parents = lambda width, dtype=BF16: pltpu.VMEM((PROWS, width), dtype)
    scratch = [
        items(W), items(W), items(W), items(W),
        pltpu.VMEM((GROUPS, HEADS * GROWS, GROWS), BF16),
        items(W), items(W), items(W), items(FF, F32), items(FF), items(FF),
        pltpu.VMEM((TX, FF), F32), items(W), items(W), items(3 * W),
        pltpu.VMEM((TX, FF), BF16),
        parents(W), parents(W), parents(W), parents(W), parents(W),
        pltpu.VMEM((PGROUPS, HEADS * GPROWS, GPROWS), BF16),
        parents(W), parents(W), parents(W), parents(3 * W), parents(W, F32),
        *[pltpu.VMEM((2, 16, n, 16, 128), BF16) for n in BLOCKS],
        parents(W), parents(W), pltpu.VMEM((W, W), BF16), pltpu.VMEM((FF, W), BF16),
        pltpu.VMEM((W, W), BF16), pltpu.VMEM((W, W), BF16),
        pltpu.SemaphoreType.DMA((len(LATER),)),
        *Exchange.scratch(), *Exchange.scratch(),
    ]
    for n in BLOCKS:
        scratch += Summing.scratch(n)
    kept = pl.pallas_call(
        encoder_kernel,
        out_shape=[pltpu.VMEM((PROWS, W), BF16)]
        + [pltpu.VMEM((2, 16, n, 16, 128), BF16) for n in BLOCKS]
        + [pltpu.VMEM((6, W, W), BF16), pltpu.VMEM((W, FF), BF16), pltpu.VMEM((3, W), F32)],
        in_specs=[vmem] * 3 + [later] * 2 + [vmem] + [later] * 4 + [vmem] + [later] * 3 + [vmem]
        + [later] * 4,
        out_specs=[vmem] * 8,
        scratch_shapes=scratch,
        compiler_params=pltpu.CompilerParams(
            collective_id=1, has_side_effects=True, vmem_limit_bytes=VMEM_LIMIT
        ),
        name="encoder",
    )(
        item_tokens, owner_index.reshape(1, TX), owner_row.reshape(1, TX),
        parent_tokens.reshape(PROWS, W), cotangent.reshape(PROWS, W),
        cgain, column_query, column_key, column_value, column_out,
        hgain, up_weight, down_weight, link_weight,
        pgain, parent_query, parent_key, parent_value, parent_out,
    )
    square = shape((W, W), F32)
    row = shape((1, W), F32)
    out = pl.pallas_call(
        unpack_kernel,
        out_shape=[
            shape((PROWS, W), BF16), row, square, square, square, square, row,
            shape((W, FF), F32), shape((FF, W), F32), square, row, square, square, square, square,
        ],
        in_specs=[vmem] * 8,
        out_specs=[later] * 15,
        scratch_shapes=[
            pltpu.VMEM((9, W, W), F32), pltpu.VMEM((W, FF), F32), pltpu.VMEM((FF, W), F32),
            pltpu.VMEM((3, 1, W), F32), pltpu.SemaphoreType.DMA((15,)),
        ],
        compiler_params=pltpu.CompilerParams(vmem_limit_bytes=UNPACK_LIMIT),
        name="unpack",
    )(*kept)
    out = [o.reshape(W) if o.shape == (1, W) else o for o in out]
    return (out[0].reshape(CUST, CTOK, W), *out[1:])


def solution(mesh):
    split, whole = P(("dp", "rep")), P()
    return jax.shard_map(
        body,
        mesh=mesh,
        in_specs=(split,) * 5 + (whole,) * 14,
        out_specs=(split,) + (whole,) * 14,
        check_vma=False,
    )
```

```python
import math

import jax
import jax.numpy as jnp
from jax import lax
from jax.experimental import pallas as pl
from jax.experimental.pallas import tpu as pltpu
from jax.sharding import PartitionSpec as P

MESH = pl.DeviceIdType.MESH
F32 = jnp.float32
BF16 = jnp.bfloat16
CHIPS = 32


def place():
    dp, rep = lax.axis_index("dp"), lax.axis_index("rep")
    z, x, core = lax.div(dp, 8), lax.rem(lax.div(dp, 2), 4), lax.rem(dp, 2)
    return dp, rep, z, core, rep * 4 + x


def core_peer(at):
    dp, rep, z, core, spot = at
    return (dp + 1 - 2 * core, rep)


def plane_peer(at, j):
    dp, rep, z, core, spot = at
    return (8 * z + 2 * lax.rem(j, 4) + core, lax.div(j, 4))


def z_peer(at, j):
    dp, rep, z, core, spot = at
    return (8 * j + lax.rem(dp, 8), rep)


def remote(src, dst, send, recv, peer):
    copy = pltpu.make_async_remote_copy(
        src_ref=src, dst_ref=dst, send_sem=send, recv_sem=recv, device_id=peer, device_id_type=MESH
    )
    copy.start()
    return copy


def wait_sent(at, like, sem):
    pltpu.make_async_remote_copy(
        src_ref=like, dst_ref=like, send_sem=sem, recv_sem=sem,
        device_id=core_peer(at), device_id_type=MESH,
    ).wait_send()


def wait_received(at, like, sem):
    pltpu.make_async_remote_copy(
        src_ref=like, dst_ref=like, send_sem=sem, recv_sem=sem,
        device_id=core_peer(at), device_id_type=MESH,
    ).wait_recv()


class Summing:
    def __init__(self, at, n, mine, total, scratch):
        self.at, self.n, self.mine, self.total = at, n, mine, total
        self.core_in, self.plane_out, self.plane_in, self.z_all, self.send, self.recv = scratch

    @staticmethod
    def scratch(n):
        return [
            pltpu.VMEM((16, n, 16, 128), BF16),
            pltpu.VMEM((16, n, 16, 128), BF16),
            pltpu.VMEM((15, n, 16, 128), BF16),
            pltpu.VMEM((8, n, 16, 128), BF16),
            pltpu.SemaphoreType.DMA((5,)),
            pltpu.SemaphoreType.DMA((20,)),
        ]

    def start(self):
        dp, rep, z, core, spot = self.at
        self.from_core = remote(
            self.mine.at[1 - core], self.core_in, self.send.at[0], self.recv.at[0], core_peer(self.at)
        )

    def scatter_plane(self):
        dp, rep, z, core, spot = self.at
        self.from_core.wait_recv()
        self.plane_out[...] = (
            self.mine[core].astype(F32) + self.core_in[...].astype(F32)
        ).astype(BF16)
        for d in range(1, 16):
            q = lax.rem(spot + d, 16)
            remote(
                self.plane_out.at[q], self.plane_in.at[d - 1], self.send.at[1], self.recv.at[1],
                plane_peer(self.at, q),
            )

    def scatter_z(self):
        dp, rep, z, core, spot = self.at
        wait_received(self.at, self.plane_in, self.recv.at[1])
        value = self.plane_out[spot].astype(F32)
        for i in range(15):
            value = value + self.plane_in[i].astype(F32)
        self.z_all[z] = value.astype(BF16)
        for d in range(1, 8):
            here = self.z_all.at[z]
            remote(here, here, self.send.at[2], self.recv.at[2], z_peer(self.at, lax.rem(z + d, 8)))

    def gather_plane(self):
        dp, rep, z, core, spot = self.at
        wait_received(self.at, self.z_all.at[pl.ds(0, 7)], self.recv.at[2])
        value = self.z_all[0].astype(F32)
        for i in range(1, 8):
            value = value + self.z_all[i].astype(F32)
        self.total[core, spot] = value.astype(BF16)
        here = self.total.at[core, spot]
        self.from_plane = [
            remote(
                here, here, self.send.at[3], self.recv.at[3 + d],
                plane_peer(self.at, lax.rem(spot + d, 16)),
            )
            for d in range(1, 16)
        ]
        remote(here, here, self.send.at[4], self.recv.at[3], core_peer(self.at))

    def gather_core(self):
        dp, rep, z, core, spot = self.at
        for d, copy in zip(range(1, 16), self.from_plane, strict=True):
            copy.wait_recv()
            here = self.total.at[core, lax.rem(spot + 16 - d, 16)]
            remote(here, here, self.send.at[4], self.recv.at[3], core_peer(self.at))

    def finish(self):
        dp, rep, z, core, spot = self.at
        wait_received(self.at, self.total.at[1 - core], self.recv.at[3])
        self.from_core.wait_send()
        wait_sent(self.at, self.plane_in, self.send.at[1])
        wait_sent(self.at, self.z_all.at[pl.ds(0, 7)], self.send.at[2])
        wait_sent(self.at, self.total.at[core, pl.ds(0, 15)], self.send.at[3])
        wait_sent(self.at, self.total.at[core], self.send.at[4])


class Exchange:
    def __init__(self, at, scratch):
        self.at = at
        self.wide, self.out, self.near, self.far, self.send, self.recv = scratch

    @staticmethod
    def scratch():
        return [
            pltpu.VMEM((CHIPS, 16, 128), F32),
            pltpu.VMEM((CHIPS, 16, 128), BF16),
            pltpu.VMEM((CHIPS, 16, 128), BF16),
            pltpu.VMEM((CHIPS, 16, 128), BF16),
            pltpu.SemaphoreType.DMA((2,)),
            pltpu.SemaphoreType.DMA((2,)),
        ]

    def put(self, p, value, extra=None):
        self.wide[:, 2 * p, :] = value[:, :128]
        self.wide[:, 2 * p + 1, :] = value[:, 128:]
        self.wide[:, 8 + p, :] = jnp.zeros((CHIPS, 128), F32) if extra is None else extra
        self.wide[:, 12 + p, :] = jnp.zeros((CHIPS, 128), F32)

    def start(self):
        dp, rep, z, core, spot = self.at
        chip = lax.div(dp, 2)
        self.out[...] = self.wide[...].astype(BF16)
        self.near[chip] = self.out[chip]

        def to(d):
            j = lax.rem(chip + d, CHIPS)
            remote(
                self.out.at[j], self.near.at[chip], self.send.at[0], self.recv.at[0],
                (2 * j + core, rep),
            )

        to(CHIPS // 2)
        for d in range(1, CHIPS // 2):
            to(CHIPS // 2 - d)
            to(CHIPS // 2 + d)

    def wait(self):
        rest = self.near.at[pl.ds(0, CHIPS - 1)]
        wait_received(self.at, rest, self.recv.at[0])
        self.across = remote(
            self.near, self.far, self.send.at[1], self.recv.at[1], core_peer(self.at)
        )

    def wait_far(self):
        self.across.wait_recv()

    def finish(self):
        wait_sent(self.at, self.near.at[pl.ds(0, CHIPS - 1)], self.send.at[0])
        self.across.wait_send()

    def rows(self, source):
        dp, rep, z, core, spot = self.at
        wide = self.wide
        wide[...] = source[...].astype(F32)
        mine = lambda r, step: jnp.where(core == 0, wide[:, r, :], wide[:, r + step, :])
        return [
            (
                jnp.concatenate([mine(2 * slot, 4), mine(2 * slot + 1, 4)], axis=1).astype(BF16),
                mine(8 + slot, 2),
            )
            for slot in range(2)
        ]


def greet_all(at, barrier):
    dp, rep, z, core, spot = at
    chip = lax.div(dp, 2)
    peers = [(2 * lax.rem(chip + d, CHIPS) + core, rep) for d in range(1, CHIPS)]
    peers += [core_peer(at)]
    peers += [(8 * z + 2 * x + core, lax.rem(rep + d, 4)) for d in range(1, 4) for x in range(4)]
    for peer in peers:
        pl.semaphore_signal(barrier, inc=1, device_id=peer, device_id_type=MESH)
    return len(peers)


VMEM_LIMIT = 56 * 1024 * 1024
UNPACK_LIMIT = 50 * 1024 * 1024
EPSILON = 1e-06
ROOT = math.sqrt(2.0 / math.pi)
HEADS = 8
W = 256
HEAD = 32
FF = 1024
TX, COLS = 24, 24
CUST, CTOK = 16, 32
ROWS = TX * COLS
PROWS = CUST * CTOK
GROUP = 4
GROWS = GROUP * COLS
GPROWS = GROUP * CTOK
GROUPS = TX // GROUP
PGROUPS = CUST // GROUP


def dot(a, b):
    return lax.dot_general(a, b, (((1,), (0,)), ((), ())), preferred_element_type=F32)


def dot_nt(a, b):
    return lax.dot_general(a, b, (((1,), (1,)), ((), ())), preferred_element_type=F32)


def dot_tn(a, b):
    return lax.dot_general(a, b, (((0,), (0,)), ((), ())), preferred_element_type=F32)


def each(count, step, body):
    for i in range(count):
        body(slice(i * step, (i + 1) * step), i)


def head_masks():
    lane = lax.broadcasted_iota(jnp.int32, (1, W), 1)
    return [jnp.where(lax.div(lane, HEAD) == h, 1.0, 0.0) for h in range(HEADS)]


def spread_heads(value, masks):
    return jnp.concatenate([value * mask.astype(BF16) for mask in masks], axis=0)


def join_heads(value, masks, rows):
    total = value[:rows] * masks[0]
    for h in range(1, HEADS):
        total = total + value[h * rows : (h + 1) * rows] * masks[h]
    return total


def same_owner(rows, length):
    i = lax.div(lax.broadcasted_iota(jnp.int32, (rows, rows), 0), length)
    j = lax.div(lax.broadcasted_iota(jnp.int32, (rows, rows), 1), length)
    return jnp.concatenate([jnp.where(i == j, 0.0, -1e30)] * HEADS, axis=0)


def attend(q, k, v, probs, mix, groups, rows, length):
    masks = head_masks()
    bias = same_owner(rows, length)
    for i in range(groups):
        at = slice(i * rows, (i + 1) * rows)
        wide = spread_heads(q[at], masks)
        scores = dot_nt(wide, k[at]) * HEAD**-0.5 + bias
        e = jnp.exp(scores - jnp.max(scores, axis=1, keepdims=True))
        p = (e * (1.0 / jnp.sum(e, axis=1, keepdims=True))).astype(BF16)
        probs[i] = p
        mix[at] = join_heads(dot(p, v[at]), masks, rows).astype(BF16)


def attend_back(q, k, v, probs, dmix, dqkv, groups, rows, meanwhile=None):
    masks = head_masks()
    for i in range(groups):
        at = slice(i * rows, (i + 1) * rows)
        p = probs[i]
        wide_d = spread_heads(dmix[at], masks)
        wide_q = spread_heads(q[at], masks)
        weighted = p.astype(F32)
        ds = weighted * dot_nt(wide_d, v[at])
        ds = ds - weighted * jnp.sum(ds, axis=1, keepdims=True)
        ds = (ds * HEAD**-0.5).astype(BF16)
        dqkv[at, 0:W] = join_heads(dot(ds, k[at]), masks, rows).astype(BF16)
        dqkv[at, W : 2 * W] = dot_tn(ds, wide_q).astype(BF16)
        dqkv[at, 2 * W : 3 * W] = dot_tn(p, wide_d).astype(BF16)
        if meanwhile is not None:
            meanwhile(i)


def put_block(mine, b, value):
    for half in range(2):
        part = value[:, half * 128 : (half + 1) * 128].astype(BF16)
        mine[half, :, b] = part.reshape(16, 16, 128)


def rms_scale(value):
    return lax.rsqrt(jnp.mean(value * value, axis=1, keepdims=True) + EPSILON)


def averaging():
    t = lax.broadcasted_iota(jnp.int32, (TX, ROWS), 0)
    r = lax.div(lax.broadcasted_iota(jnp.int32, (TX, ROWS), 1), COLS)
    return jnp.where(t == r, 1.0, 0.0).astype(BF16)


def placing(owner_ref):
    owner = owner_ref[...]
    i = lax.broadcasted_iota(jnp.int32, (TX, TX), 0)
    j = lax.broadcasted_iota(jnp.int32, (TX, TX), 1)
    along = jnp.broadcast_to(owner, (TX, TX))
    down = jnp.sum(jnp.where(i == j, along, 0), axis=1, keepdims=True)
    slot = jnp.sum(jnp.where((down == along) & (i < j), 1, 0), axis=0, keepdims=True)
    chip = lax.broadcasted_iota(jnp.int32, (CHIPS, TX), 0)
    owner = jnp.broadcast_to(owner, (CHIPS, TX))
    slot = jnp.broadcast_to(slot, (CHIPS, TX))
    return [
        jnp.where((owner == 2 * chip + core) & (slot == s), 1.0, 0.0).astype(BF16)
        for core in range(2)
        for s in range(2)
    ]


BLOCKS = (5, 4, 5, 3)
LATER = ("cq", "ck", "cv", "parent", "cot", "co", "up", "down", "link", "pq", "pk", "pv", "po")


def encoder_kernel(
    item_ref, owner_ref, row_ref, parent_any, cot_any,
    cgain, cq_any, ck_any, cv_any, co_any, hgain, up_any, down_any, link_any, pgain, pq_any, pk_any, pv_any, po_any,
    states_ref, parent_sum, down_sum, up_sum, att_sum, kept, up, gains,
    n1, q, k, v, probs, mix, s_, n2, u, h, slope, dhidden, da, dmix, dqkv, hmean,
    pbased, pn, pq_, pk_, pv_, pprobs, pmix, pda, pdmix, pdqkv, pdn,
    parent_mine, down_mine, up_mine, att_mine,
    parent_ref, cot_ref, co, down, link, po, load_sem,
    *comm_scratch,
):
    cq, ck, cv, pq, pk, pv = (kept.at[i] for i in range(6))
    loads = {}
    for i, (name, source, target) in enumerate(
        zip(
            LATER,
            (
                cq_any, ck_any, cv_any, parent_any, cot_any, co_any, up_any, down_any, link_any,
                pq_any, pk_any, pv_any, po_any,
            ),
            (cq, ck, cv, parent_ref, cot_ref, co, up, down, link, pq, pk, pv, po),
            strict=True,
        )
    ):
        loads[name] = pltpu.make_async_copy(source, target, load_sem.at[i])
    for name in ("cq", "ck", "cv", "co", "up", "down", "cot", "po", "parent", "link", "pq", "pk", "pv"):
        loads[name].start()
    at = place()
    barrier = pltpu.get_barrier_semaphore()
    greeted = greet_all(at, barrier)
    jobs = zip(
        BLOCKS,
        (parent_mine, down_mine, up_mine, att_mine),
        (parent_sum, down_sum, up_sum, att_sum),
        strict=True,
    )
    there = Exchange(at, comm_scratch[:6])
    back = Exchange(at, comm_scratch[6:12])
    job_scratch = comm_scratch[12:]
    per = len(job_scratch) // 4
    parent_job, down_job, up_job, att_job = [
        Summing(at, *job, job_scratch[i * per : (i + 1) * per]) for i, job in enumerate(jobs)
    ]

    def norm_items(rows, i):
        x = item_ref[i * GROUP : (i + 1) * GROUP].astype(F32).reshape(GROWS, W)
        n1[rows] = (x * rms_scale(x) * cgain[...].astype(F32)[None, :]).astype(BF16)

    each(GROUPS, GROWS, norm_items)
    for i, gain in enumerate((cgain, pgain, hgain)):
        gains[i : i + 1] = gain[...].astype(F32)[None, :]
    for name in ("cq", "ck", "cv"):
        loads[name].wait()
    q[...] = dot(n1[...], cq[...]).astype(BF16)
    k[...] = dot(n1[...], ck[...]).astype(BF16)
    v[...] = dot(n1[...], cv[...]).astype(BF16)
    attend(q, k, v, probs, mix, GROUPS, GROWS, COLS)
    loads["co"].wait()
    u[:, :W] = dot(mix[...], co[...])

    def norm_stream(rows, i):
        x = item_ref[i * GROUP : (i + 1) * GROUP].astype(F32).reshape(GROWS, W)
        stream = (x + u[rows, :W]).astype(BF16)
        s_[rows] = stream
        stream = stream.astype(F32)
        n2[rows] = (stream * rms_scale(stream) * hgain[...].astype(F32)[None, :]).astype(BF16)

    each(GROUPS, GROWS, norm_stream)
    loads["up"].wait()
    u[...] = dot(n2[...], up[...])

    def gelu(rows, i):
        for c in range(0, FF, 256):
            value = u[rows, c : c + 256]
            t = jnp.tanh(value * (ROOT + ROOT * 0.044715 * (value * value)))
            h[rows, c : c + 256] = (value * (0.5 + 0.5 * t)).astype(BF16)

    each(ROWS // 32, 32, gelu)
    average = averaging()
    hidden = (dot(average, h[...]) * (1.0 / COLS)).astype(BF16)
    hmean[...] = hidden
    loads["down"].wait()
    embedding = (dot(average, s_[...]) * (1.0 / COLS) + dot(hidden, down[...])).astype(BF16)

    places = placing(owner_ref)
    ids = jnp.broadcast_to(row_ref[...].astype(F32) + 1.0, (128, TX)).astype(BF16)
    for p in range(4):
        there.put(p, dot(places[p], embedding), dot_nt(places[p], ids))
    pl.semaphore_wait(barrier, greeted)
    there.start()

    def gelu_slope(rows, i):
        for c in range(0, FF, 256):
            value = u[rows, c : c + 256]
            square = value * value
            t = jnp.tanh(value * (ROOT + ROOT * 0.044715 * square))
            inner = value * (ROOT + 3 * ROOT * 0.044715 * square)
            half = 0.5 + 0.5 * t
            slope[rows, c : c + 256] = (half + 0.5 * (1.0 - t * t) * inner).astype(BF16)

    each(ROWS // 32, 32, gelu_slope)
    loads["cot"].wait()
    loads["po"].wait()
    scale = 1.0 / math.sqrt(CUST * CTOK * 256)
    pda[...] = (cot_ref[...].astype(F32) * scale).astype(BF16)
    pdmix[...] = dot_nt(pda[...], po[...]).astype(BF16)
    for name in ("parent", "link", "pq", "pk", "pv"):
        loads[name].wait()
    there.wait()

    members = []
    customer = lax.broadcasted_iota(jnp.int32, (CHIPS, CUST), 1).astype(F32) + 1.0
    counts, sums = jnp.zeros((CUST, W), F32), jnp.zeros((CUST, W), F32)
    for source in (there.near, there.far):
        if source is there.far:
            there.wait_far()
        for got, name in there.rows(source):
            member = jnp.where(name[:, :CUST] == customer, 1.0, 0.0).astype(BF16)
            members.append(member)
            counts = counts + dot_tn(member, jnp.ones((CHIPS, W), BF16))
            sums = sums + dot_tn(member, got)
    divisor = jnp.maximum(counts, 1.0)
    pooled = (sums / divisor).astype(BF16)
    linked = dot(pooled, link[...])
    pbased_value = (
        (parent_ref[...].astype(F32).reshape(CUST, CTOK, W) + linked[:, None, :])
        .astype(BF16)
        .reshape(PROWS, W)
    )
    pbased[...] = pbased_value

    def norm_based(rows, i):
        x = pbased[rows].astype(F32)
        pn[rows] = (x * rms_scale(x) * pgain[...].astype(F32)[None, :]).astype(BF16)

    each(PGROUPS, GPROWS, norm_based)
    pq_[...] = dot(pn[...], pq[...]).astype(BF16)
    pk_[...] = dot(pn[...], pk[...]).astype(BF16)
    pv_[...] = dot(pn[...], pv[...]).astype(BF16)
    attend(pq_, pk_, pv_, pprobs, pmix, PGROUPS, GPROWS, CTOK)
    attend_back(pq_, pk_, pv_, pprobs, pdmix, pdqkv, PGROUPS, GPROWS)
    pdn[...] = (
        dot_nt(pdqkv[:, :W], pq[...])
        + dot_nt(pdqkv[:, W : 2 * W], pk[...])
        + dot_nt(pdqkv[:, 2 * W :], pv[...])
    )

    dlinked = []
    for i in range(PGROUPS):
        rows = slice(i * GPROWS, (i + 1) * GPROWS)
        x = pbased[rows].astype(F32)
        r = rms_scale(x)
        unit = x * r
        dunit = pdn[rows] * pgain[...].astype(F32)[None, :]
        dx = r * (dunit - unit * jnp.mean(dunit * unit, axis=1, keepdims=True))
        dx = dx + cot_ref[rows].astype(F32) * scale
        dlinked.append(jnp.sum(dx.reshape(GROUP, CTOK, W), axis=1))
    dlinked = jnp.concatenate(dlinked, axis=0)
    dpooled = dot_nt(dlinked.astype(BF16), link[...]).astype(BF16).astype(F32)
    sum_grad = (dpooled / divisor).astype(BF16)
    core = at[3]
    moved = [dot(member, sum_grad) for member in members]
    for p in range(4):
        home, slot = p // 2, p % 2
        back.put(p, jnp.where(core == home, moved[slot], moved[2 + slot]))
    back.start()

    put_block(parent_mine, 0, dot_tn(pooled, dlinked.astype(BF16)))
    dweights = dot_tn(pn[...], pdqkv[...])
    for b in range(3):
        put_block(parent_mine, 1 + b, dweights[:, b * W : (b + 1) * W])
    put_block(parent_mine, 4, dot_tn(pmix[...], pda[...]))
    parent_job.start()
    states_ref[...] = (pbased[...].astype(F32) + dot(pmix[...], po[...])).astype(BF16)
    parent_job.scatter_plane()
    back.wait()

    ditem = jnp.zeros((TX, W), F32)
    near = back.rows(back.near)
    back.wait_far()
    far = back.rows(back.far)
    for p in range(4):
        home, slot = p // 2, p % 2
        got = jnp.where(core == home, near[slot][0].astype(F32), far[slot][0].astype(F32))
        ditem = ditem + dot_tn(places[p], got.astype(BF16))
    ditem_b = ditem.astype(BF16)
    ddown = dot_tn(hmean[...], ditem_b)
    for b in range(4):
        put_block(down_mine, b, ddown[b * W : (b + 1) * W])
    down_job.start()
    dhidden[...] = (dot_nt(ditem_b, down[...]) * (1.0 / COLS)).astype(BF16).astype(F32)
    dy = dot_tn(averaging(), ditem_b)

    def back_hidden(rows, i):
        spread = jnp.concatenate(
            [jnp.broadcast_to(dhidden[t : t + 1], (COLS, FF)) for t in (2 * i, 2 * i + 1)], axis=0
        )
        h[rows] = (spread * slope[rows].astype(F32)).astype(BF16)

    each(TX // 2, 2 * COLS, back_hidden)
    dup = dot_tn(n2[...], h[...])
    for b in range(4):
        put_block(up_mine, b, dup[:, b * W : (b + 1) * W])
    u[:, :W] = dot_nt(h[...], up[...])
    u[:, W : 2 * W] = dy
    parent_job.scatter_z()
    down_job.scatter_plane()

    def back_stream(rows, i):
        x = s_[rows].astype(F32)
        r = rms_scale(x)
        unit = x * r
        dunit = u[rows, :W].astype(BF16).astype(F32) * hgain[...].astype(F32)[None, :]
        dx = r * (dunit - unit * jnp.mean(dunit * unit, axis=1, keepdims=True))
        da[rows] = (dx + u[rows, W : 2 * W] * (1.0 / COLS)).astype(BF16)

    each(GROUPS, GROWS, back_stream)
    put_block(up_mine, 4, dot_tn(mix[...], da[...]))
    up_job.start()
    dmix[...] = dot_nt(da[...], co[...]).astype(BF16)
    meanwhile = {1: up_job.scatter_plane, 5: down_job.scatter_z}
    attend_back(q, k, v, probs, dmix, dqkv, GROUPS, GROWS, lambda i: meanwhile.get(i, int)())
    dweights = dot_tn(n1[...], dqkv[...])
    for b in range(3):
        put_block(att_mine, b, dweights[:, b * W : (b + 1) * W])
    att_job.start()

    att_job.scatter_plane()
    parent_job.gather_plane()
    up_job.scatter_z()
    att_job.scatter_z()
    down_job.gather_plane()
    up_job.gather_plane()
    parent_job.gather_core()
    down_job.gather_core()
    att_job.gather_plane()
    up_job.gather_core()
    att_job.gather_core()
    for job in (there, back, parent_job, down_job, up_job, att_job):
        job.finish()


def gain_row(weights, sums, gain):
    total = jnp.zeros((W, W), F32)
    for weight, value in zip(weights, sums, strict=True):
        total = total + weight.astype(F32) * value
    high = total.astype(BF16)
    low = (total - high.astype(F32)).astype(BF16)
    ones = jnp.ones((8, W), BF16)
    return (dot_nt(ones, high) + dot_nt(ones, low))[:1] / gain


def unpack_kernel(
    states_in, parent_sum, down_sum, up_sum, att_sum, kept, up, gains,
    states, dcg, dcq, dck, dcv, dco, dhg, dup, ddown, dlink, dpg, dpq, dpk, dpv, dpo,
    stage, wide_stage, tall_stage, gain_stage, store_sem,
):
    def block(total, b):
        return jnp.concatenate(
            [total[half, :, b].astype(F32).reshape(W, 128) for half in range(2)], axis=1
        )

    copies = []

    def store(source, target):
        copies.append(pltpu.make_async_copy(source, target, store_sem.at[len(copies)]))
        copies[-1].start()

    store(states_in, states)
    for b in range(4):
        tall_stage[b * W : (b + 1) * W] = block(down_sum, b)
    store(tall_stage, ddown)
    for b in range(4):
        wide_stage[:, b * W : (b + 1) * W] = block(up_sum, b)
    store(wide_stage, dup)
    squares = [(att_sum, b, ref) for b, ref in enumerate((dcq, dck, dcv))]
    squares += [(parent_sum, b, ref) for b, ref in enumerate((dlink, dpq, dpk, dpv, dpo))]
    squares += [(up_sum, 4, dco)]
    for i, (total, b, ref) in enumerate(squares):
        stage[i] = block(total, b)
        store(stage.at[i], ref)
    for i in range(2):
        grads = [stage[j] for j in ((0, 1, 2), (4, 5, 6))[i]]
        gain_stage[i] = gain_row([kept[3 * i + j] for j in range(3)], grads, gains[i : i + 1])
    cuts = [slice(b * W, (b + 1) * W) for b in range(4)]
    gain_stage[2] = gain_row(
        [up[:, c] for c in cuts], [wide_stage[:, c] for c in cuts], gains[2:3]
    )
    for i, ref in enumerate((dcg, dpg, dhg)):
        store(gain_stage.at[i], ref)
    for done in copies:
        done.wait()


def body(
    item_tokens, owner_index, owner_row, parent_tokens, cotangent,
    column_gain, column_query, column_key, column_value, column_out,
    hidden_gain, up_weight, down_weight, link_weight,
    parent_gain, parent_query, parent_key, parent_value, parent_out,
):
    vmem = pl.BlockSpec(memory_space=pltpu.VMEM)
    later = pl.BlockSpec(memory_space=pl.ANY)
    shape = jax.ShapeDtypeStruct
    cgain, hgain, pgain = column_gain, hidden_gain, parent_gain
    items = lambda width, dtype=BF16: pltpu.VMEM((ROWS, width), dtype)
    parents = lambda width, dtype=BF16: pltpu.VMEM((PROWS, width), dtype)
    scratch = [
        items(W), items(W), items(W), items(W),
        pltpu.VMEM((GROUPS, HEADS * GROWS, GROWS), BF16),
        items(W), items(W), items(W), items(FF, F32), items(FF), items(FF),
        pltpu.VMEM((TX, FF), F32), items(W), items(W), items(3 * W),
        pltpu.VMEM((TX, FF), BF16),
        parents(W), parents(W), parents(W), parents(W), parents(W),
        pltpu.VMEM((PGROUPS, HEADS * GPROWS, GPROWS), BF16),
        parents(W), parents(W), parents(W), parents(3 * W), parents(W, F32),
        *[pltpu.VMEM((2, 16, n, 16, 128), BF16) for n in BLOCKS],
        parents(W), parents(W), pltpu.VMEM((W, W), BF16), pltpu.VMEM((FF, W), BF16),
        pltpu.VMEM((W, W), BF16), pltpu.VMEM((W, W), BF16),
        pltpu.SemaphoreType.DMA((len(LATER),)),
        *Exchange.scratch(), *Exchange.scratch(),
    ]
    for n in BLOCKS:
        scratch += Summing.scratch(n)
    kept = pl.pallas_call(
        encoder_kernel,
        out_shape=[pltpu.VMEM((PROWS, W), BF16)]
        + [pltpu.VMEM((2, 16, n, 16, 128), BF16) for n in BLOCKS]
        + [pltpu.VMEM((6, W, W), BF16), pltpu.VMEM((W, FF), BF16), pltpu.VMEM((3, W), F32)],
        in_specs=[vmem] * 3 + [later] * 2 + [vmem] + [later] * 4 + [vmem] + [later] * 3 + [vmem]
        + [later] * 4,
        out_specs=[vmem] * 8,
        scratch_shapes=scratch,
        compiler_params=pltpu.CompilerParams(
            collective_id=1, has_side_effects=True, vmem_limit_bytes=VMEM_LIMIT
        ),
        name="encoder",
    )(
        item_tokens, owner_index.reshape(1, TX), owner_row.reshape(1, TX),
        parent_tokens.reshape(PROWS, W), cotangent.reshape(PROWS, W),
        cgain, column_query, column_key, column_value, column_out,
        hgain, up_weight, down_weight, link_weight,
        pgain, parent_query, parent_key, parent_value, parent_out,
    )
    square = shape((W, W), F32)
    row = shape((1, W), F32)
    out = pl.pallas_call(
        unpack_kernel,
        out_shape=[
            shape((PROWS, W), BF16), row, square, square, square, square, row,
            shape((W, FF), F32), shape((FF, W), F32), square, row, square, square, square, square,
        ],
        in_specs=[vmem] * 8,
        out_specs=[later] * 15,
        scratch_shapes=[
            pltpu.VMEM((9, W, W), F32), pltpu.VMEM((W, FF), F32), pltpu.VMEM((FF, W), F32),
            pltpu.VMEM((3, 1, W), F32), pltpu.SemaphoreType.DMA((15,)),
        ],
        compiler_params=pltpu.CompilerParams(vmem_limit_bytes=UNPACK_LIMIT),
        name="unpack",
    )(*kept)
    out = [o.reshape(W) if o.shape == (1, W) else o for o in out]
    return (out[0].reshape(CUST, CTOK, W), *out[1:])


def solution(mesh):
    split, whole = P(("dp", "rep")), P()
    return jax.shard_map(
        body,
        mesh=mesh,
        in_specs=(split,) * 5 + (whole,) * 14,
        out_specs=(split,) + (whole,) * 14,
        check_vma=False,
    )
```

```python
import math

import jax
import jax.numpy as jnp
from jax import lax
from jax.experimental import pallas as pl
from jax.experimental.pallas import tpu as pltpu
from jax.sharding import PartitionSpec as P

MESH = pl.DeviceIdType.MESH
F32 = jnp.float32
BF16 = jnp.bfloat16
CHIPS = 32


def place():
    dp, rep = lax.axis_index("dp"), lax.axis_index("rep")
    z, x, core = lax.div(dp, 8), lax.rem(lax.div(dp, 2), 4), lax.rem(dp, 2)
    return dp, rep, z, core, rep * 4 + x


def core_peer(at):
    dp, rep, z, core, spot = at
    return (dp + 1 - 2 * core, rep)


def plane_peer(at, j):
    dp, rep, z, core, spot = at
    return (8 * z + 2 * lax.rem(j, 4) + core, lax.div(j, 4))


def z_peer(at, j):
    dp, rep, z, core, spot = at
    return (8 * j + lax.rem(dp, 8), rep)


def remote(src, dst, send, recv, peer):
    copy = pltpu.make_async_remote_copy(
        src_ref=src, dst_ref=dst, send_sem=send, recv_sem=recv, device_id=peer, device_id_type=MESH
    )
    copy.start()
    return copy


def wait_sent(at, like, sem):
    pltpu.make_async_remote_copy(
        src_ref=like, dst_ref=like, send_sem=sem, recv_sem=sem,
        device_id=core_peer(at), device_id_type=MESH,
    ).wait_send()


def wait_received(at, like, sem):
    pltpu.make_async_remote_copy(
        src_ref=like, dst_ref=like, send_sem=sem, recv_sem=sem,
        device_id=core_peer(at), device_id_type=MESH,
    ).wait_recv()


class Summing:
    def __init__(self, at, n, mine, total, scratch):
        self.at, self.n, self.mine, self.total = at, n, mine, total
        self.core_in, self.plane_out, self.plane_in, self.z_all, self.send, self.recv = scratch

    @staticmethod
    def scratch(n):
        return [
            pltpu.VMEM((16, n, 16, 128), BF16),
            pltpu.VMEM((16, n, 16, 128), BF16),
            pltpu.VMEM((15, n, 16, 128), BF16),
            pltpu.VMEM((8, n, 16, 128), BF16),
            pltpu.SemaphoreType.DMA((5,)),
            pltpu.SemaphoreType.DMA((20,)),
        ]

    def start(self):
        dp, rep, z, core, spot = self.at
        self.from_core = remote(
            self.mine.at[1 - core], self.core_in, self.send.at[0], self.recv.at[0], core_peer(self.at)
        )

    def scatter_plane(self):
        dp, rep, z, core, spot = self.at
        self.from_core.wait_recv()
        self.plane_out[...] = (
            self.mine[core].astype(F32) + self.core_in[...].astype(F32)
        ).astype(BF16)
        for d in range(1, 16):
            q = lax.rem(spot + d, 16)
            remote(
                self.plane_out.at[q], self.plane_in.at[d - 1], self.send.at[1], self.recv.at[1],
                plane_peer(self.at, q),
            )

    def scatter_z(self):
        dp, rep, z, core, spot = self.at
        wait_received(self.at, self.plane_in, self.recv.at[1])
        value = self.plane_out[spot].astype(F32)
        for i in range(15):
            value = value + self.plane_in[i].astype(F32)
        self.z_all[z] = value.astype(BF16)
        for d in range(1, 8):
            here = self.z_all.at[z]
            remote(here, here, self.send.at[2], self.recv.at[2], z_peer(self.at, lax.rem(z + d, 8)))

    def gather_plane(self):
        dp, rep, z, core, spot = self.at
        wait_received(self.at, self.z_all.at[pl.ds(0, 7)], self.recv.at[2])
        value = self.z_all[0].astype(F32)
        for i in range(1, 8):
            value = value + self.z_all[i].astype(F32)
        self.total[core, spot] = value.astype(BF16)
        here = self.total.at[core, spot]
        self.from_plane = [
            remote(
                here, here, self.send.at[3], self.recv.at[3 + d],
                plane_peer(self.at, lax.rem(spot + d, 16)),
            )
            for d in range(1, 16)
        ]
        remote(here, here, self.send.at[4], self.recv.at[3], core_peer(self.at))

    def gather_core(self):
        dp, rep, z, core, spot = self.at
        for d, copy in zip(range(1, 16), self.from_plane, strict=True):
            copy.wait_recv()
            here = self.total.at[core, lax.rem(spot + 16 - d, 16)]
            remote(here, here, self.send.at[4], self.recv.at[3], core_peer(self.at))

    def finish(self):
        dp, rep, z, core, spot = self.at
        wait_received(self.at, self.total.at[1 - core], self.recv.at[3])
        self.from_core.wait_send()
        wait_sent(self.at, self.plane_in, self.send.at[1])
        wait_sent(self.at, self.z_all.at[pl.ds(0, 7)], self.send.at[2])
        wait_sent(self.at, self.total.at[core, pl.ds(0, 15)], self.send.at[3])
        wait_sent(self.at, self.total.at[core], self.send.at[4])


class Exchange:
    def __init__(self, at, scratch):
        self.at = at
        self.wide, self.out, self.near, self.far, self.send, self.recv = scratch

    @staticmethod
    def scratch():
        return [
            pltpu.VMEM((CHIPS, 16, 128), F32),
            pltpu.VMEM((CHIPS, 16, 128), BF16),
            pltpu.VMEM((CHIPS, 16, 128), BF16),
            pltpu.VMEM((CHIPS, 16, 128), BF16),
            pltpu.SemaphoreType.DMA((2,)),
            pltpu.SemaphoreType.DMA((2,)),
        ]

    def put(self, p, value, extra=None):
        self.wide[:, 2 * p, :] = value[:, :128]
        self.wide[:, 2 * p + 1, :] = value[:, 128:]
        self.wide[:, 8 + p, :] = jnp.zeros((CHIPS, 128), F32) if extra is None else extra
        self.wide[:, 12 + p, :] = jnp.zeros((CHIPS, 128), F32)

    def start(self):
        dp, rep, z, core, spot = self.at
        chip = lax.div(dp, 2)
        self.out[...] = self.wide[...].astype(BF16)
        self.near[chip] = self.out[chip]

        def to(d):
            j = lax.rem(chip + d, CHIPS)
            remote(
                self.out.at[j], self.near.at[chip], self.send.at[0], self.recv.at[0],
                (2 * j + core, rep),
            )

        to(CHIPS // 2)
        for d in range(1, CHIPS // 2):
            to(CHIPS // 2 - d)
            to(CHIPS // 2 + d)

    def wait(self):
        rest = self.near.at[pl.ds(0, CHIPS - 1)]
        wait_received(self.at, rest, self.recv.at[0])
        self.across = remote(
            self.near, self.far, self.send.at[1], self.recv.at[1], core_peer(self.at)
        )

    def wait_far(self):
        self.across.wait_recv()

    def finish(self):
        wait_sent(self.at, self.near.at[pl.ds(0, CHIPS - 1)], self.send.at[0])
        self.across.wait_send()

    def rows(self, source):
        dp, rep, z, core, spot = self.at
        wide = self.wide
        wide[...] = source[...].astype(F32)
        mine = lambda r, step: jnp.where(core == 0, wide[:, r, :], wide[:, r + step, :])
        return [
            (
                jnp.concatenate([mine(2 * slot, 4), mine(2 * slot + 1, 4)], axis=1).astype(BF16),
                mine(8 + slot, 2),
            )
            for slot in range(2)
        ]


def greet_all(at, barrier):
    dp, rep, z, core, spot = at
    chip = lax.div(dp, 2)
    peers = [(2 * lax.rem(chip + d, CHIPS) + core, rep) for d in range(1, CHIPS)]
    peers += [core_peer(at)]
    peers += [(8 * z + 2 * x + core, lax.rem(rep + d, 4)) for d in range(1, 4) for x in range(4)]
    for peer in peers:
        pl.semaphore_signal(barrier, inc=1, device_id=peer, device_id_type=MESH)
    return len(peers)


VMEM_LIMIT = 56 * 1024 * 1024
UNPACK_LIMIT = 50 * 1024 * 1024
EPSILON = 1e-06
ROOT = math.sqrt(2.0 / math.pi)
HEADS = 8
W = 256
HEAD = 32
FF = 1024
TX, COLS = 24, 24
CUST, CTOK = 16, 32
ROWS = TX * COLS
PROWS = CUST * CTOK
GROUP = 4
GROWS = GROUP * COLS
GPROWS = GROUP * CTOK
GROUPS = TX // GROUP
PGROUPS = CUST // GROUP


def dot(a, b):
    return lax.dot_general(a, b, (((1,), (0,)), ((), ())), preferred_element_type=F32)


def dot_nt(a, b):
    return lax.dot_general(a, b, (((1,), (1,)), ((), ())), preferred_element_type=F32)


def dot_tn(a, b):
    return lax.dot_general(a, b, (((0,), (0,)), ((), ())), preferred_element_type=F32)


def each(count, step, body):
    for i in range(count):
        body(slice(i * step, (i + 1) * step), i)


def head_masks():
    lane = lax.broadcasted_iota(jnp.int32, (1, W), 1)
    return [jnp.where(lax.div(lane, HEAD) == h, 1.0, 0.0) for h in range(HEADS)]


def spread_heads(value, masks):
    return jnp.concatenate([value * mask.astype(BF16) for mask in masks], axis=0)


def join_heads(value, masks, rows):
    total = value[:rows] * masks[0]
    for h in range(1, HEADS):
        total = total + value[h * rows : (h + 1) * rows] * masks[h]
    return total


def same_owner(rows, length):
    i = lax.div(lax.broadcasted_iota(jnp.int32, (rows, rows), 0), length)
    j = lax.div(lax.broadcasted_iota(jnp.int32, (rows, rows), 1), length)
    return jnp.concatenate([jnp.where(i == j, 0.0, -1e30)] * HEADS, axis=0)


def attend(q, k, v, probs, mix, groups, rows, length):
    masks = head_masks()
    bias = same_owner(rows, length)
    for i in range(groups):
        at = slice(i * rows, (i + 1) * rows)
        wide = spread_heads(q[at], masks)
        scores = dot_nt(wide, k[at]) * HEAD**-0.5 + bias
        e = jnp.exp(scores - jnp.max(scores, axis=1, keepdims=True))
        p = (e * (1.0 / jnp.sum(e, axis=1, keepdims=True))).astype(BF16)
        probs[i] = p
        mix[at] = join_heads(dot(p, v[at]), masks, rows).astype(BF16)


def attend_back(q, k, v, probs, dmix, dqkv, groups, rows, meanwhile=None):
    masks = head_masks()
    for i in range(groups):
        at = slice(i * rows, (i + 1) * rows)
        p = probs[i]
        wide_d = spread_heads(dmix[at], masks)
        wide_q = spread_heads(q[at], masks)
        weighted = p.astype(F32)
        ds = weighted * dot_nt(wide_d, v[at])
        ds = ds - weighted * jnp.sum(ds, axis=1, keepdims=True)
        ds = (ds * HEAD**-0.5).astype(BF16)
        dqkv[at, 0:W] = join_heads(dot(ds, k[at]), masks, rows).astype(BF16)
        dqkv[at, W : 2 * W] = dot_tn(ds, wide_q).astype(BF16)
        dqkv[at, 2 * W : 3 * W] = dot_tn(p, wide_d).astype(BF16)
        if meanwhile is not None:
            meanwhile(i)


def put_block(mine, b, value):
    for half in range(2):
        part = value[:, half * 128 : (half + 1) * 128].astype(BF16)
        mine[half, :, b] = part.reshape(16, 16, 128)


def rms_scale(value):
    return lax.rsqrt(jnp.mean(value * value, axis=1, keepdims=True) + EPSILON)


def averaging():
    t = lax.broadcasted_iota(jnp.int32, (TX, ROWS), 0)
    r = lax.div(lax.broadcasted_iota(jnp.int32, (TX, ROWS), 1), COLS)
    return jnp.where(t == r, 1.0, 0.0).astype(BF16)


def placing(owner_ref):
    owner = owner_ref[...]
    i = lax.broadcasted_iota(jnp.int32, (TX, TX), 0)
    j = lax.broadcasted_iota(jnp.int32, (TX, TX), 1)
    along = jnp.broadcast_to(owner, (TX, TX))
    down = jnp.sum(jnp.where(i == j, along, 0), axis=1, keepdims=True)
    slot = jnp.sum(jnp.where((down == along) & (i < j), 1, 0), axis=0, keepdims=True)
    chip = lax.broadcasted_iota(jnp.int32, (CHIPS, TX), 0)
    owner = jnp.broadcast_to(owner, (CHIPS, TX))
    slot = jnp.broadcast_to(slot, (CHIPS, TX))
    return [
        jnp.where((owner == 2 * chip + core) & (slot == s), 1.0, 0.0).astype(BF16)
        for core in range(2)
        for s in range(2)
    ]


BLOCKS = (5, 4, 5, 3)
LATER = ("item", "cq", "ck", "cv", "parent", "cot", "co", "up", "down", "link", "pq", "pk", "pv", "po")


def encoder_kernel(
    item_any, owner_ref, row_ref, parent_any, cot_any,
    cgain, cq_any, ck_any, cv_any, co_any, hgain, up_any, down_any, link_any, pgain, pq_any, pk_any, pv_any, po_any,
    states_ref, parent_sum, down_sum, up_sum, att_sum, kept, up, gains,
    n1, q, k, v, probs, mix, s_, n2, u, h, slope, dhidden, da, dmix, dqkv, hmean,
    pbased, pn, pq_, pk_, pv_, pprobs, pmix, pda, pdmix, pdqkv, pdn,
    parent_mine, down_mine, up_mine, att_mine,
    item_ref, parent_ref, cot_ref, co, down, link, po, load_sem,
    *comm_scratch,
):
    cq, ck, cv, pq, pk, pv = (kept.at[i] for i in range(6))
    loads = {}
    for i, (name, source, target) in enumerate(
        zip(
            LATER,
            (
                item_any, cq_any, ck_any, cv_any, parent_any, cot_any, co_any, up_any, down_any, link_any,
                pq_any, pk_any, pv_any, po_any,
            ),
            (item_ref, cq, ck, cv, parent_ref, cot_ref, co, up, down, link, pq, pk, pv, po),
            strict=True,
        )
    ):
        loads[name] = pltpu.make_async_copy(source, target, load_sem.at[i])
    for name in ("item", "cq", "ck", "cv", "co", "up", "down", "cot", "po", "parent", "link", "pq", "pk", "pv"):
        loads[name].start()
    at = place()
    barrier = pltpu.get_barrier_semaphore()
    greeted = greet_all(at, barrier)
    jobs = zip(
        BLOCKS,
        (parent_mine, down_mine, up_mine, att_mine),
        (parent_sum, down_sum, up_sum, att_sum),
        strict=True,
    )
    there = Exchange(at, comm_scratch[:6])
    back = Exchange(at, comm_scratch[6:12])
    job_scratch = comm_scratch[12:]
    per = len(job_scratch) // 4
    parent_job, down_job, up_job, att_job = [
        Summing(at, *job, job_scratch[i * per : (i + 1) * per]) for i, job in enumerate(jobs)
    ]

    loads["item"].wait()

    def norm_items(rows, i):
        x = item_ref[i * GROUP : (i + 1) * GROUP].astype(F32).reshape(GROWS, W)
        n1[rows] = (x * rms_scale(x) * cgain[...].astype(F32)[None, :]).astype(BF16)

    each(GROUPS, GROWS, norm_items)
    for i, gain in enumerate((cgain, pgain, hgain)):
        gains[i : i + 1] = gain[...].astype(F32)[None, :]
    for name in ("cq", "ck", "cv"):
        loads[name].wait()
    q[...] = dot(n1[...], cq[...]).astype(BF16)
    k[...] = dot(n1[...], ck[...]).astype(BF16)
    v[...] = dot(n1[...], cv[...]).astype(BF16)
    attend(q, k, v, probs, mix, GROUPS, GROWS, COLS)
    loads["co"].wait()
    u[:, :W] = dot(mix[...], co[...])

    def norm_stream(rows, i):
        x = item_ref[i * GROUP : (i + 1) * GROUP].astype(F32).reshape(GROWS, W)
        stream = (x + u[rows, :W]).astype(BF16)
        s_[rows] = stream
        stream = stream.astype(F32)
        n2[rows] = (stream * rms_scale(stream) * hgain[...].astype(F32)[None, :]).astype(BF16)

    each(GROUPS, GROWS, norm_stream)
    loads["up"].wait()
    u[...] = dot(n2[...], up[...])

    def gelu(rows, i):
        for c in range(0, FF, 256):
            value = u[rows, c : c + 256]
            t = jnp.tanh(value * (ROOT + ROOT * 0.044715 * (value * value)))
            h[rows, c : c + 256] = (value * (0.5 + 0.5 * t)).astype(BF16)

    each(ROWS // 32, 32, gelu)
    average = averaging()
    hidden = (dot(average, h[...]) * (1.0 / COLS)).astype(BF16)
    hmean[...] = hidden
    loads["down"].wait()
    embedding = (dot(average, s_[...]) * (1.0 / COLS) + dot(hidden, down[...])).astype(BF16)

    places = placing(owner_ref)
    ids = jnp.broadcast_to(row_ref[...].astype(F32) + 1.0, (128, TX)).astype(BF16)
    for p in range(4):
        there.put(p, dot(places[p], embedding), dot_nt(places[p], ids))
    pl.semaphore_wait(barrier, greeted)
    there.start()

    def gelu_slope(rows, i):
        for c in range(0, FF, 256):
            value = u[rows, c : c + 256]
            square = value * value
            t = jnp.tanh(value * (ROOT + ROOT * 0.044715 * square))
            inner = value * (ROOT + 3 * ROOT * 0.044715 * square)
            half = 0.5 + 0.5 * t
            slope[rows, c : c + 256] = (half + 0.5 * (1.0 - t * t) * inner).astype(BF16)

    each(ROWS // 32, 32, gelu_slope)
    loads["cot"].wait()
    loads["po"].wait()
    scale = 1.0 / math.sqrt(CUST * CTOK * 256)
    pda[...] = (cot_ref[...].astype(F32) * scale).astype(BF16)
    pdmix[...] = dot_nt(pda[...], po[...]).astype(BF16)
    for name in ("parent", "link", "pq", "pk", "pv"):
        loads[name].wait()
    there.wait()

    members = []
    customer = lax.broadcasted_iota(jnp.int32, (CHIPS, CUST), 1).astype(F32) + 1.0
    counts, sums = jnp.zeros((CUST, W), F32), jnp.zeros((CUST, W), F32)
    for source in (there.near, there.far):
        if source is there.far:
            there.wait_far()
        for got, name in there.rows(source):
            member = jnp.where(name[:, :CUST] == customer, 1.0, 0.0).astype(BF16)
            members.append(member)
            counts = counts + dot_tn(member, jnp.ones((CHIPS, W), BF16))
            sums = sums + dot_tn(member, got)
    divisor = jnp.maximum(counts, 1.0)
    pooled = (sums / divisor).astype(BF16)
    linked = dot(pooled, link[...])
    pbased_value = (
        (parent_ref[...].astype(F32).reshape(CUST, CTOK, W) + linked[:, None, :])
        .astype(BF16)
        .reshape(PROWS, W)
    )
    pbased[...] = pbased_value

    def norm_based(rows, i):
        x = pbased[rows].astype(F32)
        pn[rows] = (x * rms_scale(x) * pgain[...].astype(F32)[None, :]).astype(BF16)

    each(PGROUPS, GPROWS, norm_based)
    pq_[...] = dot(pn[...], pq[...]).astype(BF16)
    pk_[...] = dot(pn[...], pk[...]).astype(BF16)
    pv_[...] = dot(pn[...], pv[...]).astype(BF16)
    attend(pq_, pk_, pv_, pprobs, pmix, PGROUPS, GPROWS, CTOK)
    attend_back(pq_, pk_, pv_, pprobs, pdmix, pdqkv, PGROUPS, GPROWS)
    pdn[...] = (
        dot_nt(pdqkv[:, :W], pq[...])
        + dot_nt(pdqkv[:, W : 2 * W], pk[...])
        + dot_nt(pdqkv[:, 2 * W :], pv[...])
    )

    dlinked = []
    for i in range(PGROUPS):
        rows = slice(i * GPROWS, (i + 1) * GPROWS)
        x = pbased[rows].astype(F32)
        r = rms_scale(x)
        unit = x * r
        dunit = pdn[rows] * pgain[...].astype(F32)[None, :]
        dx = r * (dunit - unit * jnp.mean(dunit * unit, axis=1, keepdims=True))
        dx = dx + cot_ref[rows].astype(F32) * scale
        dlinked.append(jnp.sum(dx.reshape(GROUP, CTOK, W), axis=1))
    dlinked = jnp.concatenate(dlinked, axis=0)
    dpooled = dot_nt(dlinked.astype(BF16), link[...]).astype(BF16).astype(F32)
    sum_grad = (dpooled / divisor).astype(BF16)
    core = at[3]
    moved = [dot(member, sum_grad) for member in members]
    for p in range(4):
        home, slot = p // 2, p % 2
        back.put(p, jnp.where(core == home, moved[slot], moved[2 + slot]))
    back.start()

    put_block(parent_mine, 0, dot_tn(pooled, dlinked.astype(BF16)))
    dweights = dot_tn(pn[...], pdqkv[...])
    for b in range(3):
        put_block(parent_mine, 1 + b, dweights[:, b * W : (b + 1) * W])
    put_block(parent_mine, 4, dot_tn(pmix[...], pda[...]))
    parent_job.start()
    states_ref[...] = (pbased[...].astype(F32) + dot(pmix[...], po[...])).astype(BF16)
    parent_job.scatter_plane()
    back.wait()

    ditem = jnp.zeros((TX, W), F32)
    near = back.rows(back.near)
    back.wait_far()
    far = back.rows(back.far)
    for p in range(4):
        home, slot = p // 2, p % 2
        got = jnp.where(core == home, near[slot][0].astype(F32), far[slot][0].astype(F32))
        ditem = ditem + dot_tn(places[p], got.astype(BF16))
    ditem_b = ditem.astype(BF16)
    ddown = dot_tn(hmean[...], ditem_b)
    for b in range(4):
        put_block(down_mine, b, ddown[b * W : (b + 1) * W])
    down_job.start()
    dhidden[...] = (dot_nt(ditem_b, down[...]) * (1.0 / COLS)).astype(BF16).astype(F32)
    dy = dot_tn(averaging(), ditem_b)

    def back_hidden(rows, i):
        spread = jnp.concatenate(
            [jnp.broadcast_to(dhidden[t : t + 1], (COLS, FF)) for t in (2 * i, 2 * i + 1)], axis=0
        )
        h[rows] = (spread * slope[rows].astype(F32)).astype(BF16)

    each(TX // 2, 2 * COLS, back_hidden)
    dup = dot_tn(n2[...], h[...])
    for b in range(4):
        put_block(up_mine, b, dup[:, b * W : (b + 1) * W])
    u[:, :W] = dot_nt(h[...], up[...])
    u[:, W : 2 * W] = dy
    parent_job.scatter_z()
    down_job.scatter_plane()

    def back_stream(rows, i):
        x = s_[rows].astype(F32)
        r = rms_scale(x)
        unit = x * r
        dunit = u[rows, :W].astype(BF16).astype(F32) * hgain[...].astype(F32)[None, :]
        dx = r * (dunit - unit * jnp.mean(dunit * unit, axis=1, keepdims=True))
        da[rows] = (dx + u[rows, W : 2 * W] * (1.0 / COLS)).astype(BF16)

    each(GROUPS, GROWS, back_stream)
    put_block(up_mine, 4, dot_tn(mix[...], da[...]))
    up_job.start()
    dmix[...] = dot_nt(da[...], co[...]).astype(BF16)
    meanwhile = {1: up_job.scatter_plane, 5: down_job.scatter_z}
    attend_back(q, k, v, probs, dmix, dqkv, GROUPS, GROWS, lambda i: meanwhile.get(i, int)())
    dweights = dot_tn(n1[...], dqkv[...])
    for b in range(3):
        put_block(att_mine, b, dweights[:, b * W : (b + 1) * W])
    att_job.start()

    att_job.scatter_plane()
    parent_job.gather_plane()
    up_job.scatter_z()
    att_job.scatter_z()
    down_job.gather_plane()
    up_job.gather_plane()
    parent_job.gather_core()
    down_job.gather_core()
    att_job.gather_plane()
    up_job.gather_core()
    att_job.gather_core()
    for job in (there, back, parent_job, down_job, up_job, att_job):
        job.finish()


def gain_row(weights, sums, gain):
    total = jnp.zeros((W, W), F32)
    for weight, value in zip(weights, sums, strict=True):
        total = total + weight.astype(F32) * value
    high = total.astype(BF16)
    low = (total - high.astype(F32)).astype(BF16)
    ones = jnp.ones((8, W), BF16)
    return (dot_nt(ones, high) + dot_nt(ones, low))[:1] / gain


def unpack_kernel(
    states_in, parent_sum, down_sum, up_sum, att_sum, kept, up, gains,
    states, dcg, dcq, dck, dcv, dco, dhg, dup, ddown, dlink, dpg, dpq, dpk, dpv, dpo,
    stage, wide_stage, tall_stage, gain_stage, store_sem,
):
    def block(total, b):
        return jnp.concatenate(
            [total[half, :, b].astype(F32).reshape(W, 128) for half in range(2)], axis=1
        )

    copies = []

    def store(source, target):
        copies.append(pltpu.make_async_copy(source, target, store_sem.at[len(copies)]))
        copies[-1].start()

    store(states_in, states)
    for b in range(4):
        tall_stage[b * W : (b + 1) * W] = block(down_sum, b)
    store(tall_stage, ddown)
    for b in range(4):
        wide_stage[:, b * W : (b + 1) * W] = block(up_sum, b)
    store(wide_stage, dup)
    squares = [(att_sum, b, ref) for b, ref in enumerate((dcq, dck, dcv))]
    squares += [(parent_sum, b, ref) for b, ref in enumerate((dlink, dpq, dpk, dpv, dpo))]
    squares += [(up_sum, 4, dco)]
    for i, (total, b, ref) in enumerate(squares):
        stage[i] = block(total, b)
        store(stage.at[i], ref)
    for i in range(2):
        grads = [stage[j] for j in ((0, 1, 2), (4, 5, 6))[i]]
        gain_stage[i] = gain_row([kept[3 * i + j] for j in range(3)], grads, gains[i : i + 1])
    cuts = [slice(b * W, (b + 1) * W) for b in range(4)]
    gain_stage[2] = gain_row(
        [up[:, c] for c in cuts], [wide_stage[:, c] for c in cuts], gains[2:3]
    )
    for i, ref in enumerate((dcg, dpg, dhg)):
        store(gain_stage.at[i], ref)
    for done in copies:
        done.wait()


def body(
    item_tokens, owner_index, owner_row, parent_tokens, cotangent,
    column_gain, column_query, column_key, column_value, column_out,
    hidden_gain, up_weight, down_weight, link_weight,
    parent_gain, parent_query, parent_key, parent_value, parent_out,
):
    vmem = pl.BlockSpec(memory_space=pltpu.VMEM)
    later = pl.BlockSpec(memory_space=pl.ANY)
    shape = jax.ShapeDtypeStruct
    cgain, hgain, pgain = column_gain, hidden_gain, parent_gain
    items = lambda width, dtype=BF16: pltpu.VMEM((ROWS, width), dtype)
    parents = lambda width, dtype=BF16: pltpu.VMEM((PROWS, width), dtype)
    scratch = [
        items(W), items(W), items(W), items(W),
        pltpu.VMEM((GROUPS, HEADS * GROWS, GROWS), BF16),
        items(W), items(W), items(W), items(FF, F32), items(FF), items(FF),
        pltpu.VMEM((TX, FF), F32), items(W), items(W), items(3 * W),
        pltpu.VMEM((TX, FF), BF16),
        parents(W), parents(W), parents(W), parents(W), parents(W),
        pltpu.VMEM((PGROUPS, HEADS * GPROWS, GPROWS), BF16),
        parents(W), parents(W), parents(W), parents(3 * W), parents(W, F32),
        *[pltpu.VMEM((2, 16, n, 16, 128), BF16) for n in BLOCKS],
        pltpu.VMEM((TX, COLS, W), BF16),
        parents(W), parents(W), pltpu.VMEM((W, W), BF16), pltpu.VMEM((FF, W), BF16),
        pltpu.VMEM((W, W), BF16), pltpu.VMEM((W, W), BF16),
        pltpu.SemaphoreType.DMA((len(LATER),)),
        *Exchange.scratch(), *Exchange.scratch(),
    ]
    for n in BLOCKS:
        scratch += Summing.scratch(n)
    kept = pl.pallas_call(
        encoder_kernel,
        out_shape=[pltpu.VMEM((PROWS, W), BF16)]
        + [pltpu.VMEM((2, 16, n, 16, 128), BF16) for n in BLOCKS]
        + [pltpu.VMEM((6, W, W), BF16), pltpu.VMEM((W, FF), BF16), pltpu.VMEM((3, W), F32)],
        in_specs=[later] + [vmem] * 2 + [later] * 2 + [vmem] + [later] * 4 + [vmem] + [later] * 3 + [vmem]
        + [later] * 4,
        out_specs=[vmem] * 8,
        scratch_shapes=scratch,
        compiler_params=pltpu.CompilerParams(
            collective_id=1, has_side_effects=True, vmem_limit_bytes=VMEM_LIMIT
        ),
        name="encoder",
    )(
        item_tokens, owner_index.reshape(1, TX), owner_row.reshape(1, TX),
        parent_tokens.reshape(PROWS, W), cotangent.reshape(PROWS, W),
        cgain, column_query, column_key, column_value, column_out,
        hgain, up_weight, down_weight, link_weight,
        pgain, parent_query, parent_key, parent_value, parent_out,
    )
    square = shape((W, W), F32)
    row = shape((1, W), F32)
    out = pl.pallas_call(
        unpack_kernel,
        out_shape=[
            shape((PROWS, W), BF16), row, square, square, square, square, row,
            shape((W, FF), F32), shape((FF, W), F32), square, row, square, square, square, square,
        ],
        in_specs=[vmem] * 8,
        out_specs=[later] * 15,
        scratch_shapes=[
            pltpu.VMEM((9, W, W), F32), pltpu.VMEM((W, FF), F32), pltpu.VMEM((FF, W), F32),
            pltpu.VMEM((3, 1, W), F32), pltpu.SemaphoreType.DMA((15,)),
        ],
        compiler_params=pltpu.CompilerParams(vmem_limit_bytes=UNPACK_LIMIT),
        name="unpack",
    )(*kept)
    out = [o.reshape(W) if o.shape == (1, W) else o for o in out]
    return (out[0].reshape(CUST, CTOK, W), *out[1:])


def solution(mesh):
    split, whole = P(("dp", "rep")), P()
    return jax.shard_map(
        body,
        mesh=mesh,
        in_specs=(split,) * 5 + (whole,) * 14,
        out_specs=(split,) + (whole,) * 14,
        check_vma=False,
    )
```
